32 devices in a mesh: grp: 2 (over y), exp: 4 (over z), tp: 4 (over x, core).
Axes of the slice: x: 2, y: 2, z: 4, core: 2. Of those that a mesh axis runs over, the one named last changes fastest.
Arguments:
- tokens: bfloat16 [256, 4096], P(('grp', 'exp'), 'tp'), parts along dimension 0, may hold values from -6 to 6
- lat_down: bfloat16 [1024, 4096], P(None, 'tp'), may hold values from -0.09375 to 0.09375
- lat_up: bfloat16 [1024, 4096], P(None, 'tp'), may hold values from -0.1875 to 0.1875
- expert_up: bfloat16 [8, 2688, 1024], P('exp', 'tp'), may hold values from -0.1875 to 0.1875
- expert_down: bfloat16 [8, 2688, 1024], P('exp', 'tp'), may hold values from -0.125 to 0.125
- routes: int32 [256, 4], P(('grp', 'exp')), parts along dimension 0, may hold values from 0 to 7, all different within a row; in each aligned block of 32 rows (0 to 31, 32 to 63, ...) at most 24 rows name the same one
- route_weights: float32 [256, 4], P(('grp', 'exp')), parts along dimension 0, may hold values from 0.05 to 0.5
Outputs:
- moe_out: bfloat16 [256, 4096], P(('grp', 'exp'), 'tp'), parts along dimension 0
The draws below stay inside these ranges and needn't reach their ends.
There are 2 independent parts, one for each index of `grp`. The reference program is written for one: setup_inputs(seed, part) draws one part's arguments, and reference() takes and returns one part's arrays. A program takes and returns all parts, laid end to end along the dimension named above; an argument that names none is the same for every part. Nothing has to cross between parts.
Inputs may be any that keep to these rules, and one draw needn't show every extreme that they name: `routes`: each row names 4 different experts. In each aligned block of 32 rows (the tokens of one index of exp) no expert is named by more than 24 rows, and in every draw some expert is named by exactly 24 rows of some block.
All inputs are finite; a program needn't handle non-finite values.
Results may differ from the reference program's by a relative error of at most 0.022.
Values may be sent and summed in bfloat16 or wider, within the bound.
No kernel may reach another device: no remote copies, remote signals or barrier semaphores. Data moves between devices by JAX's collectives and lax.ppermute only.
A program may use at most 64 MiB of HBM per device.

```python
import math
import jax
import jax.numpy as jnp
import numpy as np
from jax import lax

D = 4096
L = 1024
EH = 2688
TOK_GRP = 32
EXPERTS = 8
TOP = 4
CAP = 24
TOKENS = 128
N_EXP = 4
N_TP = 4


def block_scale(stream_key, dims, shards, smallest, top_value):
    factor_of, own = 1.0, jax.random.fold_in(stream_key, 6)
    for axis_at, parts in shards:
        draws = jnp.exp(jax.random.uniform(jax.random.fold_in(own, axis_at), (parts,), jnp.float32, smallest / len(shards), top_value / len(shards)))
        factor_of = factor_of * jnp.repeat(draws, dims[axis_at] // parts).reshape([-1 if axis == axis_at else 1 for axis in range(len(dims))])
    return factor_of


def deal_out(stream_key, own, number, rows, count, top, reach, skew):
    ranking = jax.random.permutation(stream_key, count)
    packed, common = portions_of(count, rows * top, reach, skew, True), portions_of(count, rows * top, reach, skew, False)
    places = jnp.arange(count)

    def named(tallies, rotation):
        used = int((tallies > 0).sum())
        fixed = max(1, used // 4)
        moved = fixed + (places - fixed + rotation * (used - fixed)) % max(1, count - fixed)
        return jnp.zeros((count,), jnp.int32).at[ranking[jnp.where(places < fixed, places, moved)]].set(jnp.asarray(tallies, jnp.int32))

    tallies = jnp.where(number % 4 == 0, named(packed, number // 4), named(common, number - number // 4 - 1))
    mixed = jax.random.permutation(jax.random.fold_in(own, 3), count)
    source_of, receiver = mixed[0:count // 2 * 2:2], mixed[1:count // 2 * 2:2]
    margin = jnp.minimum(tallies[source_of] - 1, reach - tallies[receiver]) // 2
    margin = jnp.where((source_of == ranking[0]) | (receiver == ranking[0]) | (tallies[receiver] == 0), 0, jnp.maximum(margin, 0))
    moved = jax.random.randint(jax.random.fold_in(own, 4), (count // 2,), 0, 1 << 20) % (margin + 1)
    tallies = tallies.at[source_of].add(-moved).at[receiver].add(moved)
    labels = jnp.searchsorted(jnp.cumsum(tallies), jnp.arange(rows * top), side="right").astype(jnp.int32)
    grid = labels.reshape(top, rows).T
    grid = grid[jax.random.permutation(jax.random.fold_in(own, 1), rows)]
    rotation = jax.random.randint(jax.random.fold_in(own, 2), (rows, 1), 0, top)
    return jnp.take_along_axis(grid, (jnp.arange(top)[None, :] + rotation) % top, axis=1)


def portions_of(number_of, total, limit, skew, full):
    weights = [(1 << 20) // math.isqrt(standing ** skew) + 1 for standing in range(1, number_of + 1)]
    largest = limit if full else min(limit, max(-(-total // number_of), total * weights[0] // sum(weights)))
    least = 1 if total - largest >= number_of - 1 else 0
    given, spare = [largest] + [least] * (number_of - 1), total - largest - least * (number_of - 1)
    while spare > 0:
        movable = [i for i in range(1, number_of) if given[i] < largest] or [i for i in range(1, number_of) if given[i] < limit]
        mass, budget = sum([weights[i] for i in movable]), spare
        for i in movable:
            extra = min(limit - given[i], max(1, budget * weights[i] // mass), spare)
            given[i] = given[i] + extra
            spare = spare - extra
    return np.array(given)


def gaussian(stream_key, extent, spread, most, pieces=(), held_as=jnp.bfloat16):
    array = jax.random.normal(stream_key, extent, jnp.float32) * spread
    if len(pieces) > 0:
        array = block_scale(stream_key, extent, pieces, -0.22, 0.18) * array
    return jnp.clip(array, min=-most, max=most).astype(held_as)


def setup_inputs(seed: int = 0, part: int = 0) -> dict:
    arg_keys = jax.random.split(jax.random.key(seed), 8)
    part_splits = jax.random.split(jax.random.fold_in(arg_keys[7], part), 8)
    tokens = gaussian(part_splits[0], (TOKENS, D), 1.0, 6.0, ((0, 4), (1, 4)))
    lat_down = gaussian(arg_keys[1], (L, D), D ** -0.5, 0.09375, ((1, 4),))
    lat_up = gaussian(arg_keys[2], (L, D), L ** -0.5, 0.1875, ((1, 4),))
    expert_up = gaussian(arg_keys[3], (EXPERTS, EH, L), L ** -0.5, 0.1875, ((0, 4), (1, 4)))
    expert_down = gaussian(arg_keys[4], (EXPERTS, EH, L), EH ** -0.5, 0.125, ((0, 4), (1, 4)))
    routes_keys = jax.random.split(jax.random.fold_in(part_splits[5], 1), TOKENS // TOK_GRP)
    routes_turns = jax.random.permutation(jax.random.fold_in(part_splits[5], 3), TOKENS // TOK_GRP)
    routes = jax.vmap(lambda own, number: deal_out(jax.random.fold_in(part_splits[5], 2), own, number, TOK_GRP, EXPERTS, TOP, CAP, 2))(routes_keys, routes_turns).reshape((TOKENS, TOP))
    route_weights = jnp.clip(0.05 + 0.45 * jax.random.uniform(part_splits[6], (TOKENS, TOP), jnp.float32) ** block_scale(part_splits[6], (TOKENS, TOP), ((0, 4),), -0.2, 0.2), 0.05, 0.5)
    return dict(tokens=tokens, lat_down=lat_down, lat_up=lat_up, expert_up=expert_up, expert_down=expert_down, routes=routes, route_weights=route_weights)


def reference(tokens, lat_down, lat_up, expert_up, expert_down, routes, route_weights):
    latent = jnp.dot(tokens, lat_down.T, preferred_element_type=jnp.float32).astype(jnp.bfloat16)
    padded = jnp.concatenate([latent, jnp.zeros((1, L), jnp.bfloat16)], axis=0)
    flat_routes = routes.reshape(-1)
    rows_max = N_EXP * CAP
    slice_len = EH // N_TP

    def per_expert(expert):
        pair_hits = jnp.nonzero(flat_routes == expert, size=rows_max, fill_value=TOKENS * TOP)[0].astype(jnp.int32)
        owners = (pair_hits // TOP).astype(jnp.int32)
        expert_rows = padded[owners]
        pre_act = jnp.dot(expert_rows, expert_up[expert].T, preferred_element_type=jnp.float32)
        hidden = (jnp.maximum(pre_act, 0.0) ** 2).astype(jnp.bfloat16)
        down_rows = expert_down[expert]
        running = jnp.zeros((rows_max, L), jnp.float32)
        for piece_index in range(N_TP):
            lower_row = piece_index * slice_len
            partial_piece = jnp.dot(hidden[:, lower_row:lower_row + slice_len], down_rows[lower_row:lower_row + slice_len], preferred_element_type=jnp.float32)
            rounded = lax.optimization_barrier(partial_piece.astype(jnp.bfloat16))
            running = running + rounded.astype(jnp.float32)
        return pair_hits, running

    pair_hits, totals = lax.map(per_expert, jnp.arange(EXPERTS, dtype=jnp.int32))
    pair_values = jnp.zeros((TOKENS * TOP + 1, L), jnp.float32).at[pair_hits.reshape(-1)].set(totals.reshape(-1, L))
    per_pair = pair_values[:TOKENS * TOP].reshape(TOKENS, TOP, L)
    mixed_rows = jnp.sum(per_pair * route_weights[:, :, None], axis=1).astype(jnp.bfloat16)
    return jnp.dot(mixed_rows, lat_up, preferred_element_type=jnp.float32).astype(jnp.bfloat16)
```

```python
import jax
import jax.numpy as jnp
from jax import lax
from jax.sharding import PartitionSpec as P


def shifted(x, axis, shift):
    count = lax.axis_size(axis)
    return lax.ppermute(x, axis, [(i, (i + shift) % count) for i in range(count)])


def gathered(x, axis):
    return [x] + [shifted(x, axis, s) for s in range(1, lax.axis_size(axis))]


def summed(blocks):
    total = blocks[0].astype(jnp.float32)
    for block in blocks[1:]:
        total = total + block.astype(jnp.float32)
    return total.astype(jnp.bfloat16)


def on_device(tokens, lat_down, lat_up, expert_up, expert_down, routes, route_weights):
    exp_count = lax.axis_size("exp")
    me = lax.axis_index("exp")
    local_count = expert_up.shape[0]
    rows = tokens.shape[0]
    experts_all = local_count * exp_count
    named = routes[:, :, None] == jnp.arange(experts_all, dtype=jnp.int32)[None, None, :]
    combine = jnp.sum(jnp.where(named, route_weights[:, :, None], 0.0), axis=1)
    combine_all = jnp.concatenate(gathered(combine, "exp"), axis=0)
    combine_here = lax.dynamic_slice_in_dim(combine_all, me * local_count, local_count, axis=1)

    partial_latent = jnp.einsum("td,ld->tl", tokens, lat_down, preferred_element_type=jnp.float32)
    latent = summed(gathered(partial_latent.astype(jnp.bfloat16), "tp"))
    latent_all = jnp.concatenate(gathered(latent, "exp"), axis=0)

    pre_act = jnp.einsum("tl,khl->kth", latent_all, expert_up, preferred_element_type=jnp.float32)
    hidden = jnp.maximum(pre_act, 0.0) ** 2 * combine_here.T[:, :, None]
    partial_out = jnp.einsum(
        "kth,khl->tl", hidden.astype(jnp.bfloat16), expert_down, preferred_element_type=jnp.float32
    ).astype(jnp.bfloat16)
    blocks = partial_out.reshape(exp_count, rows, -1)
    partial_mix = summed(
        [blocks[0]] + [shifted(blocks[s], "exp", exp_count - s) for s in range(1, exp_count)]
    )
    mixed_rows = summed(gathered(partial_mix, "tp"))
    return jnp.dot(mixed_rows, lat_up, preferred_element_type=jnp.float32).astype(jnp.bfloat16)


def solution(mesh):
    return jax.shard_map(
        on_device,
        mesh=mesh,
        in_specs=(
            P(("grp", "exp"), "tp"),
            P(None, "tp"),
            P(None, "tp"),
            P("exp", "tp", None),
            P("exp", "tp", None),
            P(("grp", "exp"), None),
            P(("grp", "exp"), None),
        ),
        out_specs=P(("grp", "exp"), "tp"),
        check_vma=False,
    )
```

```python
import jax
import jax.numpy as jnp
from jax import lax
from jax.sharding import PartitionSpec as P


def swap(blocks, axes):
    return lax.all_to_all(blocks, axes, split_axis=0, concat_axis=0, tiled=True)


def spread(x, axes, count):
    return swap(jnp.broadcast_to(x[None], (count, *x.shape)), axes)


def summed(blocks):
    return jnp.sum(blocks.astype(jnp.float32), axis=0).astype(jnp.bfloat16)


def on_device(tokens, lat_down, lat_up, expert_up, expert_down, routes, route_weights):
    exp_count, tp_count = lax.axis_size("exp"), lax.axis_size("tp")
    local_count = expert_up.shape[0]
    rows, latent_len = tokens.shape[0], lat_down.shape[0]
    part_len = latent_len // tp_count
    experts_all = local_count * exp_count
    named = routes[:, :, None] == jnp.arange(experts_all, dtype=jnp.int32)[None, None, :]
    combine = jnp.sum(jnp.where(named, route_weights[:, :, None], 0.0), axis=1)
    combine_here = swap(combine.reshape(rows, exp_count, local_count).transpose(1, 0, 2), "exp")
    combine_here = combine_here.reshape(exp_count * rows, local_count)

    partial_latent = jnp.einsum("td,ld->tl", tokens, lat_down, preferred_element_type=jnp.float32)
    parts = partial_latent.astype(jnp.bfloat16).reshape(rows, tp_count, part_len).transpose(1, 0, 2)
    latent_part = summed(swap(parts, "tp"))
    latent_all = spread(latent_part, ("exp", "tp"), exp_count * tp_count)
    latent_all = latent_all.reshape(exp_count, tp_count, rows, part_len).transpose(0, 2, 1, 3)
    latent_all = latent_all.reshape(exp_count * rows, latent_len)

    pre_act = jnp.einsum("tl,khl->kth", latent_all, expert_up, preferred_element_type=jnp.float32)
    hidden = jnp.maximum(pre_act, 0.0) ** 2 * combine_here.T[:, :, None]
    partial_out = jnp.einsum(
        "kth,khl->tl", hidden.astype(jnp.bfloat16), expert_down, preferred_element_type=jnp.float32
    ).astype(jnp.bfloat16)
    blocks = partial_out.reshape(exp_count, rows, tp_count, part_len).transpose(0, 2, 1, 3)
    mixed_part = summed(swap(blocks.reshape(exp_count * tp_count, rows, part_len), ("exp", "tp")))
    mixed_rows = spread(mixed_part, "tp", tp_count).transpose(1, 0, 2).reshape(rows, latent_len)
    return jnp.dot(mixed_rows, lat_up, preferred_element_type=jnp.float32).astype(jnp.bfloat16)


def solution(mesh):
    return jax.shard_map(
        on_device,
        mesh=mesh,
        in_specs=(
            P(("grp", "exp"), "tp"),
            P(None, "tp"),
            P(None, "tp"),
            P("exp", "tp", None),
            P("exp", "tp", None),
            P(("grp", "exp"), None),
            P(("grp", "exp"), None),
        ),
        out_specs=P(("grp", "exp"), "tp"),
        check_vma=False,
    )
```

```python
import jax
import jax.numpy as jnp
from jax import lax
from jax.sharding import PartitionSpec as P

BF16, F32 = jnp.bfloat16, jnp.float32


def traded(x, axis, mask):
    return lax.ppermute(x, axis, [(i, i ^ mask) for i in range(lax.axis_size(axis))])


def summed(own, arrived):
    total = own.astype(F32)
    for block in arrived:
        total = total + block.astype(F32)
    return total


def on_device(tokens, lat_down, lat_up, expert_up, expert_down, routes, route_weights):
    exp_count, tp_count = lax.axis_size("exp"), lax.axis_size("tp")
    me = lax.axis_index("exp")
    odd = lax.axis_index("tp") % 2 == 1
    local_count = expert_up.shape[0]
    rows, latent_len = tokens.shape[0], lat_down.shape[0]
    half = latent_len // 2
    experts_all = local_count * exp_count
    pair_masks = [1 << b for b in range(1, tp_count.bit_length() - 1)]

    def mine(x):
        return jnp.where(odd, x[:, half:], x[:, :half])

    def theirs(x):
        return jnp.where(odd, x[:, :half], x[:, half:])

    def whole(own, other):
        return jnp.concatenate([jnp.where(odd, other, own), jnp.where(odd, own, other)], axis=1)

    def pair_sum(x):
        for mask in pair_masks:
            x = summed(x, [traded(x.astype(BF16), "tp", mask)])
        return x

    named = routes[:, :, None] == jnp.arange(experts_all, dtype=jnp.int32)[None, None, :]
    combine = jnp.sum(jnp.where(named, route_weights[:, :, None], 0.0), axis=1)
    high = combine.astype(BF16)
    low = (combine - high.astype(F32)).astype(BF16)
    pad = jnp.zeros((rows, -2 * experts_all % 128), BF16)

    partial_latent = jnp.einsum("td,ld->tl", tokens, lat_down, preferred_element_type=F32)
    latent_half = summed(
        mine(partial_latent), [traded(theirs(partial_latent).astype(BF16), "tp", 1)]
    )
    message = jnp.concatenate([pair_sum(latent_half).astype(BF16), high, low, pad], axis=1)
    messages = [message] + [traded(message, "exp", s) for s in range(1, exp_count)]
    messages = jnp.concatenate(messages, axis=0)
    halves = messages[:, :half]
    latent_all = whole(halves, traded(halves, "tp", 1))
    terms = messages[:, half : half + 2 * experts_all].astype(F32)
    combine_all = terms[:, :experts_all] + terms[:, experts_all:]
    combine_here = lax.dynamic_slice_in_dim(combine_all, me * local_count, local_count, axis=1)

    pre_act = jnp.einsum("tl,khl->kth", latent_all, expert_up, preferred_element_type=F32)
    hidden = jnp.maximum(pre_act, 0.0) ** 2 * combine_here.T[:, :, None]
    partial_out = jnp.einsum(
        "kth,khl->tl", hidden.astype(BF16), expert_down, preferred_element_type=F32
    )
    part_half = summed(
        mine(partial_out), [traded(theirs(partial_out).astype(BF16), "tp", 1)]
    ).astype(BF16)
    blocks = part_half.reshape(exp_count, rows, half)
    mixed_half = summed(blocks[0], [traded(blocks[s], "exp", s) for s in range(1, exp_count)])
    mixed_half = pair_sum(mixed_half).astype(BF16)
    mixed_rows = whole(mixed_half, traded(mixed_half, "tp", 1))
    return jnp.dot(mixed_rows, lat_up, preferred_element_type=F32).astype(BF16)


def solution(mesh):
    return jax.shard_map(
        on_device,
        mesh=mesh,
        in_specs=(
            P(("grp", "exp"), "tp"),
            P(None, "tp"),
            P(None, "tp"),
            P("exp", "tp", None),
            P("exp", "tp", None),
            P(("grp", "exp"), None),
            P(("grp", "exp"), None),
        ),
        out_specs=P(("grp", "exp"), "tp"),
        check_vma=False,
    )
```

```python
import jax
import jax.numpy as jnp
from jax import lax
from jax.experimental import pallas as pl
from jax.experimental.pallas import tpu as pltpu
from jax.sharding import PartitionSpec as P

BF16, F32 = jnp.bfloat16, jnp.float32
NT = (((1,), (1,)), ((), ()))
VMEM_LIMIT = 24 << 20


def traded(x, axis, mask):
    return lax.ppermute(x, axis, [(i, i ^ mask) for i in range(lax.axis_size(axis))])


def summed(own, arrived):
    total = own.astype(F32)
    for block in arrived:
        total = total + block.astype(F32)
    return total


def in_vmem(x):
    return pltpu.with_memory_space_constraint(x, pltpu.VMEM)


def params():
    return pltpu.CompilerParams(vmem_limit_bytes=VMEM_LIMIT)


def kernel_call(body, out_shape, args, specs, scratch, flops, moved):
    vmem = pl.BlockSpec(memory_space=pltpu.VMEM)
    return pl.pallas_call(
        body,
        out_shape=out_shape,
        in_specs=[vmem if s is None else pl.BlockSpec(memory_space=s) for s in specs],
        out_specs=jax.tree.map(lambda _: vmem, out_shape),
        scratch_shapes=scratch,
        compiler_params=params(),
        cost_estimate=pl.CostEstimate(flops=flops, bytes_accessed=moved, transcendentals=0),
    )(*args)


CHUNKS = 2


def down_kernel(tokens_ref, weight_ref, theirs_ref, mine_ref, held, sems):
    odd = lax.axis_index("tp") % 2
    half = held.shape[0] // 2
    size = half // CHUNKS
    copies = []
    for i in range(2 * CHUNKS):
        side = (1 - odd) if i < CHUNKS else odd
        start = pl.multiple_of(side * half + i % CHUNKS * size, size)
        copy = pltpu.make_async_copy(
            weight_ref.at[pl.ds(start, size), :], held.at[pl.ds(i * size, size), :], sems.at[i]
        )
        copy.start()
        copies.append(copy)
    x = tokens_ref[...]
    for i in range(2 * CHUNKS):
        copies[i].wait()
        part = lax.dot_general(x, held[i * size : (i + 1) * size, :], NT, preferred_element_type=F32)
        at = i % CHUNKS * size
        if i < CHUNKS:
            theirs_ref[:, at : at + size] = part.astype(BF16)
        else:
            mine_ref[:, at : at + size] = part


def expert_kernel(messages_ref, other_ref, up_ref, down_ref, theirs_ref, mine_ref, latent, hidden):
    odd = lax.axis_index("tp") % 2
    local_count, units, latent_len = up_ref.shape
    half = latent_len // 2
    experts_all = local_count * lax.axis_size("exp")
    first = lax.axis_index("exp") * local_count
    own_at = pl.multiple_of(odd * half, half)
    other_at = pl.multiple_of((1 - odd) * half, half)
    latent[:, pl.ds(own_at, half)] = messages_ref[:, :half]
    latent[:, pl.ds(other_at, half)] = other_ref[...]
    terms = messages_ref[:, half:].astype(F32)
    lane = lax.broadcasted_iota(jnp.int32, terms.shape, 1)
    rows = latent[...]
    for k in range(local_count):
        named = (lane == first + k) | (lane == first + k + experts_all)
        weight = jnp.sum(jnp.where(named, terms, 0.0), axis=1, keepdims=True)
        pre_act = lax.dot_general(rows, up_ref[k], NT, preferred_element_type=F32)
        active = jnp.maximum(pre_act, 0.0)
        hidden[:, k * units : (k + 1) * units] = (active * active * weight).astype(BF16)
    acts = hidden[...]
    theirs_ref[...] = jnp.dot(
        acts, down_ref[:, pl.ds(other_at, half)], preferred_element_type=F32
    ).astype(BF16)
    mine_ref[...] = jnp.dot(acts, down_ref[:, pl.ds(own_at, half)], preferred_element_type=F32)


def up_kernel(mine_ref, other_ref, weight_ref, out_ref):
    odd = lax.axis_index("tp") % 2
    half = mine_ref.shape[1]
    own_at = pl.multiple_of(odd * half, half)
    other_at = pl.multiple_of((1 - odd) * half, half)
    total = jnp.dot(mine_ref[...], weight_ref[pl.ds(own_at, half), :], preferred_element_type=F32)
    total += jnp.dot(other_ref[...], weight_ref[pl.ds(other_at, half), :], preferred_element_type=F32)
    out_ref[...] = total.astype(BF16)


def on_device(tokens, lat_down, lat_up, expert_up, expert_down, routes, route_weights):
    exp_count, tp_count = lax.axis_size("exp"), lax.axis_size("tp")
    local_count, units, latent_len = expert_up.shape
    rows, width = tokens.shape
    half = latent_len // 2
    all_rows = exp_count * rows
    experts_all = local_count * exp_count
    pair_masks = [1 << b for b in range(1, tp_count.bit_length() - 1)]

    def pair_sum(x):
        for mask in pair_masks:
            x = summed(x, [traded(x.astype(BF16), "tp", mask)])
        return x

    named = routes[:, :, None] == jnp.arange(experts_all, dtype=jnp.int32)[None, None, :]
    combine = jnp.sum(jnp.where(named, route_weights[:, :, None], 0.0), axis=1)
    high = combine.astype(BF16)
    low = (combine - high.astype(F32)).astype(BF16)
    pad = jnp.zeros((rows, -2 * experts_all % 128), BF16)

    theirs, mine = kernel_call(
        down_kernel,
        (jax.ShapeDtypeStruct((rows, half), BF16), jax.ShapeDtypeStruct((rows, half), F32)),
        (tokens, lat_down),
        (None, pltpu.HBM),
        [pltpu.VMEM((latent_len, width), BF16), pltpu.SemaphoreType.DMA((2 * CHUNKS,))],
        2 * rows * width * latent_len,
        2 * width * latent_len,
    )
    latent_half = summed(mine, [traded(theirs, "tp", 1)])
    message = jnp.concatenate([pair_sum(latent_half).astype(BF16), high, low, pad], axis=1)
    messages = [message] + [traded(message, "exp", s) for s in range(1, exp_count)]
    messages = jnp.concatenate(messages, axis=0)
    theirs, mine = kernel_call(
        expert_kernel,
        (jax.ShapeDtypeStruct((all_rows, half), BF16), jax.ShapeDtypeStruct((all_rows, half), F32)),
        (
            messages,
            traded(messages[:, :half], "tp", 1),
            in_vmem(expert_up),
            in_vmem(expert_down.reshape(local_count * units, latent_len)),
        ),
        (None,) * 4,
        [
            pltpu.VMEM((all_rows, latent_len), BF16),
            pltpu.VMEM((all_rows, local_count * units), BF16),
        ],
        4 * all_rows * latent_len * local_count * units,
        4 * latent_len * local_count * units,
    )
    part_half = summed(mine, [traded(theirs, "tp", 1)]).astype(BF16)
    blocks = part_half.reshape(exp_count, rows, half)
    mixed_half = summed(blocks[0], [traded(blocks[s], "exp", s) for s in range(1, exp_count)])
    mixed_half = pair_sum(mixed_half).astype(BF16)
    return kernel_call(
        up_kernel,
        jax.ShapeDtypeStruct((rows, lat_up.shape[1]), BF16),
        (mixed_half, traded(mixed_half, "tp", 1), in_vmem(lat_up)),
        (None,) * 3,
        [],
        2 * rows * latent_len * lat_up.shape[1],
        2 * latent_len * lat_up.shape[1],
    )


def solution(mesh):
    return jax.shard_map(
        on_device,
        mesh=mesh,
        in_specs=(
            P(("grp", "exp"), "tp"),
            P(None, "tp"),
            P(None, "tp"),
            P("exp", "tp", None),
            P("exp", "tp", None),
            P(("grp", "exp"), None),
            P(("grp", "exp"), None),
        ),
        out_specs=P(("grp", "exp"), "tp"),
        check_vma=False,
    )
```

```python
import jax
import jax.numpy as jnp
from jax import lax
from jax.experimental import pallas as pl
from jax.experimental.pallas import tpu as pltpu
from jax.sharding import PartitionSpec as P

BF16, F32 = jnp.bfloat16, jnp.float32
NT = (((1,), (1,)), ((), ()))
VMEM_LIMIT = 24 << 20
LANES = 128
CHUNKS = 4


def in_space(x, space):
    return pltpu.with_memory_space_constraint(x, space)


def kernel_call(body, out_shape, args, specs, scratch, flops, moved):
    vmem = pl.BlockSpec(memory_space=pltpu.VMEM)
    return pl.pallas_call(
        body,
        out_shape=out_shape,
        in_specs=[vmem if s is None else pl.BlockSpec(memory_space=s) for s in specs],
        out_specs=jax.tree.map(lambda _: vmem, out_shape),
        scratch_shapes=scratch,
        compiler_params=pltpu.CompilerParams(vmem_limit_bytes=VMEM_LIMIT),
        cost_estimate=pl.CostEstimate(flops=flops, bytes_accessed=moved, transcendentals=0),
    )(*args)


def down_kernel(
    tokens_hbm, weight_hbm, routes_hbm, scale_hbm, send_ref, keep_ref, terms_ref,
    tokens, weight, routes, scale, sems,
):
    size = weight.shape[0] // CHUNKS
    small = [(tokens_hbm, tokens), (routes_hbm, routes), (scale_hbm, scale)]
    small = [pltpu.make_async_copy(a, b, sems.at[i]) for i, (a, b) in enumerate(small)]
    small[0].start()
    chunks = []
    for i in range(CHUNKS):
        at = pl.ds(i * size, size)
        chunks.append(pltpu.make_async_copy(weight_hbm.at[at, :], weight.at[at, :], sems.at[3 + i]))
        chunks[i].start()
        if i == 0:
            small[1].start()
            small[2].start()
    small[1].wait()
    small[2].wait()
    rows = tokens.shape[0]
    width = terms_ref.shape[1]
    row = lax.broadcasted_iota(jnp.int32, (width, rows), 0)
    experts_all = width // 2
    expert = jnp.where(row < experts_all, row, row - experts_all)
    combine = jnp.zeros((width, rows), F32)
    for r in range(routes.shape[0]):
        combine += jnp.where(expert == routes[r : r + 1, :], scale[r : r + 1, :], 0.0)
    high = combine.astype(BF16).astype(F32)
    combine = jnp.where(row < experts_all, high, combine - high)
    combine = jnp.concatenate([combine, jnp.zeros((width, LANES - rows), F32)], axis=1)
    terms_ref[...] = combine.T[:rows, :].astype(BF16)
    small[0].wait()
    x = tokens[...]
    for i in range(CHUNKS):
        chunks[i].wait()
        part = lax.dot_general(x, weight[i * size : (i + 1) * size, :], NT, preferred_element_type=F32)
        send_ref[:, i * size : (i + 1) * size] = part.astype(BF16)
        keep_ref[:, i * size : (i + 1) * size] = part


def load_kernel(after_ref, up_hbm, down_hbm, up_ref, down_ref, sems):
    copies = [
        pltpu.make_async_copy(up_hbm, up_ref, sems.at[0]),
        pltpu.make_async_copy(down_hbm, down_ref, sems.at[1]),
    ]
    for copy in copies:
        copy.start()
    for copy in copies:
        copy.wait()


def expert_kernel(own_ref, other_ref, up_ref, down_ref, theirs_ref, mine_ref, latent, terms, hidden):
    local_count, units, latent_len = up_ref.shape
    side = own_ref.shape[0]
    experts_all = terms.shape[1] // 2
    first = lax.axis_index("exp") * local_count
    for at, ref in ((0, own_ref), (side, other_ref)):
        latent[at : at + side, :] = ref[:, :latent_len]
        terms[at : at + side, :] = ref[:, latent_len:].astype(F32)
    rows = latent[...]
    lane = lax.broadcasted_iota(jnp.int32, terms.shape, 1)
    for k in range(local_count):
        named = (lane == first + k) | (lane == first + k + experts_all)
        weight = jnp.sum(jnp.where(named, terms[...], 0.0), axis=1, keepdims=True)
        pre_act = lax.dot_general(rows, up_ref[k], NT, preferred_element_type=F32)
        active = jnp.maximum(pre_act, 0.0)
        hidden[:, k * units : (k + 1) * units] = (active * active * weight).astype(BF16)
    result = jnp.dot(hidden[...], down_ref[...], preferred_element_type=F32)
    mine_ref[...] = result[:side, :]
    theirs_ref[...] = result[side:, :].astype(BF16)


def up_kernel(keep_ref, other_ref, weight_ref, out_ref):
    mixed = (keep_ref[...] + other_ref[...].astype(F32)).astype(BF16)
    out_ref[...] = jnp.dot(mixed, weight_ref[...], preferred_element_type=F32).astype(BF16)


def on_device(tokens, lat_down, lat_up, expert_up, expert_down, routes, route_weights):
    exp_count, tp_count = lax.axis_size("exp"), lax.axis_size("tp")
    pairs = tp_count // 2
    local_count, units, latent_len = expert_up.shape
    rows, width = tokens.shape
    side_rows = exp_count // 2 * rows
    terms_len = -(-2 * local_count * exp_count // LANES) * LANES

    def from_pair(x):
        return lax.ppermute(x, "tp", [(t, t ^ 1) for t in range(tp_count)])

    def sent(x, step, over):
        def peer(e, t):
            return (e ^ (exp_count - 2 - 2 * step + 1 - t % 2)) * tp_count + (t ^ (2 * over))

        whole = [(e, t) for e in range(exp_count) for t in range(tp_count)]
        return lax.ppermute(x, ("exp", "tp"), [(e * tp_count + t, peer(e, t)) for e, t in whole])

    send, keep, terms = kernel_call(
        down_kernel,
        (
            jax.ShapeDtypeStruct((rows, latent_len), BF16),
            jax.ShapeDtypeStruct((rows, latent_len), F32),
            jax.ShapeDtypeStruct((rows, terms_len), BF16),
        ),
        [in_space(x, pltpu.HBM) for x in (tokens, lat_down, routes.T, route_weights.T)],
        (pltpu.HBM,) * 4,
        [
            pltpu.VMEM((rows, width), BF16),
            pltpu.VMEM((latent_len, width), BF16),
            pltpu.VMEM((routes.shape[1], rows), jnp.int32),
            pltpu.VMEM((routes.shape[1], rows), F32),
            pltpu.SemaphoreType.DMA((3 + CHUNKS,)),
        ],
        2 * rows * width * latent_len,
        2 * width * latent_len,
    )
    latent_part = (keep + from_pair(send).astype(F32)).astype(BF16)
    message = jnp.concatenate([latent_part, terms], axis=1)
    down_rows = expert_down.reshape(local_count * units, latent_len)
    up_here, down_here = kernel_call(
        load_kernel,
        (pltpu.VMEM(expert_up.shape, BF16), pltpu.VMEM(down_rows.shape, BF16)),
        (message, in_space(expert_up, pltpu.HBM), in_space(down_rows, pltpu.HBM)),
        (pl.ANY, pltpu.HBM, pltpu.HBM),
        [pltpu.SemaphoreType.DMA((2,))],
        0,
        4 * latent_len * local_count * units,
    )
    arrived = [
        [sent(latent_part if over else message, step, over) for over in range(pairs)]
        for step in range(exp_count // 2)
    ]
    arrived, up_here, down_here = lax.optimization_barrier((arrived, up_here, down_here))
    own = []
    for blocks in arrived:
        latent = sum(a[:, :latent_len].astype(F32) for a in blocks).astype(BF16)
        own.append(jnp.concatenate([latent, blocks[0][:, latent_len:]], axis=1))
    own = jnp.concatenate(own, axis=0)
    theirs, mine = kernel_call(
        expert_kernel,
        (
            jax.ShapeDtypeStruct((side_rows, latent_len), BF16),
            jax.ShapeDtypeStruct((side_rows, latent_len), F32),
        ),
        (own, from_pair(own), in_space(up_here, pltpu.VMEM), in_space(down_here, pltpu.VMEM)),
        (None,) * 4,
        [
            pltpu.VMEM((2 * side_rows, latent_len), BF16),
            pltpu.VMEM((2 * side_rows, terms_len), F32),
            pltpu.VMEM((2 * side_rows, local_count * units), BF16),
        ],
        8 * side_rows * latent_len * local_count * units,
        4 * latent_len * local_count * units,
    )
    part = (mine + from_pair(theirs).astype(F32)).astype(BF16)
    arrived = []
    for step in range(exp_count // 2):
        block = part[step * rows : (step + 1) * rows]
        arrived += [sent(block, step, over) for over in range(pairs)]
    keep = sum(a.astype(F32) for a in arrived)
    return kernel_call(
        up_kernel,
        jax.ShapeDtypeStruct((rows, lat_up.shape[1]), BF16),
        (keep, from_pair(keep.astype(BF16)), in_space(lat_up, pltpu.VMEM)),
        (None,) * 3,
        [],
        2 * rows * latent_len * lat_up.shape[1],
        2 * latent_len * lat_up.shape[1],
    )


def solution(mesh):
    return jax.shard_map(
        on_device,
        mesh=mesh,
        in_specs=(
            P(("grp", "exp"), "tp"),
            P(None, "tp"),
            P(None, "tp"),
            P("exp", "tp", None),
            P("exp", "tp", None),
            P(("grp", "exp"), None),
            P(("grp", "exp"), None),
        ),
        out_specs=P(("grp", "exp"), "tp"),
        check_vma=False,
    )
```

```python
import jax
import jax.numpy as jnp
from jax import lax
from jax.experimental import pallas as pl
from jax.experimental.pallas import tpu as pltpu
from jax.sharding import PartitionSpec as P

BF16, F32 = jnp.bfloat16, jnp.float32
NT = (((1,), (1,)), ((), ()))
VMEM_LIMIT = 24 << 20
LANES = 128
CHUNKS = 4


def in_space(x, space):
    return pltpu.with_memory_space_constraint(x, space)


def kernel_call(body, out_shape, args, specs, scratch, flops, moved, out_space=pltpu.VMEM):
    vmem = pl.BlockSpec(memory_space=pltpu.VMEM)
    out_spec = pl.BlockSpec(memory_space=out_space)
    return pl.pallas_call(
        body,
        out_shape=out_shape,
        in_specs=[vmem if s is None else pl.BlockSpec(memory_space=s) for s in specs],
        out_specs=jax.tree.map(lambda _: out_spec, out_shape),
        scratch_shapes=scratch,
        compiler_params=pltpu.CompilerParams(vmem_limit_bytes=VMEM_LIMIT),
        cost_estimate=pl.CostEstimate(flops=flops, bytes_accessed=moved, transcendentals=0),
    )(*args)


def down_kernel(
    tokens_hbm, weight_hbm, routes_hbm, scale_hbm, send_ref, keep_ref, routes_ref, scale_ref,
    tokens, weight, sems,
):
    size = weight.shape[0] // CHUNKS
    small = [(tokens_hbm, tokens), (routes_hbm, routes_ref), (scale_hbm, scale_ref)]
    small = [pltpu.make_async_copy(a, b, sems.at[i]) for i, (a, b) in enumerate(small)]
    small[0].start()
    chunks = []
    for i in range(CHUNKS):
        at = pl.ds(i * size, size)
        chunks.append(pltpu.make_async_copy(weight_hbm.at[at, :], weight.at[at, :], sems.at[3 + i]))
        chunks[i].start()
    small[1].start()
    small[2].start()
    small[0].wait()
    x = tokens[...]
    for i in range(CHUNKS):
        chunks[i].wait()
        part = lax.dot_general(x, weight[i * size : (i + 1) * size, :], NT, preferred_element_type=F32)
        send_ref[:, i * size : (i + 1) * size] = part.astype(BF16)
        keep_ref[:, i * size : (i + 1) * size] = part
    small[1].wait()
    small[2].wait()


def terms_kernel(routes_ref, scale_ref, terms_ref):
    rows, width = terms_ref.shape
    row = lax.broadcasted_iota(jnp.int32, (width, rows), 0)
    experts_all = width // 2
    expert = jnp.where(row < experts_all, row, row - experts_all)
    combine = jnp.zeros((width, rows), F32)
    for r in range(routes_ref.shape[0]):
        combine += jnp.where(expert == routes_ref[r : r + 1, :], scale_ref[r : r + 1, :], 0.0)
    high = combine.astype(BF16).astype(F32)
    combine = jnp.where(row < experts_all, high, combine - high)
    combine = jnp.concatenate([combine, jnp.zeros((width, LANES - rows), F32)], axis=1)
    terms_ref[...] = combine.T[:rows, :].astype(BF16)


def load_kernel(after_ref, up_hbm, down_hbm, up_ref, down_ref, sems):
    copies = [
        pltpu.make_async_copy(up_hbm, up_ref, sems.at[0]),
        pltpu.make_async_copy(down_hbm, down_ref, sems.at[1]),
    ]
    for copy in copies:
        copy.start()
    for copy in copies:
        copy.wait()


def expert_kernel(own_ref, other_ref, up_ref, down_ref, theirs_ref, mine_ref, latent, terms, hidden):
    local_count, units, latent_len = up_ref.shape
    side = own_ref.shape[0]
    experts_all = terms.shape[1] // 2
    first = lax.axis_index("exp") * local_count
    for at, ref in ((0, own_ref), (side, other_ref)):
        latent[at : at + side, :] = ref[:, :latent_len]
        terms[at : at + side, :] = ref[:, latent_len:].astype(F32)
    rows = latent[...]
    lane = lax.broadcasted_iota(jnp.int32, terms.shape, 1)
    for k in range(local_count):
        named = (lane == first + k) | (lane == first + k + experts_all)
        weight = jnp.sum(jnp.where(named, terms[...], 0.0), axis=1, keepdims=True)
        pre_act = lax.dot_general(rows, up_ref[k], NT, preferred_element_type=F32)
        active = jnp.maximum(pre_act, 0.0)
        hidden[:, k * units : (k + 1) * units] = (active * active * weight).astype(BF16)
    result = jnp.dot(hidden[...], down_ref[...], preferred_element_type=F32)
    mine_ref[...] = result[:side, :]
    theirs_ref[...] = result[side:, :].astype(BF16)


def up_kernel(keep_ref, other_ref, weight_ref, out_hbm, out, sems):
    mixed = (keep_ref[...] + other_ref[...].astype(F32)).astype(BF16)
    half = out.shape[1] // 2
    copies = []
    for i in range(2):
        at = slice(i * half, (i + 1) * half)
        out[:, at] = jnp.dot(mixed, weight_ref[:, at], preferred_element_type=F32).astype(BF16)
        copies.append(pltpu.make_async_copy(out.at[:, at], out_hbm.at[:, at], sems.at[i]))
        copies[i].start()
    for copy in copies:
        copy.wait()


def on_device(tokens, lat_down, lat_up, expert_up, expert_down, routes, route_weights):
    exp_count, tp_count = lax.axis_size("exp"), lax.axis_size("tp")
    pairs = tp_count // 2
    local_count, units, latent_len = expert_up.shape
    rows, width = tokens.shape
    side_rows = exp_count // 2 * rows
    terms_len = -(-2 * local_count * exp_count // LANES) * LANES

    def from_pair(x):
        return lax.ppermute(x, "tp", [(t, t ^ 1) for t in range(tp_count)])

    def sent(x, step, over):
        def peer(e, t):
            return (e ^ (exp_count - 2 - 2 * step + 1 - t % 2)) * tp_count + (t ^ (2 * over))

        whole = [(e, t) for e in range(exp_count) for t in range(tp_count)]
        return lax.ppermute(x, ("exp", "tp"), [(e * tp_count + t, peer(e, t)) for e, t in whole])

    send, keep, routes_here, scale_here = kernel_call(
        down_kernel,
        (
            jax.ShapeDtypeStruct((rows, latent_len), BF16),
            jax.ShapeDtypeStruct((rows, latent_len), F32),
            jax.ShapeDtypeStruct(routes.shape[::-1], jnp.int32),
            jax.ShapeDtypeStruct(routes.shape[::-1], F32),
        ),
        [in_space(x, pltpu.HBM) for x in (tokens, lat_down, routes.T, route_weights.T)],
        (pltpu.HBM,) * 4,
        [
            pltpu.VMEM((rows, width), BF16),
            pltpu.VMEM((latent_len, width), BF16),
            pltpu.SemaphoreType.DMA((3 + CHUNKS,)),
        ],
        2 * rows * width * latent_len,
        2 * width * latent_len,
    )
    terms = kernel_call(
        terms_kernel,
        jax.ShapeDtypeStruct((rows, terms_len), BF16),
        (routes_here, scale_here),
        (None,) * 2,
        [],
        rows * terms_len * 8,
        2 * rows * terms_len,
    )
    latent_part = (keep + from_pair(send).astype(F32)).astype(BF16)
    message = jnp.concatenate([latent_part, terms], axis=1)
    down_rows = expert_down.reshape(local_count * units, latent_len)
    up_here, down_here = kernel_call(
        load_kernel,
        (pltpu.VMEM(expert_up.shape, BF16), pltpu.VMEM(down_rows.shape, BF16)),
        (message, in_space(expert_up, pltpu.HBM), in_space(down_rows, pltpu.HBM)),
        (pl.ANY, pltpu.HBM, pltpu.HBM),
        [pltpu.SemaphoreType.DMA((2,))],
        0,
        4 * latent_len * local_count * units,
    )
    arrived = [
        [sent(message, step, over) for over in range(pairs)]
        for step in reversed(range(exp_count // 2))
    ][::-1]
    arrived, up_here, down_here = lax.optimization_barrier((arrived, up_here, down_here))
    own = []
    for blocks in arrived:
        latent = sum(a[:, :latent_len].astype(F32) for a in blocks).astype(BF16)
        own.append(jnp.concatenate([latent, blocks[0][:, latent_len:]], axis=1))
    own = jnp.concatenate(own, axis=0)
    theirs, mine = kernel_call(
        expert_kernel,
        (
            jax.ShapeDtypeStruct((side_rows, latent_len), BF16),
            jax.ShapeDtypeStruct((side_rows, latent_len), F32),
        ),
        (own, from_pair(own), in_space(up_here, pltpu.VMEM), in_space(down_here, pltpu.VMEM)),
        (None,) * 4,
        [
            pltpu.VMEM((2 * side_rows, latent_len), BF16),
            pltpu.VMEM((2 * side_rows, terms_len), F32),
            pltpu.VMEM((2 * side_rows, local_count * units), BF16),
        ],
        8 * side_rows * latent_len * local_count * units,
        4 * latent_len * local_count * units,
    )
    part = (mine + from_pair(theirs).astype(F32)).astype(BF16)
    arrived = []
    for step in range(exp_count // 2):
        block = part[step * rows : (step + 1) * rows]
        arrived += [sent(block, step, over) for over in range(pairs)]
    keep = sum(a.astype(F32) for a in arrived)
    return kernel_call(
        up_kernel,
        jax.ShapeDtypeStruct((rows, lat_up.shape[1]), BF16),
        (keep, from_pair(keep.astype(BF16)), in_space(lat_up, pltpu.VMEM)),
        (None,) * 3,
        [pltpu.VMEM((rows, lat_up.shape[1]), BF16), pltpu.SemaphoreType.DMA((2,))],
        2 * rows * latent_len * lat_up.shape[1],
        2 * latent_len * lat_up.shape[1],
        pltpu.HBM,
    )


def solution(mesh):
    return jax.shard_map(
        on_device,
        mesh=mesh,
        in_specs=(
            P(("grp", "exp"), "tp"),
            P(None, "tp"),
            P(None, "tp"),
            P("exp", "tp", None),
            P("exp", "tp", None),
            P(("grp", "exp"), None),
            P(("grp", "exp"), None),
        ),
        out_specs=P(("grp", "exp"), "tp"),
        check_vma=False,
    )
```

```python
import jax
import jax.numpy as jnp
from jax import lax
from jax.experimental import pallas as pl
from jax.experimental.pallas import tpu as pltpu
from jax.sharding import PartitionSpec as P

BF16, F32 = jnp.bfloat16, jnp.float32
NT = (((1,), (1,)), ((), ()))
NN = (((1,), (0,)), ((), ()))
VMEM_LIMIT = 24 << 20
LANES = 128
CHUNKS = 2


def hbm(x):
    return pltpu.with_memory_space_constraint(x, pltpu.HBM)


def vmem(x):
    return pltpu.with_memory_space_constraint(x, pltpu.VMEM)


def shaped(dtype, *shape):
    return jax.ShapeDtypeStruct(shape, dtype)


def kernel_call(body, out_shape, args, in_hbm, scratch, flops, moved, out_space=pltpu.VMEM):
    def spec(space):
        return pl.BlockSpec(memory_space=space)

    return pl.pallas_call(
        body,
        out_shape=out_shape,
        in_specs=[spec(pltpu.HBM if i in in_hbm else pltpu.VMEM) for i in range(len(args))],
        out_specs=jax.tree.map(lambda _: spec(out_space), out_shape),
        scratch_shapes=scratch,
        compiler_params=pltpu.CompilerParams(vmem_limit_bytes=VMEM_LIMIT),
        cost_estimate=pl.CostEstimate(flops=flops, bytes_accessed=moved, transcendentals=0),
    )(*args)


def dot(a, b, dims):
    return lax.dot_general(a, b, dims, preferred_element_type=F32)


def half_at(own, half):
    odd = lax.axis_index("tp") % 2
    return pl.multiple_of((odd if own else 1 - odd) * half, half)


def down_kernel(own, tokens_hbm, weight_hbm, out_ref, tokens, weight, sems):
    half = out_ref.shape[1]
    size = half // CHUNKS
    load = pltpu.make_async_copy(tokens_hbm, tokens, sems.at[CHUNKS])
    load.start()
    chunks = []
    for i in range(CHUNKS):
        start = pl.multiple_of(half_at(own, half) + i * size, size)
        chunks.append(
            pltpu.make_async_copy(
                weight_hbm.at[pl.ds(start, size), :],
                weight.at[pl.ds(i * size, size), :],
                sems.at[i],
            )
        )
        chunks[i].start()
    load.wait()
    x = tokens[...]
    for i in range(CHUNKS):
        chunks[i].wait()
        at = slice(i * size, (i + 1) * size)
        out_ref[:, at] = dot(x, weight[at, :], NT).astype(out_ref.dtype)


def load_kernel(
    after_ref, routes_hbm, scale_hbm, up_hbm, down_hbm, terms_ref, up_ref, down_ref,
    routes, scale, sems,
):
    pairs = [(routes_hbm, routes), (scale_hbm, scale), (up_hbm, up_ref), (down_hbm, down_ref)]
    copies = [pltpu.make_async_copy(a, b, sems.at[i]) for i, (a, b) in enumerate(pairs)]
    for copy in copies:
        copy.start()
    copies[0].wait()
    copies[1].wait()
    rows, width = terms_ref.shape
    row = lax.broadcasted_iota(jnp.int32, (width, rows), 0)
    experts_all = width // 2
    expert = jnp.where(row < experts_all, row, row - experts_all)
    combine = jnp.zeros((width, rows), F32)
    for r in range(routes.shape[0]):
        combine += jnp.where(expert == routes[r : r + 1, :], scale[r : r + 1, :], 0.0)
    high = combine.astype(BF16).astype(F32)
    combine = jnp.where(row < experts_all, high, combine - high)
    combine = jnp.concatenate([combine, jnp.zeros((width, LANES - rows), F32)], axis=1)
    terms_ref[...] = combine.T[:rows, :].astype(BF16)
    copies[2].wait()
    copies[3].wait()


def first_kernel(messages_ref, up_ref, pre_ref):
    local_count, units, latent_len = up_ref.shape
    half = latent_len // 2
    rows = messages_ref[:, :half]
    for k in range(local_count):
        weight = up_ref[k, :, pl.ds(half_at(True, half), half)]
        pre_ref[:, k * units : (k + 1) * units] = dot(rows, weight, NT)


def second_kernel(messages_ref, other_ref, pre_ref, up_ref, down_ref, hidden_ref, theirs_ref):
    local_count, units, latent_len = up_ref.shape
    half = latent_len // 2
    terms = messages_ref[:, half:].astype(F32)
    lane = lax.broadcasted_iota(jnp.int32, terms.shape, 1)
    first = lax.axis_index("exp") * local_count
    rows = other_ref[...]
    for k in range(local_count):
        named = (lane == first + k) | (lane == first + k + terms.shape[1] // 2)
        weight = jnp.sum(jnp.where(named, terms, 0.0), axis=1, keepdims=True)
        at = slice(k * units, (k + 1) * units)
        pre_act = pre_ref[:, at] + dot(rows, up_ref[k, :, pl.ds(half_at(False, half), half)], NT)
        active = jnp.maximum(pre_act, 0.0)
        hidden_ref[:, at] = (active * active * weight).astype(BF16)
    theirs = dot(hidden_ref[...], down_ref[:, pl.ds(half_at(False, half), half)], NN)
    theirs_ref[...] = theirs.astype(BF16)


def third_kernel(hidden_ref, down_ref, mine_ref):
    half = mine_ref.shape[1]
    mine_ref[...] = dot(hidden_ref[...], down_ref[:, pl.ds(half_at(True, half), half)], NN)


def up_own_kernel(own_ref, weight_ref, out_ref):
    half = own_ref.shape[1]
    out_ref[...] = dot(own_ref[...], weight_ref[pl.ds(half_at(True, half), half), :], NN)


def up_kernel(part_ref, other_ref, weight_ref, out_hbm, out, sems):
    other = other_ref[...]
    at_rows = pl.ds(half_at(False, other.shape[1]), other.shape[1])
    half = out.shape[1] // 2
    copies = []
    for i in range(2):
        at = slice(i * half, (i + 1) * half)
        out[:, at] = (part_ref[:, at] + dot(other, weight_ref[at_rows, at], NN)).astype(BF16)
        copies.append(pltpu.make_async_copy(out.at[:, at], out_hbm.at[:, at], sems.at[i]))
        copies[i].start()
    for copy in copies:
        copy.wait()


def on_device(tokens, lat_down, lat_up, expert_up, expert_down, routes, route_weights):
    exp_count, tp_count = lax.axis_size("exp"), lax.axis_size("tp")
    local_count, units, latent_len = expert_up.shape
    rows, width = tokens.shape
    half = latent_len // 2
    all_rows = exp_count * rows
    all_units = local_count * units
    out_len = lat_up.shape[1]
    terms_len = -(-2 * local_count * exp_count // LANES) * LANES
    pair_masks = [1 << b for b in range(1, tp_count.bit_length() - 1)]

    def traded(x, axis, mask):
        return lax.ppermute(x, axis, [(i, i ^ mask) for i in range(lax.axis_size(axis))])

    def across(x):
        for mask in pair_masks:
            x = x + traded(x.astype(BF16), "tp", mask).astype(F32)
        return x

    def down_half(own, dtype):
        return kernel_call(
            lambda *refs: down_kernel(own, *refs),
            shaped(dtype, rows, half),
            (hbm(tokens), hbm(lat_down)),
            (0, 1),
            [
                pltpu.VMEM((rows, width), BF16),
                pltpu.VMEM((half, width), BF16),
                pltpu.SemaphoreType.DMA((CHUNKS + 1,)),
            ],
            2 * rows * width * half,
            2 * width * half,
        )

    theirs = down_half(False, BF16)
    mine = down_half(True, F32)
    mine = mine + traded(theirs, "tp", 1).astype(F32)
    down_rows = expert_down.reshape(all_units, latent_len)
    terms, up_here, down_here = kernel_call(
        load_kernel,
        (
            shaped(BF16, rows, terms_len),
            pltpu.VMEM(expert_up.shape, BF16),
            pltpu.VMEM(down_rows.shape, BF16),
        ),
        (mine.astype(BF16), *(hbm(x) for x in (routes.T, route_weights.T, expert_up, down_rows))),
        (1, 2, 3, 4),
        [
            pltpu.VMEM(routes.shape[::-1], jnp.int32),
            pltpu.VMEM(routes.shape[::-1], F32),
            pltpu.SemaphoreType.DMA((4,)),
        ],
        0,
        4 * latent_len * all_units,
    )
    up_here, down_here = vmem(up_here), vmem(down_here)
    message = jnp.concatenate([across(mine).astype(BF16), terms], axis=1)
    messages = [message] + [traded(message, "exp", s) for s in range(1, exp_count)]
    messages = jnp.concatenate(messages, axis=0)
    other = traded(messages[:, :half], "tp", 1)
    pre = kernel_call(
        first_kernel,
        shaped(F32, all_rows, all_units),
        (messages, up_here),
        (),
        [],
        all_rows * latent_len * all_units,
        latent_len * all_units,
    )
    hidden, theirs = kernel_call(
        second_kernel,
        (shaped(BF16, all_rows, all_units), shaped(BF16, all_rows, half)),
        (messages, other, pre, up_here, down_here),
        (),
        [],
        2 * all_rows * latent_len * all_units,
        2 * latent_len * all_units,
    )
    mine = kernel_call(
        third_kernel,
        shaped(F32, all_rows, half),
        (hidden, down_here),
        (),
        [],
        all_rows * latent_len * all_units,
        latent_len * all_units,
    )
    part = (mine + traded(theirs, "tp", 1).astype(F32)).astype(BF16)
    blocks = part.reshape(exp_count, rows, half)
    mixed = blocks[0].astype(F32)
    for s in range(1, exp_count):
        mixed = mixed + traded(blocks[s], "exp", s).astype(F32)
    mixed = across(mixed).astype(BF16)
    lat_up = vmem(lat_up)
    own_part = kernel_call(
        up_own_kernel,
        shaped(F32, rows, out_len),
        (mixed, lat_up),
        (),
        [],
        rows * latent_len * out_len,
        latent_len * out_len,
    )
    return kernel_call(
        up_kernel,
        shaped(BF16, rows, out_len),
        (own_part, traded(mixed, "tp", 1), lat_up),
        (),
        [pltpu.VMEM((rows, out_len), BF16), pltpu.SemaphoreType.DMA((2,))],
        rows * latent_len * out_len,
        latent_len * out_len,
        pltpu.HBM,
    )


def solution(mesh):
    return jax.shard_map(
        on_device,
        mesh=mesh,
        in_specs=(
            P(("grp", "exp"), "tp"),
            P(None, "tp"),
            P(None, "tp"),
            P("exp", "tp", None),
            P("exp", "tp", None),
            P(("grp", "exp"), None),
            P(("grp", "exp"), None),
        ),
        out_specs=P(("grp", "exp"), "tp"),
        check_vma=False,
    )
```

```python
import jax
import jax.numpy as jnp
from jax import lax
from jax.experimental import pallas as pl
from jax.experimental.pallas import tpu as pltpu
from jax.sharding import PartitionSpec as P

BF16, F32 = jnp.bfloat16, jnp.float32
NT = (((1,), (1,)), ((), ()))
NN = (((1,), (0,)), ((), ()))
VMEM_LIMIT = 24 << 20
LANES = 128
CHUNKS = 2


def hbm(x):
    return pltpu.with_memory_space_constraint(x, pltpu.HBM)


def vmem(x):
    return pltpu.with_memory_space_constraint(x, pltpu.VMEM)


def shaped(dtype, *shape):
    return jax.ShapeDtypeStruct(shape, dtype)


def kernel_call(body, out_shape, args, in_hbm, scratch, flops, moved, out_space=pltpu.VMEM):
    def spec(space):
        return pl.BlockSpec(memory_space=space)

    return pl.pallas_call(
        body,
        out_shape=out_shape,
        in_specs=[spec(pltpu.HBM if i in in_hbm else pltpu.VMEM) for i in range(len(args))],
        out_specs=jax.tree.map(lambda _: spec(out_space), out_shape),
        scratch_shapes=scratch,
        compiler_params=pltpu.CompilerParams(vmem_limit_bytes=VMEM_LIMIT),
        cost_estimate=pl.CostEstimate(flops=flops, bytes_accessed=moved, transcendentals=0),
    )(*args)


def dot(a, b, dims):
    return lax.dot_general(a, b, dims, preferred_element_type=F32)


def half_at(own, half):
    odd = lax.axis_index("tp") % 2
    return pl.multiple_of((odd if own else 1 - odd) * half, half)


def down_kernel(tokens_hbm, weight_hbm, theirs_ref, tokens, mine_weight, weight, sems):
    half = theirs_ref.shape[1]
    size = half // CHUNKS
    load = pltpu.make_async_copy(tokens_hbm, tokens, sems.at[0])
    load.start()
    chunks = []
    for i in range(CHUNKS):
        start = pl.multiple_of(half_at(False, half) + i * size, size)
        chunks.append(
            pltpu.make_async_copy(
                weight_hbm.at[pl.ds(start, size), :],
                weight.at[pl.ds(i * size, size), :],
                sems.at[2 + i],
            )
        )
        chunks[i].start()
    later = pltpu.make_async_copy(
        weight_hbm.at[pl.ds(half_at(True, half), half), :], mine_weight, sems.at[1]
    )
    later.start()
    load.wait()
    x = tokens[...]
    for i in range(CHUNKS):
        chunks[i].wait()
        at = slice(i * size, (i + 1) * size)
        theirs_ref[:, at] = dot(x, weight[at, :], NT).astype(BF16)
    later.wait()


def down_own_kernel(tokens_ref, weight_ref, mine_ref):
    mine_ref[...] = dot(tokens_ref[...], weight_ref[...], NT)


def load_kernel(
    after_ref, routes_hbm, scale_hbm, up_hbm, down_hbm, terms_ref, up_ref, down_ref,
    routes, scale, sems,
):
    pairs = [(routes_hbm, routes), (scale_hbm, scale), (up_hbm, up_ref), (down_hbm, down_ref)]
    copies = [pltpu.make_async_copy(a, b, sems.at[i]) for i, (a, b) in enumerate(pairs)]
    for copy in copies:
        copy.start()
    copies[0].wait()
    copies[1].wait()
    rows, width = terms_ref.shape
    row = lax.broadcasted_iota(jnp.int32, (width, rows), 0)
    experts_all = width // 2
    expert = jnp.where(row < experts_all, row, row - experts_all)
    combine = jnp.zeros((width, rows), F32)
    for r in range(routes.shape[0]):
        combine += jnp.where(expert == routes[r : r + 1, :], scale[r : r + 1, :], 0.0)
    high = combine.astype(BF16).astype(F32)
    combine = jnp.where(row < experts_all, high, combine - high)
    combine = jnp.concatenate([combine, jnp.zeros((width, LANES - rows), F32)], axis=1)
    terms_ref[...] = combine.T[:rows, :].astype(BF16)
    copies[2].wait()
    copies[3].wait()


def first_kernel(messages_ref, up_ref, pre_ref):
    local_count, units, latent_len = up_ref.shape
    half = latent_len // 2
    rows = messages_ref[:, :half]
    for k in range(local_count):
        weight = up_ref[k, :, pl.ds(half_at(True, half), half)]
        pre_ref[:, k * units : (k + 1) * units] = dot(rows, weight, NT)


def second_kernel(messages_ref, other_ref, pre_ref, up_ref, down_ref, hidden_ref, theirs_ref):
    local_count, units, latent_len = up_ref.shape
    half = latent_len // 2
    terms = messages_ref[:, half:].astype(F32)
    lane = lax.broadcasted_iota(jnp.int32, terms.shape, 1)
    first = lax.axis_index("exp") * local_count
    rows = other_ref[...]
    for k in range(local_count):
        named = (lane == first + k) | (lane == first + k + terms.shape[1] // 2)
        weight = jnp.sum(jnp.where(named, terms, 0.0), axis=1, keepdims=True)
        at = slice(k * units, (k + 1) * units)
        pre_act = pre_ref[:, at] + dot(rows, up_ref[k, :, pl.ds(half_at(False, half), half)], NT)
        active = jnp.maximum(pre_act, 0.0)
        hidden_ref[:, at] = (active * active * weight).astype(BF16)
    theirs = dot(hidden_ref[...], down_ref[:, pl.ds(half_at(False, half), half)], NN)
    theirs_ref[...] = theirs.astype(BF16)


def third_kernel(hidden_ref, down_ref, mine_ref):
    half = mine_ref.shape[1]
    mine_ref[...] = dot(hidden_ref[...], down_ref[:, pl.ds(half_at(True, half), half)], NN)


def up_own_kernel(own_ref, weight_ref, out_ref):
    half = own_ref.shape[1]
    out_ref[...] = dot(own_ref[...], weight_ref[pl.ds(half_at(True, half), half), :], NN)


def up_kernel(part_ref, other_ref, weight_ref, out_hbm, out, sems):
    other = other_ref[...]
    at_rows = pl.ds(half_at(False, other.shape[1]), other.shape[1])
    half = out.shape[1] // 2
    copies = []
    for i in range(2):
        at = slice(i * half, (i + 1) * half)
        out[:, at] = (part_ref[:, at] + dot(other, weight_ref[at_rows, at], NN)).astype(BF16)
        copies.append(pltpu.make_async_copy(out.at[:, at], out_hbm.at[:, at], sems.at[i]))
        copies[i].start()
    for copy in copies:
        copy.wait()


def on_device(tokens, lat_down, lat_up, expert_up, expert_down, routes, route_weights):
    exp_count, tp_count = lax.axis_size("exp"), lax.axis_size("tp")
    local_count, units, latent_len = expert_up.shape
    rows, width = tokens.shape
    half = latent_len // 2
    all_rows = exp_count * rows
    all_units = local_count * units
    out_len = lat_up.shape[1]
    terms_len = -(-2 * local_count * exp_count // LANES) * LANES
    pair_masks = [1 << b for b in range(1, tp_count.bit_length() - 1)]

    def traded(x, axis, mask):
        return lax.ppermute(x, axis, [(i, i ^ mask) for i in range(lax.axis_size(axis))])

    def across(x):
        for mask in pair_masks:
            x = x + traded(x.astype(BF16), "tp", mask).astype(F32)
        return x

    theirs, tokens_here, weight_here = kernel_call(
        down_kernel,
        (
            shaped(BF16, rows, half),
            pltpu.VMEM((rows, width), BF16),
            pltpu.VMEM((half, width), BF16),
        ),
        (hbm(tokens), hbm(lat_down)),
        (0, 1),
        [pltpu.VMEM((half, width), BF16), pltpu.SemaphoreType.DMA((CHUNKS + 2,))],
        2 * rows * width * half,
        4 * width * half,
    )
    mine = kernel_call(
        down_own_kernel,
        shaped(F32, rows, half),
        (vmem(tokens_here), vmem(weight_here)),
        (),
        [],
        2 * rows * width * half,
        2 * width * half,
    )
    mine = mine + traded(theirs, "tp", 1).astype(F32)
    down_rows = expert_down.reshape(all_units, latent_len)
    terms, up_here, down_here = kernel_call(
        load_kernel,
        (
            shaped(BF16, rows, terms_len),
            pltpu.VMEM(expert_up.shape, BF16),
            pltpu.VMEM(down_rows.shape, BF16),
        ),
        (mine.astype(BF16), *(hbm(x) for x in (routes.T, route_weights.T, expert_up, down_rows))),
        (1, 2, 3, 4),
        [
            pltpu.VMEM(routes.shape[::-1], jnp.int32),
            pltpu.VMEM(routes.shape[::-1], F32),
            pltpu.SemaphoreType.DMA((4,)),
        ],
        0,
        4 * latent_len * all_units,
    )
    up_here, down_here = vmem(up_here), vmem(down_here)
    message = jnp.concatenate([across(mine).astype(BF16), terms], axis=1)
    messages = [message] + [traded(message, "exp", s) for s in range(1, exp_count)]
    messages = jnp.concatenate(messages, axis=0)
    other = traded(messages[:, :half], "tp", 1)
    pre = kernel_call(
        first_kernel,
        shaped(F32, all_rows, all_units),
        (messages, up_here),
        (),
        [],
        all_rows * latent_len * all_units,
        latent_len * all_units,
    )
    hidden, theirs = kernel_call(
        second_kernel,
        (shaped(BF16, all_rows, all_units), shaped(BF16, all_rows, half)),
        (messages, other, pre, up_here, down_here),
        (),
        [],
        2 * all_rows * latent_len * all_units,
        2 * latent_len * all_units,
    )
    mine = kernel_call(
        third_kernel,
        shaped(F32, all_rows, half),
        (hidden, down_here),
        (),
        [],
        all_rows * latent_len * all_units,
        latent_len * all_units,
    )
    part = (mine + traded(theirs, "tp", 1).astype(F32)).astype(BF16)
    blocks = part.reshape(exp_count, rows, half)
    mixed = blocks[0].astype(F32)
    for s in (exp_count - 1, *range(1, exp_count - 1)):
        mixed = mixed + traded(blocks[s], "exp", s).astype(F32)
    mixed = across(mixed).astype(BF16)
    lat_up = vmem(lat_up)
    own_part = kernel_call(
        up_own_kernel,
        shaped(F32, rows, out_len),
        (mixed, lat_up),
        (),
        [],
        rows * latent_len * out_len,
        latent_len * out_len,
    )
    return kernel_call(
        up_kernel,
        shaped(BF16, rows, out_len),
        (own_part, traded(mixed, "tp", 1), lat_up),
        (),
        [pltpu.VMEM((rows, out_len), BF16), pltpu.SemaphoreType.DMA((2,))],
        rows * latent_len * out_len,
        latent_len * out_len,
        pltpu.HBM,
    )


def solution(mesh):
    return jax.shard_map(
        on_device,
        mesh=mesh,
        in_specs=(
            P(("grp", "exp"), "tp"),
            P(None, "tp"),
            P(None, "tp"),
            P("exp", "tp", None),
            P("exp", "tp", None),
            P(("grp", "exp"), None),
            P(("grp", "exp"), None),
        ),
        out_specs=P(("grp", "exp"), "tp"),
        check_vma=False,
    )
```

```python
import jax
import jax.numpy as jnp
from jax import lax
from jax.experimental import pallas as pl
from jax.experimental.pallas import tpu as pltpu
from jax.sharding import PartitionSpec as P

BF16, F32 = jnp.bfloat16, jnp.float32
NT = (((1,), (1,)), ((), ()))
NN = (((1,), (0,)), ((), ()))
VMEM_LIMIT = 24 << 20
LANES = 128
CHUNKS = 2


def hbm(x):
    return pltpu.with_memory_space_constraint(x, pltpu.HBM)


def vmem(x):
    return pltpu.with_memory_space_constraint(x, pltpu.VMEM)


def shaped(dtype, *shape):
    return jax.ShapeDtypeStruct(shape, dtype)


def kernel_call(body, out_shape, args, in_hbm, scratch, flops, moved, out_space=pltpu.VMEM):
    def spec(space):
        return pl.BlockSpec(memory_space=space)

    return pl.pallas_call(
        body,
        out_shape=out_shape,
        in_specs=[spec(pltpu.HBM if i in in_hbm else pltpu.VMEM) for i in range(len(args))],
        out_specs=jax.tree.map(lambda _: spec(out_space), out_shape),
        scratch_shapes=scratch,
        compiler_params=pltpu.CompilerParams(vmem_limit_bytes=VMEM_LIMIT),
        cost_estimate=pl.CostEstimate(flops=flops, bytes_accessed=moved, transcendentals=0),
    )(*args)


def dot(a, b, dims):
    return lax.dot_general(a, b, dims, preferred_element_type=F32)


def half_at(own, half):
    odd = lax.axis_index("tp") % 2
    return pl.multiple_of((odd if own else 1 - odd) * half, half)


def down_kernel(tokens_hbm, weight_hbm, theirs_ref, tokens, mine_weight, weight, sems):
    half = theirs_ref.shape[1]
    size = half // CHUNKS
    load = pltpu.make_async_copy(tokens_hbm, tokens, sems.at[0])
    load.start()
    chunks = []
    for i in range(CHUNKS):
        start = pl.multiple_of(half_at(False, half) + i * size, size)
        chunks.append(
            pltpu.make_async_copy(
                weight_hbm.at[pl.ds(start, size), :],
                weight.at[pl.ds(i * size, size), :],
                sems.at[2 + i],
            )
        )
        chunks[i].start()
    later = pltpu.make_async_copy(
        weight_hbm.at[pl.ds(half_at(True, half), half), :], mine_weight, sems.at[1]
    )
    later.start()
    load.wait()
    x = tokens[...]
    for i in range(CHUNKS):
        chunks[i].wait()
        at = slice(i * size, (i + 1) * size)
        theirs_ref[:, at] = dot(x, weight[at, :], NT).astype(BF16)
    later.wait()


def down_own_kernel(tokens_ref, weight_ref, mine_ref):
    mine_ref[...] = dot(tokens_ref[...], weight_ref[...], NT)


def load_kernel(
    after_ref, routes_hbm, scale_hbm, up_hbm, down_hbm, terms_ref, up_ref, down_ref,
    routes, scale, sems,
):
    pairs = [(routes_hbm, routes), (scale_hbm, scale), (up_hbm, up_ref), (down_hbm, down_ref)]
    copies = [pltpu.make_async_copy(a, b, sems.at[i]) for i, (a, b) in enumerate(pairs)]
    for copy in copies:
        copy.start()
    copies[0].wait()
    copies[1].wait()
    rows, width = terms_ref.shape
    row = lax.broadcasted_iota(jnp.int32, (width, rows), 0)
    experts_all = width // 2
    expert = jnp.where(row < experts_all, row, row - experts_all)
    combine = jnp.zeros((width, rows), F32)
    for r in range(routes.shape[0]):
        combine += jnp.where(expert == routes[r : r + 1, :], scale[r : r + 1, :], 0.0)
    high = combine.astype(BF16).astype(F32)
    combine = jnp.where(row < experts_all, high, combine - high)
    combine = jnp.concatenate([combine, jnp.zeros((width, LANES - rows), F32)], axis=1)
    terms_ref[...] = combine.T[:rows, :].astype(BF16)
    copies[2].wait()
    copies[3].wait()


def first_kernel(messages_ref, up_ref, pre_ref):
    local_count, units, latent_len = up_ref.shape
    half = latent_len // 2
    rows = messages_ref[:, :half]
    for k in range(local_count):
        weight = up_ref[k, :, pl.ds(half_at(True, half), half)]
        pre_ref[:, k * units : (k + 1) * units] = dot(rows, weight, NT)


def second_kernel(messages_ref, other_ref, pre_ref, up_ref, down_ref, hidden_ref, theirs_ref):
    local_count, units, latent_len = up_ref.shape
    half = latent_len // 2
    terms = messages_ref[:, half:].astype(F32)
    lane = lax.broadcasted_iota(jnp.int32, terms.shape, 1)
    first = lax.axis_index("exp") * local_count
    rows = other_ref[...]
    for k in range(local_count):
        named = (lane == first + k) | (lane == first + k + terms.shape[1] // 2)
        weight = jnp.sum(jnp.where(named, terms, 0.0), axis=1, keepdims=True)
        at = slice(k * units, (k + 1) * units)
        pre_act = pre_ref[:, at] + dot(rows, up_ref[k, :, pl.ds(half_at(False, half), half)], NT)
        active = jnp.maximum(pre_act, 0.0)
        hidden_ref[:, at] = (active * active * weight).astype(BF16)
    theirs = dot(hidden_ref[...], down_ref[:, pl.ds(half_at(False, half), half)], NN)
    theirs_ref[...] = theirs.astype(BF16)


def third_kernel(hidden_ref, down_ref, mine_ref):
    half = mine_ref.shape[1]
    mine_ref[...] = dot(hidden_ref[...], down_ref[:, pl.ds(half_at(True, half), half)], NN)


def up_own_kernel(own_ref, weight_ref, out_ref):
    half = own_ref.shape[1]
    out_ref[...] = dot(own_ref[...], weight_ref[pl.ds(half_at(True, half), half), :], NN)


def up_kernel(part_ref, other_ref, weight_ref, out_hbm, out, sems):
    other = other_ref[...]
    at_rows = pl.ds(half_at(False, other.shape[1]), other.shape[1])
    half = out.shape[1] // 2
    copies = []
    for i in range(2):
        at = slice(i * half, (i + 1) * half)
        out[:, at] = (part_ref[:, at] + dot(other, weight_ref[at_rows, at], NN)).astype(BF16)
        copies.append(pltpu.make_async_copy(out.at[:, at], out_hbm.at[:, at], sems.at[i]))
        copies[i].start()
    for copy in copies:
        copy.wait()


def on_device(tokens, lat_down, lat_up, expert_up, expert_down, routes, route_weights):
    exp_count, tp_count = lax.axis_size("exp"), lax.axis_size("tp")
    local_count, units, latent_len = expert_up.shape
    rows, width = tokens.shape
    half = latent_len // 2
    all_rows = exp_count * rows
    all_units = local_count * units
    out_len = lat_up.shape[1]
    terms_len = -(-2 * local_count * exp_count // LANES) * LANES
    pair_masks = [1 << b for b in range(1, tp_count.bit_length() - 1)]

    def traded(x, axis, mask):
        return lax.ppermute(x, axis, [(i, i ^ mask) for i in range(lax.axis_size(axis))])

    def turned(x, shift):
        return lax.ppermute(x, "exp", [(i, (i + shift) % exp_count) for i in range(exp_count)])

    def across(x):
        for mask in pair_masks:
            x = x + traded(x.astype(BF16), "tp", mask).astype(F32)
        return x

    theirs, tokens_here, weight_here = kernel_call(
        down_kernel,
        (
            shaped(BF16, rows, half),
            pltpu.VMEM((rows, width), BF16),
            pltpu.VMEM((half, width), BF16),
        ),
        (hbm(tokens), hbm(lat_down)),
        (0, 1),
        [pltpu.VMEM((half, width), BF16), pltpu.SemaphoreType.DMA((CHUNKS + 2,))],
        2 * rows * width * half,
        4 * width * half,
    )
    mine = kernel_call(
        down_own_kernel,
        shaped(F32, rows, half),
        (vmem(tokens_here), vmem(weight_here)),
        (),
        [],
        2 * rows * width * half,
        2 * width * half,
    )
    mine = mine + traded(theirs, "tp", 1).astype(F32)
    down_rows = expert_down.reshape(all_units, latent_len)
    terms, up_here, down_here = kernel_call(
        load_kernel,
        (
            shaped(BF16, rows, terms_len),
            pltpu.VMEM(expert_up.shape, BF16),
            pltpu.VMEM(down_rows.shape, BF16),
        ),
        (mine.astype(BF16), *(hbm(x) for x in (routes.T, route_weights.T, expert_up, down_rows))),
        (1, 2, 3, 4),
        [
            pltpu.VMEM(routes.shape[::-1], jnp.int32),
            pltpu.VMEM(routes.shape[::-1], F32),
            pltpu.SemaphoreType.DMA((4,)),
        ],
        0,
        4 * latent_len * all_units,
    )
    up_here, down_here = vmem(up_here), vmem(down_here)
    message = jnp.concatenate([across(mine).astype(BF16), terms], axis=1)
    order = (*range(2, exp_count), 1)
    found = {s: turned(message, s) for s in order}
    messages = jnp.concatenate([message] + [found[s] for s in range(1, exp_count)], axis=0)
    other = traded(messages[:, :half], "tp", 1)
    pre = kernel_call(
        first_kernel,
        shaped(F32, all_rows, all_units),
        (messages, up_here),
        (),
        [],
        all_rows * latent_len * all_units,
        latent_len * all_units,
    )
    hidden, theirs = kernel_call(
        second_kernel,
        (shaped(BF16, all_rows, all_units), shaped(BF16, all_rows, half)),
        (messages, other, pre, up_here, down_here),
        (),
        [],
        2 * all_rows * latent_len * all_units,
        2 * latent_len * all_units,
    )
    mine = kernel_call(
        third_kernel,
        shaped(F32, all_rows, half),
        (hidden, down_here),
        (),
        [],
        all_rows * latent_len * all_units,
        latent_len * all_units,
    )
    part = (mine + traded(theirs, "tp", 1).astype(F32)).astype(BF16)
    blocks = part.reshape(exp_count, rows, half)
    mixed = blocks[0].astype(F32)
    for s in range(1, exp_count):
        mixed = mixed + turned(blocks[s], exp_count - s).astype(F32)
    mixed = across(mixed).astype(BF16)
    lat_up = vmem(lat_up)
    own_part = kernel_call(
        up_own_kernel,
        shaped(F32, rows, out_len),
        (mixed, lat_up),
        (),
        [],
        rows * latent_len * out_len,
        latent_len * out_len,
    )
    return kernel_call(
        up_kernel,
        shaped(BF16, rows, out_len),
        (own_part, traded(mixed, "tp", 1), lat_up),
        (),
        [pltpu.VMEM((rows, out_len), BF16), pltpu.SemaphoreType.DMA((2,))],
        rows * latent_len * out_len,
        latent_len * out_len,
        pltpu.HBM,
    )


def solution(mesh):
    return jax.shard_map(
        on_device,
        mesh=mesh,
        in_specs=(
            P(("grp", "exp"), "tp"),
            P(None, "tp"),
            P(None, "tp"),
            P("exp", "tp", None),
            P("exp", "tp", None),
            P(("grp", "exp"), None),
            P(("grp", "exp"), None),
        ),
        out_specs=P(("grp", "exp"), "tp"),
        check_vma=False,
    )
```

```python
import jax
import jax.numpy as jnp
from jax import lax
from jax.experimental import pallas as pl
from jax.experimental.pallas import tpu as pltpu
from jax.sharding import PartitionSpec as P

BF16, F32 = jnp.bfloat16, jnp.float32
NT = (((1,), (1,)), ((), ()))
NN = (((1,), (0,)), ((), ()))
VMEM_LIMIT = 24 << 20
LANES = 128
CHUNKS = 4
STORES = 4


def hbm(x):
    return pltpu.with_memory_space_constraint(x, pltpu.HBM)


def vmem(x):
    return pltpu.with_memory_space_constraint(x, pltpu.VMEM)


def shaped(dtype, *shape):
    return jax.ShapeDtypeStruct(shape, dtype)


def kernel_call(body, out_shape, args, in_hbm, scratch, flops, moved, out_space=pltpu.VMEM):
    def spec(space):
        return pl.BlockSpec(memory_space=space)

    return pl.pallas_call(
        body,
        out_shape=out_shape,
        in_specs=[spec(pltpu.HBM if i in in_hbm else pltpu.VMEM) for i in range(len(args))],
        out_specs=jax.tree.map(lambda _: spec(out_space), out_shape),
        scratch_shapes=scratch,
        compiler_params=pltpu.CompilerParams(vmem_limit_bytes=VMEM_LIMIT),
        cost_estimate=pl.CostEstimate(flops=flops, bytes_accessed=moved, transcendentals=0),
    )(*args)


def dot(a, b, dims):
    return lax.dot_general(a, b, dims, preferred_element_type=F32)


def half_at(own, half):
    odd = lax.axis_index("tp") % 2
    return pl.multiple_of((odd if own else 1 - odd) * half, half)


def down_kernel(tokens_hbm, weight_hbm, theirs_ref, tokens, mine_weight, weight, sems):
    half = theirs_ref.shape[1]
    size = half // CHUNKS
    load = pltpu.make_async_copy(tokens_hbm, tokens, sems.at[0])
    load.start()
    chunks = []
    for i in range(CHUNKS):
        start = pl.multiple_of(half_at(False, half) + i * size, size)
        chunks.append(
            pltpu.make_async_copy(
                weight_hbm.at[pl.ds(start, size), :],
                weight.at[pl.ds(i * size, size), :],
                sems.at[2 + i],
            )
        )
        chunks[i].start()
    later = pltpu.make_async_copy(
        weight_hbm.at[pl.ds(half_at(True, half), half), :], mine_weight, sems.at[1]
    )
    later.start()
    load.wait()
    x = tokens[...]
    for i in range(CHUNKS):
        chunks[i].wait()
        at = slice(i * size, (i + 1) * size)
        theirs_ref[:, at] = dot(x, weight[at, :], NT).astype(BF16)
    later.wait()


def down_own_kernel(tokens_ref, weight_ref, mine_ref):
    mine_ref[...] = dot(tokens_ref[...], weight_ref[...], NT)


def load_kernel(
    after_ref, routes_hbm, scale_hbm, up_hbm, down_hbm, terms_ref, up_ref, down_ref,
    routes, scale, sems,
):
    pairs = [(routes_hbm, routes), (scale_hbm, scale), (up_hbm, up_ref), (down_hbm, down_ref)]
    copies = [pltpu.make_async_copy(a, b, sems.at[i]) for i, (a, b) in enumerate(pairs)]
    for copy in copies:
        copy.start()
    copies[0].wait()
    copies[1].wait()
    rows, width = terms_ref.shape
    row = lax.broadcasted_iota(jnp.int32, (width, rows), 0)
    experts_all = width // 2
    expert = jnp.where(row < experts_all, row, row - experts_all)
    combine = jnp.zeros((width, rows), F32)
    for r in range(routes.shape[0]):
        combine += jnp.where(expert == routes[r : r + 1, :], scale[r : r + 1, :], 0.0)
    high = combine.astype(BF16).astype(F32)
    combine = jnp.where(row < experts_all, high, combine - high)
    combine = jnp.concatenate([combine, jnp.zeros((width, LANES - rows), F32)], axis=1)
    terms_ref[...] = combine.T[:rows, :].astype(BF16)
    copies[2].wait()
    copies[3].wait()


def first_kernel(messages_ref, up_ref, pre_ref):
    local_count, units, latent_len = up_ref.shape
    half = latent_len // 2
    rows = messages_ref[:, :half]
    for k in range(local_count):
        weight = up_ref[k, :, pl.ds(half_at(True, half), half)]
        pre_ref[:, k * units : (k + 1) * units] = dot(rows, weight, NT)


def second_kernel(messages_ref, other_ref, pre_ref, up_ref, down_ref, hidden_ref, theirs_ref):
    local_count, units, latent_len = up_ref.shape
    half = latent_len // 2
    terms = messages_ref[:, half:].astype(F32)
    lane = lax.broadcasted_iota(jnp.int32, terms.shape, 1)
    first = lax.axis_index("exp") * local_count
    rows = other_ref[...]
    for k in range(local_count):
        named = (lane == first + k) | (lane == first + k + terms.shape[1] // 2)
        weight = jnp.sum(jnp.where(named, terms, 0.0), axis=1, keepdims=True)
        at = slice(k * units, (k + 1) * units)
        pre_act = pre_ref[:, at] + dot(rows, up_ref[k, :, pl.ds(half_at(False, half), half)], NT)
        active = jnp.maximum(pre_act, 0.0)
        hidden_ref[:, at] = (active * active * weight).astype(BF16)
    theirs = dot(hidden_ref[...], down_ref[:, pl.ds(half_at(False, half), half)], NN)
    theirs_ref[...] = theirs.astype(BF16)


def third_kernel(hidden_ref, down_ref, mine_ref):
    half = mine_ref.shape[1]
    mine_ref[...] = dot(hidden_ref[...], down_ref[:, pl.ds(half_at(True, half), half)], NN)


def up_own_kernel(own_ref, weight_ref, out_ref):
    half = own_ref.shape[1]
    out_ref[...] = dot(own_ref[...], weight_ref[pl.ds(half_at(True, half), half), :], NN)


def up_kernel(part_ref, other_ref, weight_ref, out_hbm, out, sems):
    other = other_ref[...]
    at_rows = pl.ds(half_at(False, other.shape[1]), other.shape[1])
    size = out.shape[1] // STORES
    copies = []
    for i in range(STORES):
        at = slice(i * size, (i + 1) * size)
        out[:, at] = (part_ref[:, at] + dot(other, weight_ref[at_rows, at], NN)).astype(BF16)
        copies.append(pltpu.make_async_copy(out.at[:, at], out_hbm.at[:, at], sems.at[i]))
        copies[i].start()
    for copy in copies:
        copy.wait()


def on_device(tokens, lat_down, lat_up, expert_up, expert_down, routes, route_weights):
    exp_count, tp_count = lax.axis_size("exp"), lax.axis_size("tp")
    local_count, units, latent_len = expert_up.shape
    rows, width = tokens.shape
    half = latent_len // 2
    all_rows = exp_count * rows
    all_units = local_count * units
    out_len = lat_up.shape[1]
    terms_len = -(-2 * local_count * exp_count // LANES) * LANES
    order = (*range(exp_count // 2, exp_count), *range(exp_count // 2 - 1, 0, -1))
    pair_masks = [1 << b for b in range(1, tp_count.bit_length() - 1)]

    def traded(x, axis, mask):
        return lax.ppermute(x, axis, [(i, i ^ mask) for i in range(lax.axis_size(axis))])

    def across(x):
        for mask in pair_masks:
            x = x + traded(x.astype(BF16), "tp", mask).astype(F32)
        return x

    theirs, tokens_here, weight_here = kernel_call(
        down_kernel,
        (
            shaped(BF16, rows, half),
            pltpu.VMEM((rows, width), BF16),
            pltpu.VMEM((half, width), BF16),
        ),
        (hbm(tokens), hbm(lat_down)),
        (0, 1),
        [pltpu.VMEM((half, width), BF16), pltpu.SemaphoreType.DMA((CHUNKS + 2,))],
        2 * rows * width * half,
        4 * width * half,
    )
    mine = kernel_call(
        down_own_kernel,
        shaped(F32, rows, half),
        (vmem(tokens_here), vmem(weight_here)),
        (),
        [],
        2 * rows * width * half,
        2 * width * half,
    )
    mine = mine + traded(theirs, "tp", 1).astype(F32)
    down_rows = expert_down.reshape(all_units, latent_len)
    terms, up_here, down_here = kernel_call(
        load_kernel,
        (
            shaped(BF16, rows, terms_len),
            pltpu.VMEM(expert_up.shape, BF16),
            pltpu.VMEM(down_rows.shape, BF16),
        ),
        (mine.astype(BF16), *(hbm(x) for x in (routes.T, route_weights.T, expert_up, down_rows))),
        (1, 2, 3, 4),
        [
            pltpu.VMEM(routes.shape[::-1], jnp.int32),
            pltpu.VMEM(routes.shape[::-1], F32),
            pltpu.SemaphoreType.DMA((4,)),
        ],
        0,
        4 * latent_len * all_units,
    )
    up_here, down_here = vmem(up_here), vmem(down_here)
    message = jnp.concatenate([across(mine).astype(BF16), terms], axis=1)
    found = {s: traded(message, "exp", s) for s in order[::-1]}
    messages = jnp.concatenate([message] + [found[s] for s in range(1, exp_count)], axis=0)
    other = traded(messages[:, :half], "tp", 1)
    pre = kernel_call(
        first_kernel,
        shaped(F32, all_rows, all_units),
        (messages, up_here),
        (),
        [],
        all_rows * latent_len * all_units,
        latent_len * all_units,
    )
    hidden, theirs = kernel_call(
        second_kernel,
        (shaped(BF16, all_rows, all_units), shaped(BF16, all_rows, half)),
        (messages, other, pre, up_here, down_here),
        (),
        [],
        2 * all_rows * latent_len * all_units,
        2 * latent_len * all_units,
    )
    mine = kernel_call(
        third_kernel,
        shaped(F32, all_rows, half),
        (hidden, down_here),
        (),
        [],
        all_rows * latent_len * all_units,
        latent_len * all_units,
    )
    part = (mine + traded(theirs, "tp", 1).astype(F32)).astype(BF16)
    blocks = part.reshape(exp_count, rows, half)
    mixed = blocks[0].astype(F32)
    for s in (order[0], *order[:0:-1]):
        mixed = mixed + traded(blocks[s], "exp", s).astype(F32)
    mixed = across(mixed).astype(BF16)
    lat_up = vmem(lat_up)
    own_part = kernel_call(
        up_own_kernel,
        shaped(F32, rows, out_len),
        (mixed, lat_up),
        (),
        [],
        rows * latent_len * out_len,
        latent_len * out_len,
    )
    return kernel_call(
        up_kernel,
        shaped(BF16, rows, out_len),
        (own_part, traded(mixed, "tp", 1), lat_up),
        (),
        [pltpu.VMEM((rows, out_len), BF16), pltpu.SemaphoreType.DMA((STORES,))],
        rows * latent_len * out_len,
        latent_len * out_len,
        pltpu.HBM,
    )


def solution(mesh):
    return jax.shard_map(
        on_device,
        mesh=mesh,
        in_specs=(
            P(("grp", "exp"), "tp"),
            P(None, "tp"),
            P(None, "tp"),
            P("exp", "tp", None),
            P("exp", "tp", None),
            P(("grp", "exp"), None),
            P(("grp", "exp"), None),
        ),
        out_specs=P(("grp", "exp"), "tp"),
        check_vma=False,
    )
```

```python
import jax
import jax.numpy as jnp
from jax import lax
from jax.experimental import pallas as pl
from jax.experimental.pallas import tpu as pltpu
from jax.sharding import PartitionSpec as P

BF16, F32 = jnp.bfloat16, jnp.float32
NT = (((1,), (1,)), ((), ()))
NN = (((1,), (0,)), ((), ()))
VMEM_LIMIT = 24 << 20
LANES = 128


def hbm(x):
    return pltpu.with_memory_space_constraint(x, pltpu.HBM)


def vmem(x):
    return pltpu.with_memory_space_constraint(x, pltpu.VMEM)


def shaped(dtype, *shape):
    return jax.ShapeDtypeStruct(shape, dtype)


def kernel_call(body, out_shape, args, in_hbm, scratch, flops, moved, out_space=pltpu.VMEM):
    def spec(space):
        return pl.BlockSpec(memory_space=space)

    return pl.pallas_call(
        body,
        out_shape=out_shape,
        in_specs=[spec(pltpu.HBM if i in in_hbm else pltpu.VMEM) for i in range(len(args))],
        out_specs=jax.tree.map(lambda _: spec(out_space), out_shape),
        scratch_shapes=scratch,
        compiler_params=pltpu.CompilerParams(vmem_limit_bytes=VMEM_LIMIT),
        cost_estimate=pl.CostEstimate(flops=flops, bytes_accessed=moved, transcendentals=0),
    )(*args)


def dot(a, b, dims):
    return lax.dot_general(a, b, dims, preferred_element_type=F32)


def speaks():
    return lax.axis_index("tp") % 2 == 1


def down_kernel(tokens_hbm, weight_hbm, out_ref, tokens, weight, sems):
    length = out_ref.shape[1]
    load = pltpu.make_async_copy(tokens_hbm, tokens, sems.at[0])
    load.start()
    pieces = [slice(0, length // 4), slice(length // 4, length // 2), slice(length // 2, length)]
    copies = []
    for i, at in enumerate(pieces):
        copies.append(pltpu.make_async_copy(weight_hbm.at[at, :], weight.at[at, :], sems.at[1 + i]))
        copies[i].start()
    load.wait()
    x = tokens[...]
    for copy, at in zip(copies, pieces):
        copy.wait()
        out_ref[:, at] = dot(x, weight[at, :], NT).astype(BF16)


def load_kernel(
    after_ref, routes_hbm, scale_hbm, up_hbm, down_hbm, terms_ref, up_ref, down_ref,
    routes, scale, sems,
):
    pairs = [(routes_hbm, routes), (scale_hbm, scale), (up_hbm, up_ref), (down_hbm, down_ref)]
    copies = [pltpu.make_async_copy(a, b, sems.at[i]) for i, (a, b) in enumerate(pairs)]
    for copy in copies:
        copy.start()
    copies[0].wait()
    copies[1].wait()
    rows, width = terms_ref.shape
    row = lax.broadcasted_iota(jnp.int32, (width, rows), 0)
    experts_all = width // 2
    expert = jnp.where(row < experts_all, row, row - experts_all)
    combine = jnp.zeros((width, rows), F32)
    for r in range(routes.shape[0]):
        combine += jnp.where(expert == routes[r : r + 1, :], scale[r : r + 1, :], 0.0)
    high = combine.astype(BF16).astype(F32)
    combine = jnp.where(row < experts_all, high, combine - high)
    combine = jnp.concatenate([combine, jnp.zeros((width, LANES - rows), F32)], axis=1)
    terms_ref[...] = combine.T[:rows, :].astype(BF16)
    copies[2].wait()
    copies[3].wait()


def first_kernel(own_ref, other_ref, up_ref, pre_ref):
    local_count, units, latent_len = up_ref.shape
    half = latent_len // 2
    rows = jnp.where(speaks(), own_ref[:, :half], other_ref[:, :half])
    for k in range(local_count):
        pre_ref[:, k * units : (k + 1) * units] = dot(rows, up_ref[k, :, :half], NT)


def second_kernel(
    own_ref, other_ref, late_own_ref, late_other_ref, pre_ref, up_ref, down_ref, out_ref, hidden
):
    local_count, units, latent_len = up_ref.shape
    half = latent_len // 2
    speaking = speaks()
    terms = jnp.where(speaking, own_ref[:, half:], other_ref[:, half:]).astype(F32)
    rows = jnp.where(speaking, late_own_ref[...], late_other_ref[...])
    lane = lax.broadcasted_iota(jnp.int32, terms.shape, 1)
    first = lax.axis_index("exp") * local_count
    for k in range(local_count):
        named = (lane == first + k) | (lane == first + k + terms.shape[1] // 2)
        weight = jnp.sum(jnp.where(named, terms, 0.0), axis=1, keepdims=True)
        at = slice(k * units, (k + 1) * units)
        active = jnp.maximum(pre_ref[:, at] + dot(rows, up_ref[k, :, half:], NT), 0.0)
        hidden[:, at] = (active * active * weight).astype(BF16)
    acts = hidden[...]
    for at in (slice(0, half), slice(half, latent_len)):
        out_ref[:, at] = dot(acts, down_ref[:, at], NN).astype(BF16)


def up_kernel(own_ref, other_ref, weight_ref, out_hbm, out, sems):
    mixed = jnp.where(speaks(), own_ref[...], other_ref[...])
    half = out.shape[1] // 2
    copies = []
    for i in range(2):
        at = slice(i * half, (i + 1) * half)
        out[:, at] = dot(mixed, weight_ref[:, at], NN).astype(BF16)
        copies.append(pltpu.make_async_copy(out.at[:, at], out_hbm.at[:, at], sems.at[i]))
        copies[i].start()
    for copy in copies:
        copy.wait()


def on_device(tokens, lat_down, lat_up, expert_up, expert_down, routes, route_weights):
    exp_count, tp_count = lax.axis_size("exp"), lax.axis_size("tp")
    local_count, units, latent_len = expert_up.shape
    rows, width = tokens.shape
    half = latent_len // 2
    all_rows = exp_count * rows
    all_units = local_count * units
    out_len = lat_up.shape[1]
    terms_len = -(-2 * local_count * exp_count // LANES) * LANES
    pair_masks = [1 << b for b in range(1, tp_count.bit_length() - 1)]
    odd = range(1, tp_count, 2)

    def to_speaker(x):
        return lax.ppermute(x, "tp", [(t - 1, t) for t in odd])

    def from_speaker(x):
        return lax.ppermute(x, "tp", [(t, t - 1) for t in odd])

    def traded(x, mask):
        places = [(e, t) for e in range(exp_count) for t in odd]
        hops = [(e * tp_count + t, (e ^ mask) * tp_count + t) for e, t in places]
        return lax.ppermute(x, ("exp", "tp"), hops)

    def total(*parts):
        return sum(p.astype(F32) for p in parts).astype(BF16)

    def across(x):
        for mask in pair_masks:
            x = total(x, lax.ppermute(x, "tp", [(t, t ^ mask) for t in odd]))
        return x

    partial = kernel_call(
        down_kernel,
        shaped(BF16, rows, latent_len),
        (hbm(tokens), hbm(lat_down)),
        (0, 1),
        [
            pltpu.VMEM((rows, width), BF16),
            pltpu.VMEM((latent_len, width), BF16),
            pltpu.SemaphoreType.DMA((4,)),
        ],
        2 * rows * width * latent_len,
        2 * width * latent_len,
    )
    partial = total(partial, to_speaker(partial))
    down_rows = expert_down.reshape(all_units, latent_len)
    terms, up_here, down_here = kernel_call(
        load_kernel,
        (
            shaped(BF16, rows, terms_len),
            pltpu.VMEM(expert_up.shape, BF16),
            pltpu.VMEM(down_rows.shape, BF16),
        ),
        (partial, *(hbm(x) for x in (routes.T, route_weights.T, expert_up, down_rows))),
        (1, 2, 3, 4),
        [
            pltpu.VMEM(routes.shape[::-1], jnp.int32),
            pltpu.VMEM(routes.shape[::-1], F32),
            pltpu.SemaphoreType.DMA((4,)),
        ],
        0,
        4 * latent_len * all_units,
    )
    up_here, down_here = vmem(up_here), vmem(down_here)
    latent = across(partial)
    message = jnp.concatenate([latent[:, :half], terms, latent[:, half:]], axis=1)
    messages = [message] + [traded(message, s) for s in range(1, exp_count)]
    messages = jnp.concatenate(messages, axis=0)
    early, late = messages[:, : half + terms_len], messages[:, half + terms_len :]
    early_other, late_other = from_speaker(early), from_speaker(late)
    pre = kernel_call(
        first_kernel,
        shaped(F32, all_rows, all_units),
        (early, early_other, up_here),
        (),
        [],
        all_rows * latent_len * all_units,
        latent_len * all_units,
    )
    part = kernel_call(
        second_kernel,
        shaped(BF16, all_rows, latent_len),
        (early, early_other, late, late_other, pre, up_here, down_here),
        (),
        [pltpu.VMEM((all_rows, all_units), BF16)],
        3 * all_rows * latent_len * all_units,
        3 * latent_len * all_units,
    )
    part = total(part, to_speaker(part))
    blocks = part.reshape(exp_count, rows, latent_len)
    mixed = blocks[0].astype(F32)
    for s in (exp_count - 1, *range(1, exp_count - 1)):
        mixed = mixed + traded(blocks[s], s).astype(F32)
    mixed = across(mixed.astype(BF16))
    return kernel_call(
        up_kernel,
        shaped(BF16, rows, out_len),
        (mixed, from_speaker(mixed), vmem(lat_up)),
        (),
        [pltpu.VMEM((rows, out_len), BF16), pltpu.SemaphoreType.DMA((2,))],
        2 * rows * latent_len * out_len,
        2 * latent_len * out_len,
        pltpu.HBM,
    )


def solution(mesh):
    return jax.shard_map(
        on_device,
        mesh=mesh,
        in_specs=(
            P(("grp", "exp"), "tp"),
            P(None, "tp"),
            P(None, "tp"),
            P("exp", "tp", None),
            P("exp", "tp", None),
            P(("grp", "exp"), None),
            P(("grp", "exp"), None),
        ),
        out_specs=P(("grp", "exp"), "tp"),
        check_vma=False,
    )
```

```python
import jax
import jax.numpy as jnp
from jax import lax
from jax.experimental import pallas as pl
from jax.experimental.pallas import tpu as pltpu
from jax.sharding import PartitionSpec as P

BF16, F32 = jnp.bfloat16, jnp.float32
NT = (((1,), (1,)), ((), ()))
NN = (((1,), (0,)), ((), ()))
VMEM_LIMIT = 24 << 20
LANES = 128
CHUNKS = 2


def hbm(x):
    return pltpu.with_memory_space_constraint(x, pltpu.HBM)


def vmem(x):
    return pltpu.with_memory_space_constraint(x, pltpu.VMEM)


def shaped(dtype, *shape):
    return jax.ShapeDtypeStruct(shape, dtype)


def kernel_call(body, out_shape, args, in_hbm, scratch, flops, moved, out_space=pltpu.VMEM):
    def spec(space):
        return pl.BlockSpec(memory_space=space)

    return pl.pallas_call(
        body,
        out_shape=out_shape,
        in_specs=[spec(pltpu.HBM if i in in_hbm else pltpu.VMEM) for i in range(len(args))],
        out_specs=jax.tree.map(lambda _: spec(out_space), out_shape),
        scratch_shapes=scratch,
        compiler_params=pltpu.CompilerParams(vmem_limit_bytes=VMEM_LIMIT),
        cost_estimate=pl.CostEstimate(flops=flops, bytes_accessed=moved, transcendentals=0),
    )(*args)


def dot(a, b, dims):
    return lax.dot_general(a, b, dims, preferred_element_type=F32)


def half_at(own, half):
    bits = lax.axis_index("exp") // (lax.axis_size("exp") // 2)
    for b in range(lax.axis_size("tp").bit_length() - 1):
        bits = bits + lax.axis_index("tp") // (1 << b)
    odd = bits % 2
    return pl.multiple_of((odd if own else 1 - odd) * half, half)


def down_kernel(tokens_hbm, weight_hbm, theirs_ref, tokens, mine_weight, weight, sems):
    half = theirs_ref.shape[1]
    size = half // CHUNKS
    load = pltpu.make_async_copy(tokens_hbm, tokens, sems.at[0])
    load.start()
    chunks = []
    for i in range(CHUNKS):
        start = pl.multiple_of(half_at(False, half) + i * size, size)
        chunks.append(
            pltpu.make_async_copy(
                weight_hbm.at[pl.ds(start, size), :],
                weight.at[pl.ds(i * size, size), :],
                sems.at[2 + i],
            )
        )
        chunks[i].start()
    later = pltpu.make_async_copy(
        weight_hbm.at[pl.ds(half_at(True, half), half), :], mine_weight, sems.at[1]
    )
    later.start()
    load.wait()
    x = tokens[...]
    for i in range(CHUNKS):
        chunks[i].wait()
        at = slice(i * size, (i + 1) * size)
        theirs_ref[:, at] = dot(x, weight[at, :], NT).astype(BF16)
    later.wait()


def down_own_kernel(tokens_ref, weight_ref, mine_ref):
    mine_ref[...] = dot(tokens_ref[...], weight_ref[...], NT)


def load_kernel(
    after_ref, routes_hbm, scale_hbm, up_hbm, down_hbm, terms_ref, up_ref, down_ref,
    routes, scale, sems,
):
    pairs = [(routes_hbm, routes), (scale_hbm, scale), (up_hbm, up_ref), (down_hbm, down_ref)]
    copies = [pltpu.make_async_copy(a, b, sems.at[i]) for i, (a, b) in enumerate(pairs)]
    for copy in copies:
        copy.start()
    copies[0].wait()
    copies[1].wait()
    rows, width = terms_ref.shape
    row = lax.broadcasted_iota(jnp.int32, (width, rows), 0)
    experts_all = width // 2
    expert = jnp.where(row < experts_all, row, row - experts_all)
    combine = jnp.zeros((width, rows), F32)
    for r in range(routes.shape[0]):
        combine += jnp.where(expert == routes[r : r + 1, :], scale[r : r + 1, :], 0.0)
    high = combine.astype(BF16).astype(F32)
    combine = jnp.where(row < experts_all, high, combine - high)
    combine = jnp.concatenate([combine, jnp.zeros((width, LANES - rows), F32)], axis=1)
    terms_ref[...] = combine.T[:rows, :].astype(BF16)
    copies[2].wait()
    copies[3].wait()


def first_kernel(messages_ref, up_ref, pre_ref):
    local_count, units, latent_len = up_ref.shape
    half = latent_len // 2
    rows = messages_ref[:, :half]
    for k in range(local_count):
        weight = up_ref[k, :, pl.ds(half_at(True, half), half)]
        pre_ref[:, k * units : (k + 1) * units] = dot(rows, weight, NT)


def second_kernel(messages_ref, other_ref, pre_ref, up_ref, down_ref, hidden_ref, theirs_ref):
    local_count, units, latent_len = up_ref.shape
    half = latent_len // 2
    terms = messages_ref[:, half:].astype(F32)
    lane = lax.broadcasted_iota(jnp.int32, terms.shape, 1)
    first = lax.axis_index("exp") * local_count
    rows = other_ref[...]
    for k in range(local_count):
        named = (lane == first + k) | (lane == first + k + terms.shape[1] // 2)
        weight = jnp.sum(jnp.where(named, terms, 0.0), axis=1, keepdims=True)
        at = slice(k * units, (k + 1) * units)
        pre_act = pre_ref[:, at] + dot(rows, up_ref[k, :, pl.ds(half_at(False, half), half)], NT)
        active = jnp.maximum(pre_act, 0.0)
        hidden_ref[:, at] = (active * active * weight).astype(BF16)
    theirs = dot(hidden_ref[...], down_ref[:, pl.ds(half_at(False, half), half)], NN)
    theirs_ref[...] = theirs.astype(BF16)


def third_kernel(hidden_ref, down_ref, mine_ref):
    half = mine_ref.shape[1]
    mine_ref[...] = dot(hidden_ref[...], down_ref[:, pl.ds(half_at(True, half), half)], NN)


def up_own_kernel(own_ref, weight_ref, out_ref):
    half = own_ref.shape[1]
    out_ref[...] = dot(own_ref[...], weight_ref[pl.ds(half_at(True, half), half), :], NN)


def up_kernel(part_ref, other_ref, weight_ref, out_hbm, out, sems):
    other = other_ref[...]
    at_rows = pl.ds(half_at(False, other.shape[1]), other.shape[1])
    half = out.shape[1] // 2
    copies = []
    for i in range(2):
        at = slice(i * half, (i + 1) * half)
        out[:, at] = (part_ref[:, at] + dot(other, weight_ref[at_rows, at], NN)).astype(BF16)
        copies.append(pltpu.make_async_copy(out.at[:, at], out_hbm.at[:, at], sems.at[i]))
        copies[i].start()
    for copy in copies:
        copy.wait()


def on_device(tokens, lat_down, lat_up, expert_up, expert_down, routes, route_weights):
    exp_count, tp_count = lax.axis_size("exp"), lax.axis_size("tp")
    local_count, units, latent_len = expert_up.shape
    rows, width = tokens.shape
    half = latent_len // 2
    all_rows = exp_count * rows
    all_units = local_count * units
    out_len = lat_up.shape[1]
    terms_len = -(-2 * local_count * exp_count // LANES) * LANES
    pair_masks = [(1 << b) + 1 for b in range(1, tp_count.bit_length() - 1)]

    def over_tp(x, mask):
        return lax.ppermute(x, "tp", [(t, t ^ mask) for t in range(tp_count)])

    def over_exp(x, mask):
        turn = mask // (exp_count // 2)
        places = [(e, t) for e in range(exp_count) for t in range(tp_count)]
        hops = [(e * tp_count + t, (e ^ mask) * tp_count + (t ^ turn)) for e, t in places]
        return lax.ppermute(x, ("exp", "tp"), hops)

    def across(x):
        for mask in pair_masks:
            x = x + over_tp(x.astype(BF16), mask).astype(F32)
        return x

    theirs, tokens_here, weight_here = kernel_call(
        down_kernel,
        (
            shaped(BF16, rows, half),
            pltpu.VMEM((rows, width), BF16),
            pltpu.VMEM((half, width), BF16),
        ),
        (hbm(tokens), hbm(lat_down)),
        (0, 1),
        [pltpu.VMEM((half, width), BF16), pltpu.SemaphoreType.DMA((CHUNKS + 2,))],
        2 * rows * width * half,
        4 * width * half,
    )
    mine = kernel_call(
        down_own_kernel,
        shaped(F32, rows, half),
        (vmem(tokens_here), vmem(weight_here)),
        (),
        [],
        2 * rows * width * half,
        2 * width * half,
    )
    mine = mine + over_tp(theirs, 1).astype(F32)
    down_rows = expert_down.reshape(all_units, latent_len)
    terms, up_here, down_here = kernel_call(
        load_kernel,
        (
            shaped(BF16, rows, terms_len),
            pltpu.VMEM(expert_up.shape, BF16),
            pltpu.VMEM(down_rows.shape, BF16),
        ),
        (mine.astype(BF16), *(hbm(x) for x in (routes.T, route_weights.T, expert_up, down_rows))),
        (1, 2, 3, 4),
        [
            pltpu.VMEM(routes.shape[::-1], jnp.int32),
            pltpu.VMEM(routes.shape[::-1], F32),
            pltpu.SemaphoreType.DMA((4,)),
        ],
        0,
        4 * latent_len * all_units,
    )
    up_here, down_here = vmem(up_here), vmem(down_here)
    message = jnp.concatenate([across(mine).astype(BF16), terms], axis=1)
    messages = [message] + [over_exp(message, s) for s in range(1, exp_count)]
    messages = jnp.concatenate(messages, axis=0)
    other = over_tp(messages[:, :half], 1)
    pre = kernel_call(
        first_kernel,
        shaped(F32, all_rows, all_units),
        (messages, up_here),
        (),
        [],
        all_rows * latent_len * all_units,
        latent_len * all_units,
    )
    hidden, theirs = kernel_call(
        second_kernel,
        (shaped(BF16, all_rows, all_units), shaped(BF16, all_rows, half)),
        (messages, other, pre, up_here, down_here),
        (),
        [],
        2 * all_rows * latent_len * all_units,
        2 * latent_len * all_units,
    )
    mine = kernel_call(
        third_kernel,
        shaped(F32, all_rows, half),
        (hidden, down_here),
        (),
        [],
        all_rows * latent_len * all_units,
        latent_len * all_units,
    )
    part = (mine + over_tp(theirs, 1).astype(F32)).astype(BF16)
    blocks = part.reshape(exp_count, rows, half)
    mixed = blocks[0].astype(F32)
    for s in (exp_count - 1, *range(1, exp_count - 1)):
        mixed = mixed + over_exp(blocks[s], s).astype(F32)
    mixed = across(mixed).astype(BF16)
    lat_up = vmem(lat_up)
    own_part = kernel_call(
        up_own_kernel,
        shaped(F32, rows, out_len),
        (mixed, lat_up),
        (),
        [],
        rows * latent_len * out_len,
        latent_len * out_len,
    )
    return kernel_call(
        up_kernel,
        shaped(BF16, rows, out_len),
        (own_part, over_tp(mixed, 1), lat_up),
        (),
        [pltpu.VMEM((rows, out_len), BF16), pltpu.SemaphoreType.DMA((2,))],
        rows * latent_len * out_len,
        latent_len * out_len,
        pltpu.HBM,
    )


def solution(mesh):
    return jax.shard_map(
        on_device,
        mesh=mesh,
        in_specs=(
            P(("grp", "exp"), "tp"),
            P(None, "tp"),
            P(None, "tp"),
            P("exp", "tp", None),
            P("exp", "tp", None),
            P(("grp", "exp"), None),
            P(("grp", "exp"), None),
        ),
        out_specs=P(("grp", "exp"), "tp"),
        check_vma=False,
    )
```

```python
import jax
import jax.numpy as jnp
from jax import lax
from jax.experimental import pallas as pl
from jax.experimental.pallas import tpu as pltpu
from jax.sharding import PartitionSpec as P

BF16, F32 = jnp.bfloat16, jnp.float32
NT = (((1,), (1,)), ((), ()))
NN = (((1,), (0,)), ((), ()))
VMEM_LIMIT = 24 << 20
LANES = 128
CHUNKS = 2


def hbm(x):
    return pltpu.with_memory_space_constraint(x, pltpu.HBM)


def vmem(x):
    return pltpu.with_memory_space_constraint(x, pltpu.VMEM)


def shaped(dtype, *shape):
    return jax.ShapeDtypeStruct(shape, dtype)


def kernel_call(body, out_shape, args, in_hbm, scratch, flops, moved, out_space=pltpu.VMEM):
    def spec(space):
        return pl.BlockSpec(memory_space=space)

    return pl.pallas_call(
        body,
        out_shape=out_shape,
        in_specs=[spec(pltpu.HBM if i in in_hbm else pltpu.VMEM) for i in range(len(args))],
        out_specs=jax.tree.map(lambda _: spec(out_space), out_shape),
        scratch_shapes=scratch,
        compiler_params=pltpu.CompilerParams(vmem_limit_bytes=VMEM_LIMIT),
        cost_estimate=pl.CostEstimate(flops=flops, bytes_accessed=moved, transcendentals=0),
    )(*args)


def dot(a, b, dims):
    return lax.dot_general(a, b, dims, preferred_element_type=F32)


def half_at(own, half):
    bits = 0
    for axis in ("exp", "tp"):
        for b in range(lax.axis_size(axis).bit_length() - 1):
            bits = bits + lax.axis_index(axis) // (1 << b)
    odd = bits % 2
    return pl.multiple_of((odd if own else 1 - odd) * half, half)


def down_kernel(tokens_hbm, weight_hbm, theirs_ref, tokens, mine_weight, weight, sems):
    half = theirs_ref.shape[1]
    size = half // CHUNKS
    load = pltpu.make_async_copy(tokens_hbm, tokens, sems.at[0])
    load.start()
    chunks = []
    for i in range(CHUNKS):
        start = pl.multiple_of(half_at(False, half) + i * size, size)
        chunks.append(
            pltpu.make_async_copy(
                weight_hbm.at[pl.ds(start, size), :],
                weight.at[pl.ds(i * size, size), :],
                sems.at[2 + i],
            )
        )
        chunks[i].start()
    later = pltpu.make_async_copy(
        weight_hbm.at[pl.ds(half_at(True, half), half), :], mine_weight, sems.at[1]
    )
    later.start()
    load.wait()
    x = tokens[...]
    for i in range(CHUNKS):
        chunks[i].wait()
        at = slice(i * size, (i + 1) * size)
        theirs_ref[:, at] = dot(x, weight[at, :], NT).astype(BF16)
    later.wait()


def down_own_kernel(tokens_ref, weight_ref, mine_ref):
    mine_ref[...] = dot(tokens_ref[...], weight_ref[...], NT)


def load_kernel(
    after_ref, routes_hbm, scale_hbm, up_hbm, down_hbm, terms_ref, up_ref, down_ref,
    routes, scale, sems,
):
    pairs = [(routes_hbm, routes), (scale_hbm, scale), (up_hbm, up_ref), (down_hbm, down_ref)]
    copies = [pltpu.make_async_copy(a, b, sems.at[i]) for i, (a, b) in enumerate(pairs)]
    for copy in copies:
        copy.start()
    copies[0].wait()
    copies[1].wait()
    rows, width = terms_ref.shape
    row = lax.broadcasted_iota(jnp.int32, (width, rows), 0)
    experts_all = width // 2
    expert = jnp.where(row < experts_all, row, row - experts_all)
    combine = jnp.zeros((width, rows), F32)
    for r in range(routes.shape[0]):
        combine += jnp.where(expert == routes[r : r + 1, :], scale[r : r + 1, :], 0.0)
    high = combine.astype(BF16).astype(F32)
    combine = jnp.where(row < experts_all, high, combine - high)
    combine = jnp.concatenate([combine, jnp.zeros((width, LANES - rows), F32)], axis=1)
    terms_ref[...] = combine.T[:rows, :].astype(BF16)
    copies[2].wait()
    copies[3].wait()


def first_kernel(messages_ref, up_ref, pre_ref):
    local_count, units, latent_len = up_ref.shape
    half = latent_len // 2
    rows = messages_ref[:, :half]
    for k in range(local_count):
        weight = up_ref[k, :, pl.ds(half_at(True, half), half)]
        pre_ref[:, k * units : (k + 1) * units] = dot(rows, weight, NT)


def second_kernel(messages_ref, other_ref, pre_ref, up_ref, down_ref, hidden_ref, theirs_ref):
    local_count, units, latent_len = up_ref.shape
    half = latent_len // 2
    terms = messages_ref[:, half:].astype(F32)
    lane = lax.broadcasted_iota(jnp.int32, terms.shape, 1)
    first = lax.axis_index("exp") * local_count
    rows = other_ref[...]
    for k in range(local_count):
        named = (lane == first + k) | (lane == first + k + terms.shape[1] // 2)
        weight = jnp.sum(jnp.where(named, terms, 0.0), axis=1, keepdims=True)
        at = slice(k * units, (k + 1) * units)
        pre_act = pre_ref[:, at] + dot(rows, up_ref[k, :, pl.ds(half_at(False, half), half)], NT)
        active = jnp.maximum(pre_act, 0.0)
        hidden_ref[:, at] = (active * active * weight).astype(BF16)
    theirs = dot(hidden_ref[...], down_ref[:, pl.ds(half_at(False, half), half)], NN)
    theirs_ref[...] = theirs.astype(BF16)


def third_kernel(hidden_ref, down_ref, mine_ref):
    half = mine_ref.shape[1]
    mine_ref[...] = dot(hidden_ref[...], down_ref[:, pl.ds(half_at(True, half), half)], NN)


def up_own_kernel(own_ref, weight_ref, out_ref):
    half = own_ref.shape[1]
    out_ref[...] = dot(own_ref[...], weight_ref[pl.ds(half_at(True, half), half), :], NN)


def up_kernel(part_ref, other_ref, weight_ref, out_hbm, out, sems):
    other = other_ref[...]
    at_rows = pl.ds(half_at(False, other.shape[1]), other.shape[1])
    half = out.shape[1] // 2
    copies = []
    for i in range(2):
        at = slice(i * half, (i + 1) * half)
        out[:, at] = (part_ref[:, at] + dot(other, weight_ref[at_rows, at], NN)).astype(BF16)
        copies.append(pltpu.make_async_copy(out.at[:, at], out_hbm.at[:, at], sems.at[i]))
        copies[i].start()
    for copy in copies:
        copy.wait()


def on_device(tokens, lat_down, lat_up, expert_up, expert_down, routes, route_weights):
    exp_count, tp_count = lax.axis_size("exp"), lax.axis_size("tp")
    local_count, units, latent_len = expert_up.shape
    rows, width = tokens.shape
    half = latent_len // 2
    all_rows = exp_count * rows
    all_units = local_count * units
    out_len = lat_up.shape[1]
    terms_len = -(-2 * local_count * exp_count // LANES) * LANES
    pair_masks = [(1 << b) + 1 for b in range(1, tp_count.bit_length() - 1)]

    def over_tp(x, mask):
        return lax.ppermute(x, "tp", [(t, t ^ mask) for t in range(tp_count)])

    def over_exp(x, mask):
        turn = mask.bit_count() % 2
        places = [(e, t) for e in range(exp_count) for t in range(tp_count)]
        hops = [(e * tp_count + t, (e ^ mask) * tp_count + (t ^ turn)) for e, t in places]
        return lax.ppermute(x, ("exp", "tp"), hops)

    def across(x):
        for mask in pair_masks:
            x = x + over_tp(x.astype(BF16), mask).astype(F32)
        return x

    theirs, tokens_here, weight_here = kernel_call(
        down_kernel,
        (
            shaped(BF16, rows, half),
            pltpu.VMEM((rows, width), BF16),
            pltpu.VMEM((half, width), BF16),
        ),
        (hbm(tokens), hbm(lat_down)),
        (0, 1),
        [pltpu.VMEM((half, width), BF16), pltpu.SemaphoreType.DMA((CHUNKS + 2,))],
        2 * rows * width * half,
        4 * width * half,
    )
    mine = kernel_call(
        down_own_kernel,
        shaped(F32, rows, half),
        (vmem(tokens_here), vmem(weight_here)),
        (),
        [],
        2 * rows * width * half,
        2 * width * half,
    )
    mine = mine + over_tp(theirs, 1).astype(F32)
    down_rows = expert_down.reshape(all_units, latent_len)
    terms, up_here, down_here = kernel_call(
        load_kernel,
        (
            shaped(BF16, rows, terms_len),
            pltpu.VMEM(expert_up.shape, BF16),
            pltpu.VMEM(down_rows.shape, BF16),
        ),
        (mine.astype(BF16), *(hbm(x) for x in (routes.T, route_weights.T, expert_up, down_rows))),
        (1, 2, 3, 4),
        [
            pltpu.VMEM(routes.shape[::-1], jnp.int32),
            pltpu.VMEM(routes.shape[::-1], F32),
            pltpu.SemaphoreType.DMA((4,)),
        ],
        0,
        4 * latent_len * all_units,
    )
    up_here, down_here = vmem(up_here), vmem(down_here)
    message = jnp.concatenate([across(mine).astype(BF16), terms], axis=1)
    messages = [message] + [over_exp(message, s) for s in range(1, exp_count)]
    messages = jnp.concatenate(messages, axis=0)
    other = over_tp(messages[:, :half], 1)
    pre = kernel_call(
        first_kernel,
        shaped(F32, all_rows, all_units),
        (messages, up_here),
        (),
        [],
        all_rows * latent_len * all_units,
        latent_len * all_units,
    )
    hidden, theirs = kernel_call(
        second_kernel,
        (shaped(BF16, all_rows, all_units), shaped(BF16, all_rows, half)),
        (messages, other, pre, up_here, down_here),
        (),
        [],
        2 * all_rows * latent_len * all_units,
        2 * latent_len * all_units,
    )
    mine = kernel_call(
        third_kernel,
        shaped(F32, all_rows, half),
        (hidden, down_here),
        (),
        [],
        all_rows * latent_len * all_units,
        latent_len * all_units,
    )
    part = (mine + over_tp(theirs, 1).astype(F32)).astype(BF16)
    blocks = part.reshape(exp_count, rows, half)
    mixed = blocks[0].astype(F32)
    for s in (exp_count - 1, *range(1, exp_count - 1)):
        mixed = mixed + over_exp(blocks[s], s).astype(F32)
    mixed = across(mixed).astype(BF16)
    lat_up = vmem(lat_up)
    own_part = kernel_call(
        up_own_kernel,
        shaped(F32, rows, out_len),
        (mixed, lat_up),
        (),
        [],
        rows * latent_len * out_len,
        latent_len * out_len,
    )
    return kernel_call(
        up_kernel,
        shaped(BF16, rows, out_len),
        (own_part, over_tp(mixed, 1), lat_up),
        (),
        [pltpu.VMEM((rows, out_len), BF16), pltpu.SemaphoreType.DMA((2,))],
        rows * latent_len * out_len,
        latent_len * out_len,
        pltpu.HBM,
    )


def solution(mesh):
    return jax.shard_map(
        on_device,
        mesh=mesh,
        in_specs=(
            P(("grp", "exp"), "tp"),
            P(None, "tp"),
            P(None, "tp"),
            P("exp", "tp", None),
            P("exp", "tp", None),
            P(("grp", "exp"), None),
            P(("grp", "exp"), None),
        ),
        out_specs=P(("grp", "exp"), "tp"),
        check_vma=False,
    )
```

```python
import jax
import jax.numpy as jnp
from jax import lax
from jax.experimental import pallas as pl
from jax.experimental.pallas import tpu as pltpu
from jax.sharding import PartitionSpec as P

BF16, F32 = jnp.bfloat16, jnp.float32
NT = (((1,), (1,)), ((), ()))
NN = (((1,), (0,)), ((), ()))
VMEM_LIMIT = 24 << 20
LANES = 128
CHUNKS = 2


def hbm(x):
    return pltpu.with_memory_space_constraint(x, pltpu.HBM)


def vmem(x):
    return pltpu.with_memory_space_constraint(x, pltpu.VMEM)


def shaped(dtype, *shape):
    return jax.ShapeDtypeStruct(shape, dtype)


def kernel_call(body, out_shape, args, in_hbm, scratch, flops, moved, out_space=pltpu.VMEM):
    def spec(space):
        return pl.BlockSpec(memory_space=space)

    return pl.pallas_call(
        body,
        out_shape=out_shape,
        in_specs=[spec(pltpu.HBM if i in in_hbm else pltpu.VMEM) for i in range(len(args))],
        out_specs=jax.tree.map(lambda _: spec(out_space), out_shape),
        scratch_shapes=scratch,
        compiler_params=pltpu.CompilerParams(vmem_limit_bytes=VMEM_LIMIT),
        cost_estimate=pl.CostEstimate(flops=flops, bytes_accessed=moved, transcendentals=0),
    )(*args)


def dot(a, b, dims):
    return lax.dot_general(a, b, dims, preferred_element_type=F32)


def half_at(own, half):
    bits = 0
    for axis in ("exp", "tp"):
        for b in range(lax.axis_size(axis).bit_length() - 1):
            bits = bits + lax.axis_index(axis) // (1 << b)
    odd = bits % 2
    return pl.multiple_of((odd if own else 1 - odd) * half, half)


def down_kernel(tokens_hbm, weight_hbm, theirs_ref, tokens, mine_weight, weight, sems):
    half = theirs_ref.shape[1]
    size = half // CHUNKS
    load = pltpu.make_async_copy(tokens_hbm, tokens, sems.at[0])
    load.start()
    chunks = []
    for i in range(CHUNKS):
        start = pl.multiple_of(half_at(False, half) + i * size, size)
        chunks.append(
            pltpu.make_async_copy(
                weight_hbm.at[pl.ds(start, size), :],
                weight.at[pl.ds(i * size, size), :],
                sems.at[2 + i],
            )
        )
        chunks[i].start()
    later = pltpu.make_async_copy(
        weight_hbm.at[pl.ds(half_at(True, half), half), :], mine_weight, sems.at[1]
    )
    later.start()
    load.wait()
    x = tokens[...]
    for i in range(CHUNKS):
        chunks[i].wait()
        at = slice(i * size, (i + 1) * size)
        theirs_ref[:, at] = dot(x, weight[at, :], NT).astype(BF16)
    later.wait()


def down_own_kernel(tokens_ref, weight_ref, mine_ref):
    mine_ref[...] = dot(tokens_ref[...], weight_ref[...], NT)


def load_kernel(after_ref, hbm_ref, here_ref, sem):
    copy = pltpu.make_async_copy(hbm_ref, here_ref, sem)
    copy.start()
    copy.wait()


def terms_kernel(
    after_ref, routes_hbm, scale_hbm, up_hbm, terms_ref, up_ref, routes, scale, sems
):
    pairs = [(routes_hbm, routes), (scale_hbm, scale), (up_hbm, up_ref)]
    copies = [pltpu.make_async_copy(a, b, sems.at[i]) for i, (a, b) in enumerate(pairs)]
    for copy in copies:
        copy.start()
    copies[0].wait()
    copies[1].wait()
    rows, width = terms_ref.shape
    row = lax.broadcasted_iota(jnp.int32, (width, rows), 0)
    experts_all = width // 2
    expert = jnp.where(row < experts_all, row, row - experts_all)
    combine = jnp.zeros((width, rows), F32)
    for r in range(routes.shape[0]):
        combine += jnp.where(expert == routes[r : r + 1, :], scale[r : r + 1, :], 0.0)
    high = combine.astype(BF16).astype(F32)
    combine = jnp.where(row < experts_all, high, combine - high)
    combine = jnp.concatenate([combine, jnp.zeros((width, LANES - rows), F32)], axis=1)
    terms_ref[...] = combine.T[:rows, :].astype(BF16)
    copies[2].wait()


def first_kernel(messages_ref, up_ref, pre_ref):
    local_count, units, latent_len = up_ref.shape
    half = latent_len // 2
    rows = messages_ref[:, :half]
    for k in range(local_count):
        weight = up_ref[k, :, pl.ds(half_at(True, half), half)]
        pre_ref[:, k * units : (k + 1) * units] = dot(rows, weight, NT)


def second_kernel(messages_ref, other_ref, pre_ref, up_ref, down_ref, hidden_ref, theirs_ref):
    local_count, units, latent_len = up_ref.shape
    half = latent_len // 2
    terms = messages_ref[:, half:].astype(F32)
    lane = lax.broadcasted_iota(jnp.int32, terms.shape, 1)
    first = lax.axis_index("exp") * local_count
    rows = other_ref[...]
    for k in range(local_count):
        named = (lane == first + k) | (lane == first + k + terms.shape[1] // 2)
        weight = jnp.sum(jnp.where(named, terms, 0.0), axis=1, keepdims=True)
        at = slice(k * units, (k + 1) * units)
        pre_act = pre_ref[:, at] + dot(rows, up_ref[k, :, pl.ds(half_at(False, half), half)], NT)
        active = jnp.maximum(pre_act, 0.0)
        hidden_ref[:, at] = (active * active * weight).astype(BF16)
    theirs = dot(hidden_ref[...], down_ref[:, pl.ds(half_at(False, half), half)], NN)
    theirs_ref[...] = theirs.astype(BF16)


def third_kernel(hidden_ref, down_ref, mine_ref):
    half = mine_ref.shape[1]
    mine_ref[...] = dot(hidden_ref[...], down_ref[:, pl.ds(half_at(True, half), half)], NN)


def up_own_kernel(own_ref, weight_ref, out_ref):
    half = own_ref.shape[1]
    out_ref[...] = dot(own_ref[...], weight_ref[pl.ds(half_at(True, half), half), :], NN)


def up_kernel(part_ref, other_ref, weight_ref, out_hbm, out, sems):
    other = other_ref[...]
    at_rows = pl.ds(half_at(False, other.shape[1]), other.shape[1])
    half = out.shape[1] // 2
    copies = []
    for i in range(2):
        at = slice(i * half, (i + 1) * half)
        out[:, at] = (part_ref[:, at] + dot(other, weight_ref[at_rows, at], NN)).astype(BF16)
        copies.append(pltpu.make_async_copy(out.at[:, at], out_hbm.at[:, at], sems.at[i]))
        copies[i].start()
    for copy in copies:
        copy.wait()


def on_device(tokens, lat_down, lat_up, expert_up, expert_down, routes, route_weights):
    exp_count, tp_count = lax.axis_size("exp"), lax.axis_size("tp")
    local_count, units, latent_len = expert_up.shape
    rows, width = tokens.shape
    half = latent_len // 2
    all_rows = exp_count * rows
    all_units = local_count * units
    out_len = lat_up.shape[1]
    terms_len = -(-2 * local_count * exp_count // LANES) * LANES
    pair_masks = [(1 << b) + 1 for b in range(1, tp_count.bit_length() - 1)]

    def over_tp(x, mask):
        return lax.ppermute(x, "tp", [(t, t ^ mask) for t in range(tp_count)])

    def over_exp(x, mask):
        turn = mask.bit_count() % 2
        places = [(e, t) for e in range(exp_count) for t in range(tp_count)]
        hops = [(e * tp_count + t, (e ^ mask) * tp_count + (t ^ turn)) for e, t in places]
        return lax.ppermute(x, ("exp", "tp"), hops)

    def across(x):
        for mask in pair_masks:
            x = x + over_tp(x.astype(BF16), mask).astype(F32)
        return x

    theirs, tokens_here, weight_here = kernel_call(
        down_kernel,
        (
            shaped(BF16, rows, half),
            pltpu.VMEM((rows, width), BF16),
            pltpu.VMEM((half, width), BF16),
        ),
        (hbm(tokens), hbm(lat_down)),
        (0, 1),
        [pltpu.VMEM((half, width), BF16), pltpu.SemaphoreType.DMA((CHUNKS + 2,))],
        2 * rows * width * half,
        4 * width * half,
    )
    mine = kernel_call(
        down_own_kernel,
        shaped(F32, rows, half),
        (vmem(tokens_here), vmem(weight_here)),
        (),
        [],
        2 * rows * width * half,
        2 * width * half,
    )
    mine = mine + over_tp(theirs, 1).astype(F32)
    terms, up_here = kernel_call(
        terms_kernel,
        (shaped(BF16, rows, terms_len), pltpu.VMEM(expert_up.shape, BF16)),
        (mine.astype(BF16), *(hbm(x) for x in (routes.T, route_weights.T, expert_up))),
        (1, 2, 3),
        [
            pltpu.VMEM(routes.shape[::-1], jnp.int32),
            pltpu.VMEM(routes.shape[::-1], F32),
            pltpu.SemaphoreType.DMA((3,)),
        ],
        0,
        2 * latent_len * all_units,
    )
    up_here = vmem(up_here)
    message = jnp.concatenate([across(mine).astype(BF16), terms], axis=1)
    down_rows = expert_down.reshape(all_units, latent_len)
    down_here = kernel_call(
        load_kernel,
        pltpu.VMEM(down_rows.shape, BF16),
        (message, hbm(down_rows)),
        (1,),
        [pltpu.SemaphoreType.DMA],
        0,
        2 * latent_len * all_units,
    )
    messages = [message] + [over_exp(message, s) for s in range(1, exp_count)]
    messages[-1], down_here = lax.optimization_barrier((messages[-1], down_here))
    messages, down_here = jnp.concatenate(messages, axis=0), vmem(down_here)
    other = over_tp(messages[:, :half], 1)
    pre = kernel_call(
        first_kernel,
        shaped(F32, all_rows, all_units),
        (messages, up_here),
        (),
        [],
        all_rows * latent_len * all_units,
        latent_len * all_units,
    )
    hidden, theirs = kernel_call(
        second_kernel,
        (shaped(BF16, all_rows, all_units), shaped(BF16, all_rows, half)),
        (messages, other, pre, up_here, down_here),
        (),
        [],
        2 * all_rows * latent_len * all_units,
        2 * latent_len * all_units,
    )
    mine = kernel_call(
        third_kernel,
        shaped(F32, all_rows, half),
        (hidden, down_here),
        (),
        [],
        all_rows * latent_len * all_units,
        latent_len * all_units,
    )
    part = (mine + over_tp(theirs, 1).astype(F32)).astype(BF16)
    blocks = part.reshape(exp_count, rows, half)
    mixed = blocks[0].astype(F32)
    for s in (exp_count - 1, *range(1, exp_count - 1)):
        mixed = mixed + over_exp(blocks[s], s).astype(F32)
    mixed = across(mixed).astype(BF16)
    lat_up = vmem(lat_up)
    own_part = kernel_call(
        up_own_kernel,
        shaped(F32, rows, out_len),
        (mixed, lat_up),
        (),
        [],
        rows * latent_len * out_len,
        latent_len * out_len,
    )
    return kernel_call(
        up_kernel,
        shaped(BF16, rows, out_len),
        (own_part, over_tp(mixed, 1), lat_up),
        (),
        [pltpu.VMEM((rows, out_len), BF16), pltpu.SemaphoreType.DMA((2,))],
        rows * latent_len * out_len,
        latent_len * out_len,
        pltpu.HBM,
    )


def solution(mesh):
    return jax.shard_map(
        on_device,
        mesh=mesh,
        in_specs=(
            P(("grp", "exp"), "tp"),
            P(None, "tp"),
            P(None, "tp"),
            P("exp", "tp", None),
            P("exp", "tp", None),
            P(("grp", "exp"), None),
            P(("grp", "exp"), None),
        ),
        out_specs=P(("grp", "exp"), "tp"),
        check_vma=False,
    )
```

```python
import jax
import jax.numpy as jnp
from jax import lax
from jax.experimental import pallas as pl
from jax.experimental.pallas import tpu as pltpu
from jax.sharding import PartitionSpec as P

BF16, F32 = jnp.bfloat16, jnp.float32
NT = (((1,), (1,)), ((), ()))
NN = (((1,), (0,)), ((), ()))
VMEM_LIMIT = 24 << 20
LANES = 128
CHUNKS = 1
TILE = 16


def hbm(x):
    return pltpu.with_memory_space_constraint(x, pltpu.HBM)


def vmem(x):
    return pltpu.with_memory_space_constraint(x, pltpu.VMEM)


def shaped(dtype, *shape):
    return jax.ShapeDtypeStruct(shape, dtype)


def kernel_call(body, out_shape, args, in_hbm, scratch, flops, moved, out_space=pltpu.VMEM):
    def spec(space):
        return pl.BlockSpec(memory_space=space)

    return pl.pallas_call(
        body,
        out_shape=out_shape,
        in_specs=[spec(pltpu.HBM if i in in_hbm else pltpu.VMEM) for i in range(len(args))],
        out_specs=jax.tree.map(lambda _: spec(out_space), out_shape),
        scratch_shapes=scratch,
        compiler_params=pltpu.CompilerParams(vmem_limit_bytes=VMEM_LIMIT),
        cost_estimate=pl.CostEstimate(flops=flops, bytes_accessed=moved, transcendentals=0),
    )(*args)


def dot(a, b, dims):
    return lax.dot_general(a, b, dims, preferred_element_type=F32)


def half_at(own, half):
    bits = 0
    for axis in ("exp", "tp"):
        for b in range(lax.axis_size(axis).bit_length() - 1):
            bits = bits + lax.axis_index(axis) // (1 << b)
    odd = bits % 2
    return pl.multiple_of((odd if own else 1 - odd) * half, half)


def down_kernel(tokens_hbm, weight_hbm, theirs_ref, tokens, mine_weight, weight, sems):
    half = theirs_ref.shape[1]
    size = half // CHUNKS
    load = pltpu.make_async_copy(tokens_hbm, tokens, sems.at[0])
    load.start()
    chunks = []
    for i in range(CHUNKS):
        start = pl.multiple_of(half_at(False, half) + i * size, size)
        chunks.append(
            pltpu.make_async_copy(
                weight_hbm.at[pl.ds(start, size), :],
                weight.at[pl.ds(i * size, size), :],
                sems.at[2 + i],
            )
        )
        chunks[i].start()
    later = pltpu.make_async_copy(
        weight_hbm.at[pl.ds(half_at(True, half), half), :], mine_weight, sems.at[1]
    )
    later.start()
    load.wait()
    x = tokens[...]
    for i in range(CHUNKS):
        chunks[i].wait()
        at = slice(i * size, (i + 1) * size)
        theirs_ref[:, at] = dot(x, weight[at, :], NT).astype(BF16)
    later.wait()


def down_own_kernel(tokens_ref, weight_ref, mine_ref):
    mine_ref[...] = dot(tokens_ref[...], weight_ref[...], NT)


def load_kernel(after_ref, hbm_ref, here_ref, sem):
    copy = pltpu.make_async_copy(hbm_ref, here_ref, sem)
    copy.start()
    copy.wait()


def group_at(group, experts_all):
    side_by_side = LANES // (2 * experts_all)
    return group // side_by_side, group % side_by_side * 2 * experts_all


def terms_kernel(
    experts_all, after_ref, routes_hbm, scale_hbm, up_hbm, terms_ref, up_ref, routes, scale, sems
):
    pairs = [(routes_hbm, routes), (scale_hbm, scale), (up_hbm, up_ref)]
    copies = [pltpu.make_async_copy(a, b, sems.at[i]) for i, (a, b) in enumerate(pairs)]
    for copy in copies:
        copy.start()
    copies[0].wait()
    copies[1].wait()
    rows = routes.shape[1]
    row = lax.broadcasted_iota(jnp.int32, (LANES, rows), 0)
    expert = jnp.where(row < experts_all, row, row - experts_all)
    combine = jnp.zeros((LANES, rows), F32)
    for r in range(routes.shape[0]):
        combine += jnp.where(expert == routes[r : r + 1, :], scale[r : r + 1, :], 0.0)
    combine = jnp.where(row < 2 * experts_all, combine, 0.0)
    high = combine.astype(BF16).astype(F32)
    combine = jnp.where(row < experts_all, high, combine - high)
    combine = jnp.concatenate([combine, jnp.zeros((LANES, LANES - rows), F32)], axis=1)
    turned = combine.T
    packed = [jnp.zeros((TILE, LANES), F32)] * (terms_ref.shape[0] // TILE)
    for g in range(rows // TILE):
        tile, at = group_at(g, experts_all)
        part = turned[g * TILE : (g + 1) * TILE, :]
        packed[tile] += pltpu.roll(part, at, 1) if at else part
    for tile, part in enumerate(packed):
        terms_ref[tile * TILE : (tile + 1) * TILE, :] = part.astype(BF16)
    copies[2].wait()


def fold_kernel(latent_ref, terms_ref, message_ref):
    rows, half = latent_ref.shape
    for c in range(half // LANES):
        columns = latent_ref[:, c * LANES : (c + 1) * LANES]
        message_ref[c * rows : (c + 1) * rows, :] = columns.astype(BF16)
    message_ref[half // LANES * rows :, :] = terms_ref[...]


def unfold_kernel(*refs):
    *messages, latent_ref, terms_ref = refs
    rows = latent_ref.shape[0] // len(messages)
    tiles = terms_ref.shape[0] // len(messages)
    parts = latent_ref.shape[1] // LANES
    for b, message in enumerate(messages):
        for c in range(parts):
            columns = message[c * rows : (c + 1) * rows, :]
            latent_ref[b * rows : (b + 1) * rows, c * LANES : (c + 1) * LANES] = columns
        terms_ref[b * tiles : (b + 1) * tiles, :] = message[parts * rows :, :]


def first_kernel(own_ref, up_ref, pre_ref):
    local_count, units, latent_len = up_ref.shape
    half = latent_len // 2
    rows = own_ref[...]
    for k in range(local_count):
        weight = up_ref[k, :, pl.ds(half_at(True, half), half)]
        pre_ref[:, k * units : (k + 1) * units] = dot(rows, weight, NT)


def second_kernel(terms_ref, other_ref, pre_ref, up_ref, down_ref, hidden_ref, theirs_ref):
    local_count, units, latent_len = up_ref.shape
    half = latent_len // 2
    blocks = lax.axis_size("exp")
    experts_all = local_count * blocks
    groups = other_ref.shape[0] // blocks // TILE
    tiles = terms_ref.shape[0] // blocks // TILE
    first = lax.axis_index("exp") * local_count
    lane = lax.broadcasted_iota(jnp.int32, (TILE, LANES), 1)
    rows = other_ref[...]
    for k in range(local_count):
        weight = []
        for b in range(blocks):
            for g in range(groups):
                tile, at = group_at(g, experts_all)
                tile = (b * tiles + tile) * TILE
                terms = terms_ref[tile : tile + TILE, :].astype(F32)
                named = (lane == at + first + k) | (lane == at + first + k + experts_all)
                weight.append(jnp.sum(jnp.where(named, terms, 0.0), axis=1, keepdims=True))
        weight = jnp.concatenate(weight, axis=0)
        at = slice(k * units, (k + 1) * units)
        pre_act = pre_ref[:, at] + dot(rows, up_ref[k, :, pl.ds(half_at(False, half), half)], NT)
        active = jnp.maximum(pre_act, 0.0)
        hidden_ref[:, at] = (active * active * weight).astype(BF16)
    theirs = dot(hidden_ref[...], down_ref[:, pl.ds(half_at(False, half), half)], NN)
    theirs_ref[...] = theirs.astype(BF16)


def third_kernel(hidden_ref, down_ref, mine_ref):
    half = mine_ref.shape[1]
    mine_ref[...] = dot(hidden_ref[...], down_ref[:, pl.ds(half_at(True, half), half)], NN)


def up_own_kernel(own_ref, weight_ref, out_ref):
    half = own_ref.shape[1]
    out_ref[...] = dot(own_ref[...], weight_ref[pl.ds(half_at(True, half), half), :], NN)


def up_kernel(part_ref, other_ref, weight_ref, out_hbm, out, sems):
    other = other_ref[...]
    at_rows = pl.ds(half_at(False, other.shape[1]), other.shape[1])
    half = out.shape[1] // 2
    copies = []
    for i in range(2):
        at = slice(i * half, (i + 1) * half)
        out[:, at] = (part_ref[:, at] + dot(other, weight_ref[at_rows, at], NN)).astype(BF16)
        copies.append(pltpu.make_async_copy(out.at[:, at], out_hbm.at[:, at], sems.at[i]))
        copies[i].start()
    for copy in copies:
        copy.wait()


def on_device(tokens, lat_down, lat_up, expert_up, expert_down, routes, route_weights):
    exp_count, tp_count = lax.axis_size("exp"), lax.axis_size("tp")
    local_count, units, latent_len = expert_up.shape
    rows, width = tokens.shape
    half = latent_len // 2
    all_rows = exp_count * rows
    all_units = local_count * units
    out_len = lat_up.shape[1]
    experts_all = local_count * exp_count
    parts = half // LANES
    terms_rows = -(-rows // TILE // (LANES // (2 * experts_all))) * TILE
    pair_masks = [(1 << b) + 1 for b in range(1, tp_count.bit_length() - 1)]

    def over_tp(x, mask):
        return lax.ppermute(x, "tp", [(t, t ^ mask) for t in range(tp_count)])

    def over_exp(x, mask):
        turn = mask.bit_count() % 2
        places = [(e, t) for e in range(exp_count) for t in range(tp_count)]
        hops = [(e * tp_count + t, (e ^ mask) * tp_count + (t ^ turn)) for e, t in places]
        return lax.ppermute(x, ("exp", "tp"), hops)

    def across(x):
        for mask in pair_masks:
            x = x + over_tp(x.astype(BF16), mask).astype(F32)
        return x

    theirs, tokens_here, weight_here = kernel_call(
        down_kernel,
        (
            shaped(BF16, rows, half),
            pltpu.VMEM((rows, width), BF16),
            pltpu.VMEM((half, width), BF16),
        ),
        (hbm(tokens), hbm(lat_down)),
        (0, 1),
        [pltpu.VMEM((half, width), BF16), pltpu.SemaphoreType.DMA((CHUNKS + 2,))],
        2 * rows * width * half,
        4 * width * half,
    )
    mine = kernel_call(
        down_own_kernel,
        shaped(F32, rows, half),
        (vmem(tokens_here), vmem(weight_here)),
        (),
        [],
        2 * rows * width * half,
        2 * width * half,
    )
    mine = mine + over_tp(theirs, 1).astype(F32)
    terms, up_here = kernel_call(
        lambda *refs: terms_kernel(experts_all, *refs),
        (shaped(BF16, terms_rows, LANES), pltpu.VMEM(expert_up.shape, BF16)),
        (mine.astype(BF16), *(hbm(x) for x in (routes.T, route_weights.T, expert_up))),
        (1, 2, 3),
        [
            pltpu.VMEM(routes.shape[::-1], jnp.int32),
            pltpu.VMEM(routes.shape[::-1], F32),
            pltpu.SemaphoreType.DMA((3,)),
        ],
        0,
        2 * latent_len * all_units,
    )
    up_here = vmem(up_here)
    message = kernel_call(
        fold_kernel,
        shaped(BF16, parts * rows + terms_rows, LANES),
        (across(mine), terms),
        (),
        [],
        0,
        6 * rows * half,
    )
    down_rows = expert_down.reshape(all_units, latent_len)
    down_here = kernel_call(
        load_kernel,
        pltpu.VMEM(down_rows.shape, BF16),
        (message, hbm(down_rows)),
        (1,),
        [pltpu.SemaphoreType.DMA],
        0,
        2 * latent_len * all_units,
    )
    messages = [message] + [over_exp(message, s) for s in range(1, exp_count)]
    messages[-1], down_here = lax.optimization_barrier((messages[-1], down_here))
    down_here = vmem(down_here)
    latent, terms = kernel_call(
        unfold_kernel,
        (shaped(BF16, all_rows, half), shaped(BF16, exp_count * terms_rows, LANES)),
        messages,
        (),
        [],
        0,
        4 * all_rows * half,
    )
    other = over_tp(latent, 1)
    pre = kernel_call(
        first_kernel,
        shaped(F32, all_rows, all_units),
        (latent, up_here),
        (),
        [],
        all_rows * latent_len * all_units,
        latent_len * all_units,
    )
    hidden, theirs = kernel_call(
        second_kernel,
        (shaped(BF16, all_rows, all_units), shaped(BF16, all_rows, half)),
        (terms, other, pre, up_here, down_here),
        (),
        [],
        2 * all_rows * latent_len * all_units,
        2 * latent_len * all_units,
    )
    mine = kernel_call(
        third_kernel,
        shaped(F32, all_rows, half),
        (hidden, down_here),
        (),
        [],
        all_rows * latent_len * all_units,
        latent_len * all_units,
    )
    part = (mine + over_tp(theirs, 1).astype(F32)).astype(BF16)
    blocks = part.reshape(exp_count, rows, half)
    mixed = blocks[0].astype(F32)
    for s in (exp_count - 1, *range(1, exp_count - 1)):
        mixed = mixed + over_exp(blocks[s], s).astype(F32)
    mixed = across(mixed).astype(BF16)
    lat_up = vmem(lat_up)
    own_part = kernel_call(
        up_own_kernel,
        shaped(F32, rows, out_len),
        (mixed, lat_up),
        (),
        [],
        rows * latent_len * out_len,
        latent_len * out_len,
    )
    return kernel_call(
        up_kernel,
        shaped(BF16, rows, out_len),
        (own_part, over_tp(mixed, 1), lat_up),
        (),
        [pltpu.VMEM((rows, out_len), BF16), pltpu.SemaphoreType.DMA((2,))],
        rows * latent_len * out_len,
        latent_len * out_len,
        pltpu.HBM,
    )


def solution(mesh):
    return jax.shard_map(
        on_device,
        mesh=mesh,
        in_specs=(
            P(("grp", "exp"), "tp"),
            P(None, "tp"),
            P(None, "tp"),
            P("exp", "tp", None),
            P("exp", "tp", None),
            P(("grp", "exp"), None),
            P(("grp", "exp"), None),
        ),
        out_specs=P(("grp", "exp"), "tp"),
        check_vma=False,
    )
```

```python
import jax
import jax.numpy as jnp
from jax import lax
from jax.experimental import pallas as pl
from jax.experimental.pallas import tpu as pltpu
from jax.sharding import PartitionSpec as P

BF16, F32 = jnp.bfloat16, jnp.float32
NT = (((1,), (1,)), ((), ()))
NN = (((1,), (0,)), ((), ()))
VMEM_LIMIT = 24 << 20
LANES = 128
CHUNKS = 1
TILE = 16


def hbm(x):
    return pltpu.with_memory_space_constraint(x, pltpu.HBM)


def vmem(x):
    return pltpu.with_memory_space_constraint(x, pltpu.VMEM)


def shaped(dtype, *shape):
    return jax.ShapeDtypeStruct(shape, dtype)


def kernel_call(body, out_shape, args, in_hbm, scratch, flops, moved, out_space=pltpu.VMEM):
    def spec(space):
        return pl.BlockSpec(memory_space=space)

    return pl.pallas_call(
        body,
        out_shape=out_shape,
        in_specs=[spec(pltpu.HBM if i in in_hbm else pltpu.VMEM) for i in range(len(args))],
        out_specs=jax.tree.map(lambda _: spec(out_space), out_shape),
        scratch_shapes=scratch,
        compiler_params=pltpu.CompilerParams(vmem_limit_bytes=VMEM_LIMIT),
        cost_estimate=pl.CostEstimate(flops=flops, bytes_accessed=moved, transcendentals=0),
    )(*args)


def dot(a, b, dims):
    return lax.dot_general(a, b, dims, preferred_element_type=F32)


def half_at(own, half):
    bits = 0
    for axis in ("exp", "tp"):
        for b in range(lax.axis_size(axis).bit_length() - 1):
            bits = bits + lax.axis_index(axis) // (1 << b)
    odd = bits % 2
    return pl.multiple_of((odd if own else 1 - odd) * half, half)


def down_kernel(tokens_hbm, weight_hbm, theirs_ref, tokens, mine_weight, weight, sems):
    half = theirs_ref.shape[1]
    size = half // CHUNKS
    load = pltpu.make_async_copy(tokens_hbm, tokens, sems.at[0])
    load.start()
    chunks = []
    for i in range(CHUNKS):
        start = pl.multiple_of(half_at(False, half) + i * size, size)
        chunks.append(
            pltpu.make_async_copy(
                weight_hbm.at[pl.ds(start, size), :],
                weight.at[pl.ds(i * size, size), :],
                sems.at[2 + i],
            )
        )
        chunks[i].start()
    later = pltpu.make_async_copy(
        weight_hbm.at[pl.ds(half_at(True, half), half), :], mine_weight, sems.at[1]
    )
    later.start()
    load.wait()
    x = tokens[...]
    for i in range(CHUNKS):
        chunks[i].wait()
        at = slice(i * size, (i + 1) * size)
        theirs_ref[:, at] = dot(x, weight[at, :], NT).astype(BF16)
    later.wait()


def down_own_kernel(tokens_ref, weight_ref, mine_ref):
    mine_ref[...] = dot(tokens_ref[...], weight_ref[...], NT)


def load_kernel(after_ref, hbm_ref, here_ref, sem):
    copy = pltpu.make_async_copy(hbm_ref, here_ref, sem)
    copy.start()
    copy.wait()


def group_at(group, experts_all):
    side_by_side = LANES // (2 * experts_all)
    return group // side_by_side, group % side_by_side * 2 * experts_all


def terms_kernel(
    experts_all, after_ref, routes_hbm, scale_hbm, up_hbm, terms_ref, up_ref, routes, scale, sems
):
    pairs = [(routes_hbm, routes), (scale_hbm, scale), (up_hbm, up_ref)]
    copies = [pltpu.make_async_copy(a, b, sems.at[i]) for i, (a, b) in enumerate(pairs)]
    for copy in copies:
        copy.start()
    copies[0].wait()
    copies[1].wait()
    rows = routes.shape[1]
    row = lax.broadcasted_iota(jnp.int32, (LANES, rows), 0)
    expert = jnp.where(row < experts_all, row, row - experts_all)
    combine = jnp.zeros((LANES, rows), F32)
    for r in range(routes.shape[0]):
        combine += jnp.where(expert == routes[r : r + 1, :], scale[r : r + 1, :], 0.0)
    combine = jnp.where(row < 2 * experts_all, combine, 0.0)
    high = combine.astype(BF16).astype(F32)
    combine = jnp.where(row < experts_all, high, combine - high)
    combine = jnp.concatenate([combine, jnp.zeros((LANES, LANES - rows), F32)], axis=1)
    turned = combine.T
    packed = [jnp.zeros((TILE, LANES), F32)] * (terms_ref.shape[0] // TILE)
    for g in range(rows // TILE):
        tile, at = group_at(g, experts_all)
        part = turned[g * TILE : (g + 1) * TILE, :]
        packed[tile] += pltpu.roll(part, at, 1) if at else part
    for tile, part in enumerate(packed):
        terms_ref[tile * TILE : (tile + 1) * TILE, :] = part.astype(BF16)
    copies[2].wait()


def fold_kernel(latent_ref, terms_ref, message_ref):
    rows, half = latent_ref.shape
    for c in range(half // LANES):
        columns = latent_ref[:, c * LANES : (c + 1) * LANES]
        message_ref[c * rows : (c + 1) * rows, :] = columns.astype(BF16)
    message_ref[half // LANES * rows :, :] = terms_ref[...]


def unfold_kernel(spots, *refs):
    *messages, latent_ref, terms_ref = refs
    rows = latent_ref.shape[0] // len(messages)
    tiles = terms_ref.shape[0] // len(messages)
    parts = latent_ref.shape[1] // LANES
    for s, message in enumerate(messages):
        b = spots.index(s)
        for c in range(parts):
            columns = message[c * rows : (c + 1) * rows, :]
            latent_ref[b * rows : (b + 1) * rows, c * LANES : (c + 1) * LANES] = columns
        terms_ref[b * tiles : (b + 1) * tiles, :] = message[parts * rows :, :]


def first_kernel(own_ref, up_ref, pre_ref):
    local_count, units, latent_len = up_ref.shape
    half = latent_len // 2
    rows = own_ref[...]
    for k in range(local_count):
        weight = up_ref[k, :, pl.ds(half_at(True, half), half)]
        pre_ref[:, k * units : (k + 1) * units] = dot(rows, weight, NT)


def second_kernel(late, terms_ref, other_ref, pre_ref, up_ref, down_ref, hidden_ref, theirs_ref):
    local_count, units, latent_len = up_ref.shape
    half = latent_len // 2
    blocks = lax.axis_size("exp")
    experts_all = local_count * blocks
    groups = other_ref.shape[0] // blocks // TILE
    tiles = terms_ref.shape[0] // blocks // TILE
    first = lax.axis_index("exp") * local_count
    lane = lax.broadcasted_iota(jnp.int32, (TILE, LANES), 1)
    side = other_ref.shape[0] // 2
    mine = slice(side, 2 * side) if late else slice(0, side)
    rows = other_ref[mine, :]
    for k in range(local_count):
        weight = []
        for b in range(blocks // 2):
            for g in range(groups):
                tile, at = group_at(g, experts_all)
                tile = ((b + late * (blocks // 2)) * tiles + tile) * TILE
                terms = terms_ref[tile : tile + TILE, :].astype(F32)
                named = (lane == at + first + k) | (lane == at + first + k + experts_all)
                weight.append(jnp.sum(jnp.where(named, terms, 0.0), axis=1, keepdims=True))
        weight = jnp.concatenate(weight, axis=0)
        at = slice(k * units, (k + 1) * units)
        product = dot(rows, up_ref[k, :, pl.ds(half_at(False, half), half)], NT)
        active = jnp.maximum(pre_ref[mine, at] + product, 0.0)
        hidden_ref[:, at] = (active * active * weight).astype(BF16)
    theirs = dot(hidden_ref[...], down_ref[:, pl.ds(half_at(False, half), half)], NN)
    theirs_ref[...] = theirs.astype(BF16)


def third_kernel(late_ref, early_ref, down_ref, late_out_ref, early_out_ref):
    half = early_out_ref.shape[1]
    side = early_out_ref.shape[0]
    rows = jnp.concatenate([early_ref[...], late_ref[...]], axis=0)
    result = dot(rows, down_ref[:, pl.ds(half_at(True, half), half)], NN)
    early_out_ref[...] = result[:side, :]
    late_out_ref[...] = result[side:, :]


def up_own_kernel(own_ref, weight_ref, out_ref):
    half = own_ref.shape[1]
    out_ref[...] = dot(own_ref[...], weight_ref[pl.ds(half_at(True, half), half), :], NN)


def up_kernel(part_ref, other_ref, weight_ref, out_hbm, out, sems):
    other = other_ref[...]
    at_rows = pl.ds(half_at(False, other.shape[1]), other.shape[1])
    half = out.shape[1] // 2
    copies = []
    for i in range(2):
        at = slice(i * half, (i + 1) * half)
        out[:, at] = (part_ref[:, at] + dot(other, weight_ref[at_rows, at], NN)).astype(BF16)
        copies.append(pltpu.make_async_copy(out.at[:, at], out_hbm.at[:, at], sems.at[i]))
        copies[i].start()
    for copy in copies:
        copy.wait()


def on_device(tokens, lat_down, lat_up, expert_up, expert_down, routes, route_weights):
    exp_count, tp_count = lax.axis_size("exp"), lax.axis_size("tp")
    local_count, units, latent_len = expert_up.shape
    rows, width = tokens.shape
    half = latent_len // 2
    all_rows = exp_count * rows
    all_units = local_count * units
    out_len = lat_up.shape[1]
    experts_all = local_count * exp_count
    parts = half // LANES
    spots = (0, exp_count - 1, *range(1, exp_count - 1))
    terms_rows = -(-rows // TILE // (LANES // (2 * experts_all))) * TILE
    pair_masks = [(1 << b) + 1 for b in range(1, tp_count.bit_length() - 1)]

    def over_tp(x, mask):
        return lax.ppermute(x, "tp", [(t, t ^ mask) for t in range(tp_count)])

    def over_exp(x, mask):
        turn = mask.bit_count() % 2
        places = [(e, t) for e in range(exp_count) for t in range(tp_count)]
        hops = [(e * tp_count + t, (e ^ mask) * tp_count + (t ^ turn)) for e, t in places]
        return lax.ppermute(x, ("exp", "tp"), hops)

    def across(x):
        for mask in pair_masks:
            x = x + over_tp(x.astype(BF16), mask).astype(F32)
        return x

    theirs, tokens_here, weight_here = kernel_call(
        down_kernel,
        (
            shaped(BF16, rows, half),
            pltpu.VMEM((rows, width), BF16),
            pltpu.VMEM((half, width), BF16),
        ),
        (hbm(tokens), hbm(lat_down)),
        (0, 1),
        [pltpu.VMEM((half, width), BF16), pltpu.SemaphoreType.DMA((CHUNKS + 2,))],
        2 * rows * width * half,
        4 * width * half,
    )
    mine = kernel_call(
        down_own_kernel,
        shaped(F32, rows, half),
        (vmem(tokens_here), vmem(weight_here)),
        (),
        [],
        2 * rows * width * half,
        2 * width * half,
    )
    mine = mine + over_tp(theirs, 1).astype(F32)
    terms, up_here = kernel_call(
        lambda *refs: terms_kernel(experts_all, *refs),
        (shaped(BF16, terms_rows, LANES), pltpu.VMEM(expert_up.shape, BF16)),
        (mine.astype(BF16), *(hbm(x) for x in (routes.T, route_weights.T, expert_up))),
        (1, 2, 3),
        [
            pltpu.VMEM(routes.shape[::-1], jnp.int32),
            pltpu.VMEM(routes.shape[::-1], F32),
            pltpu.SemaphoreType.DMA((3,)),
        ],
        0,
        2 * latent_len * all_units,
    )
    up_here = vmem(up_here)
    message = kernel_call(
        fold_kernel,
        shaped(BF16, parts * rows + terms_rows, LANES),
        (across(mine), terms),
        (),
        [],
        0,
        6 * rows * half,
    )
    down_rows = expert_down.reshape(all_units, latent_len)
    down_here = kernel_call(
        load_kernel,
        pltpu.VMEM(down_rows.shape, BF16),
        (message, hbm(down_rows)),
        (1,),
        [pltpu.SemaphoreType.DMA],
        0,
        2 * latent_len * all_units,
    )
    messages = [message] + [over_exp(message, s) for s in range(1, exp_count)]
    messages[-1], down_here = lax.optimization_barrier((messages[-1], down_here))
    down_here = vmem(down_here)
    latent, terms = kernel_call(
        lambda *refs: unfold_kernel(spots, *refs),
        (shaped(BF16, all_rows, half), shaped(BF16, exp_count * terms_rows, LANES)),
        messages,
        (),
        [],
        0,
        4 * all_rows * half,
    )
    other = over_tp(latent, 1)
    pre = kernel_call(
        first_kernel,
        shaped(F32, all_rows, all_units),
        (latent, up_here),
        (),
        [],
        all_rows * latent_len * all_units,
        latent_len * all_units,
    )
    side_rows = all_rows // 2

    def experts(late):
        return kernel_call(
            lambda *refs: second_kernel(late, *refs),
            (shaped(BF16, side_rows, all_units), shaped(BF16, side_rows, half)),
            (terms, other, pre, up_here, down_here),
            (),
            [],
            2 * side_rows * latent_len * all_units,
            2 * latent_len * all_units,
        )

    early_hidden, early_theirs = experts(False)
    late_hidden, late_theirs = experts(True)
    late_mine, early_mine = kernel_call(
        third_kernel,
        (shaped(F32, side_rows, half), shaped(F32, side_rows, half)),
        (late_hidden, early_hidden, down_here),
        (),
        [],
        all_rows * latent_len * all_units,
        latent_len * all_units,
    )
    early_part = (early_mine + over_tp(early_theirs, 1).astype(F32)).astype(BF16)
    late_part = (late_mine + over_tp(late_theirs, 1).astype(F32)).astype(BF16)
    blocks = (
        *early_part.reshape(exp_count // 2, rows, half),
        *late_part.reshape(exp_count // 2, rows, half),
    )
    mixed = blocks[0].astype(F32)
    for s in range(exp_count - 1, 0, -1):
        mixed = mixed + over_exp(blocks[spots.index(s)], s).astype(F32)
    mixed = across(mixed).astype(BF16)
    lat_up = vmem(lat_up)
    own_part = kernel_call(
        up_own_kernel,
        shaped(F32, rows, out_len),
        (mixed, lat_up),
        (),
        [],
        rows * latent_len * out_len,
        latent_len * out_len,
    )
    return kernel_call(
        up_kernel,
        shaped(BF16, rows, out_len),
        (own_part, over_tp(mixed, 1), lat_up),
        (),
        [pltpu.VMEM((rows, out_len), BF16), pltpu.SemaphoreType.DMA((2,))],
        rows * latent_len * out_len,
        latent_len * out_len,
        pltpu.HBM,
    )


def solution(mesh):
    return jax.shard_map(
        on_device,
        mesh=mesh,
        in_specs=(
            P(("grp", "exp"), "tp"),
            P(None, "tp"),
            P(None, "tp"),
            P("exp", "tp", None),
            P("exp", "tp", None),
            P(("grp", "exp"), None),
            P(("grp", "exp"), None),
        ),
        out_specs=P(("grp", "exp"), "tp"),
        check_vma=False,
    )
```

```python
import jax
import jax.numpy as jnp
from jax import lax
from jax.experimental import pallas as pl
from jax.experimental.pallas import tpu as pltpu
from jax.sharding import PartitionSpec as P

BF16, F32 = jnp.bfloat16, jnp.float32
NT = (((1,), (1,)), ((), ()))
NN = (((1,), (0,)), ((), ()))
VMEM_LIMIT = 24 << 20
LANES = 128
CHUNKS = 1
TILE = 16


def hbm(x):
    return pltpu.with_memory_space_constraint(x, pltpu.HBM)


def vmem(x):
    return pltpu.with_memory_space_constraint(x, pltpu.VMEM)


def shaped(dtype, *shape):
    return jax.ShapeDtypeStruct(shape, dtype)


def kernel_call(body, out_shape, args, in_hbm, scratch, flops, moved, out_space=pltpu.VMEM):
    def spec(space):
        return pl.BlockSpec(memory_space=space)

    return pl.pallas_call(
        body,
        out_shape=out_shape,
        in_specs=[spec(pltpu.HBM if i in in_hbm else pltpu.VMEM) for i in range(len(args))],
        out_specs=jax.tree.map(lambda _: spec(out_space), out_shape),
        scratch_shapes=scratch,
        compiler_params=pltpu.CompilerParams(vmem_limit_bytes=VMEM_LIMIT),
        cost_estimate=pl.CostEstimate(flops=flops, bytes_accessed=moved, transcendentals=0),
    )(*args)


def dot(a, b, dims):
    return lax.dot_general(a, b, dims, preferred_element_type=F32)


def half_at(own, half):
    bits = lax.axis_index("exp")
    for b in range(lax.axis_size("tp").bit_length() - 1):
        bits = bits + lax.axis_index("tp") // (1 << b)
    odd = bits % 2
    return pl.multiple_of((odd if own else 1 - odd) * half, half)


def down_kernel(tokens_hbm, weight_hbm, theirs_ref, tokens, mine_weight, weight, sems):
    half = theirs_ref.shape[1]
    size = half // CHUNKS
    load = pltpu.make_async_copy(tokens_hbm, tokens, sems.at[0])
    load.start()
    chunks = []
    for i in range(CHUNKS):
        start = pl.multiple_of(half_at(False, half) + i * size, size)
        chunks.append(
            pltpu.make_async_copy(
                weight_hbm.at[pl.ds(start, size), :],
                weight.at[pl.ds(i * size, size), :],
                sems.at[2 + i],
            )
        )
        chunks[i].start()
    later = pltpu.make_async_copy(
        weight_hbm.at[pl.ds(half_at(True, half), half), :], mine_weight, sems.at[1]
    )
    later.start()
    load.wait()
    x = tokens[...]
    for i in range(CHUNKS):
        chunks[i].wait()
        at = slice(i * size, (i + 1) * size)
        theirs_ref[:, at] = dot(x, weight[at, :], NT).astype(BF16)
    later.wait()


def down_own_kernel(tokens_ref, weight_ref, mine_ref):
    mine_ref[...] = dot(tokens_ref[...], weight_ref[...], NT)


def load_kernel(after_ref, hbm_ref, here_ref, sem):
    copy = pltpu.make_async_copy(hbm_ref, here_ref, sem)
    copy.start()
    copy.wait()


def group_at(group, experts_all):
    side_by_side = LANES // (2 * experts_all)
    return group // side_by_side, group % side_by_side * 2 * experts_all


def terms_kernel(
    experts_all, after_ref, routes_hbm, scale_hbm, up_hbm, terms_ref, up_ref, routes, scale, sems
):
    pairs = [(routes_hbm, routes), (scale_hbm, scale), (up_hbm, up_ref)]
    copies = [pltpu.make_async_copy(a, b, sems.at[i]) for i, (a, b) in enumerate(pairs)]
    for copy in copies:
        copy.start()
    copies[0].wait()
    copies[1].wait()
    rows = routes.shape[1]
    row = lax.broadcasted_iota(jnp.int32, (LANES, rows), 0)
    expert = jnp.where(row < experts_all, row, row - experts_all)
    combine = jnp.zeros((LANES, rows), F32)
    for r in range(routes.shape[0]):
        combine += jnp.where(expert == routes[r : r + 1, :], scale[r : r + 1, :], 0.0)
    combine = jnp.where(row < 2 * experts_all, combine, 0.0)
    high = combine.astype(BF16).astype(F32)
    combine = jnp.where(row < experts_all, high, combine - high)
    combine = jnp.concatenate([combine, jnp.zeros((LANES, LANES - rows), F32)], axis=1)
    turned = combine.T
    packed = [jnp.zeros((TILE, LANES), F32)] * (terms_ref.shape[0] // TILE)
    for g in range(rows // TILE):
        tile, at = group_at(g, experts_all)
        part = turned[g * TILE : (g + 1) * TILE, :]
        packed[tile] += pltpu.roll(part, at, 1) if at else part
    for tile, part in enumerate(packed):
        terms_ref[tile * TILE : (tile + 1) * TILE, :] = part.astype(BF16)
    copies[2].wait()


def fold_kernel(latent_ref, terms_ref, message_ref):
    rows, half = latent_ref.shape
    for c in range(half // LANES):
        columns = latent_ref[:, c * LANES : (c + 1) * LANES]
        message_ref[c * rows : (c + 1) * rows, :] = columns.astype(BF16)
    message_ref[half // LANES * rows :, :] = terms_ref[...]


def unfold_kernel(*refs):
    *messages, latent_ref, terms_ref = refs
    rows = latent_ref.shape[0] // len(messages)
    tiles = terms_ref.shape[0] // len(messages)
    parts = latent_ref.shape[1] // LANES
    for b, message in enumerate(messages):
        for c in range(parts):
            columns = message[c * rows : (c + 1) * rows, :]
            latent_ref[b * rows : (b + 1) * rows, c * LANES : (c + 1) * LANES] = columns
        terms_ref[b * tiles : (b + 1) * tiles, :] = message[parts * rows :, :]


def first_kernel(own_ref, up_ref, pre_ref):
    local_count, units, latent_len = up_ref.shape
    half = latent_len // 2
    rows = own_ref[...]
    for k in range(local_count):
        weight = up_ref[k, :, pl.ds(half_at(True, half), half)]
        pre_ref[:, k * units : (k + 1) * units] = dot(rows, weight, NT)


def second_kernel(terms_ref, other_ref, pre_ref, up_ref, down_ref, hidden_ref, theirs_ref):
    local_count, units, latent_len = up_ref.shape
    half = latent_len // 2
    blocks = lax.axis_size("exp")
    experts_all = local_count * blocks
    groups = other_ref.shape[0] // blocks // TILE
    tiles = terms_ref.shape[0] // blocks // TILE
    first = lax.axis_index("exp") * local_count
    lane = lax.broadcasted_iota(jnp.int32, (TILE, LANES), 1)
    rows = other_ref[...]
    for k in range(local_count):
        weight = []
        for b in range(blocks):
            for g in range(groups):
                tile, at = group_at(g, experts_all)
                tile = (b * tiles + tile) * TILE
                terms = terms_ref[tile : tile + TILE, :].astype(F32)
                named = (lane == at + first + k) | (lane == at + first + k + experts_all)
                weight.append(jnp.sum(jnp.where(named, terms, 0.0), axis=1, keepdims=True))
        weight = jnp.concatenate(weight, axis=0)
        at = slice(k * units, (k + 1) * units)
        pre_act = pre_ref[:, at] + dot(rows, up_ref[k, :, pl.ds(half_at(False, half), half)], NT)
        active = jnp.maximum(pre_act, 0.0)
        hidden_ref[:, at] = (active * active * weight).astype(BF16)
    theirs = dot(hidden_ref[...], down_ref[:, pl.ds(half_at(False, half), half)], NN)
    theirs_ref[...] = theirs.astype(BF16)


def third_kernel(hidden_ref, down_ref, mine_ref):
    half = mine_ref.shape[1]
    mine_ref[...] = dot(hidden_ref[...], down_ref[:, pl.ds(half_at(True, half), half)], NN)


def up_own_kernel(own_ref, weight_ref, out_ref):
    half = own_ref.shape[1]
    out_ref[...] = dot(own_ref[...], weight_ref[pl.ds(half_at(True, half), half), :], NN)


def up_kernel(part_ref, other_ref, weight_ref, out_hbm, out, sems):
    other = other_ref[...]
    at_rows = pl.ds(half_at(False, other.shape[1]), other.shape[1])
    half = out.shape[1] // 2
    copies = []
    for i in range(2):
        at = slice(i * half, (i + 1) * half)
        out[:, at] = (part_ref[:, at] + dot(other, weight_ref[at_rows, at], NN)).astype(BF16)
        copies.append(pltpu.make_async_copy(out.at[:, at], out_hbm.at[:, at], sems.at[i]))
        copies[i].start()
    for copy in copies:
        copy.wait()


def on_device(tokens, lat_down, lat_up, expert_up, expert_down, routes, route_weights):
    exp_count, tp_count = lax.axis_size("exp"), lax.axis_size("tp")
    local_count, units, latent_len = expert_up.shape
    rows, width = tokens.shape
    half = latent_len // 2
    all_rows = exp_count * rows
    all_units = local_count * units
    out_len = lat_up.shape[1]
    experts_all = local_count * exp_count
    parts = half // LANES
    terms_rows = -(-rows // TILE // (LANES // (2 * experts_all))) * TILE
    pair_masks = [(1 << b) + 1 for b in range(1, tp_count.bit_length() - 1)]

    def over_tp(x, mask):
        return lax.ppermute(x, "tp", [(t, t ^ mask) for t in range(tp_count)])

    def over_exp(x, mask):
        turn = mask % 2
        places = [(e, t) for e in range(exp_count) for t in range(tp_count)]
        hops = [(e * tp_count + t, (e ^ mask) * tp_count + (t ^ turn)) for e, t in places]
        return lax.ppermute(x, ("exp", "tp"), hops)

    def across(x):
        for mask in pair_masks:
            x = x + over_tp(x.astype(BF16), mask).astype(F32)
        return x

    theirs, tokens_here, weight_here = kernel_call(
        down_kernel,
        (
            shaped(BF16, rows, half),
            pltpu.VMEM((rows, width), BF16),
            pltpu.VMEM((half, width), BF16),
        ),
        (hbm(tokens), hbm(lat_down)),
        (0, 1),
        [pltpu.VMEM((half, width), BF16), pltpu.SemaphoreType.DMA((CHUNKS + 2,))],
        2 * rows * width * half,
        4 * width * half,
    )
    mine = kernel_call(
        down_own_kernel,
        shaped(F32, rows, half),
        (vmem(tokens_here), vmem(weight_here)),
        (),
        [],
        2 * rows * width * half,
        2 * width * half,
    )
    mine = mine + over_tp(theirs, 1).astype(F32)
    terms, up_here = kernel_call(
        lambda *refs: terms_kernel(experts_all, *refs),
        (shaped(BF16, terms_rows, LANES), pltpu.VMEM(expert_up.shape, BF16)),
        (mine.astype(BF16), *(hbm(x) for x in (routes.T, route_weights.T, expert_up))),
        (1, 2, 3),
        [
            pltpu.VMEM(routes.shape[::-1], jnp.int32),
            pltpu.VMEM(routes.shape[::-1], F32),
            pltpu.SemaphoreType.DMA((3,)),
        ],
        0,
        2 * latent_len * all_units,
    )
    up_here = vmem(up_here)
    message = kernel_call(
        fold_kernel,
        shaped(BF16, parts * rows + terms_rows, LANES),
        (across(mine), terms),
        (),
        [],
        0,
        6 * rows * half,
    )
    down_rows = expert_down.reshape(all_units, latent_len)
    down_here = kernel_call(
        load_kernel,
        pltpu.VMEM(down_rows.shape, BF16),
        (message, hbm(down_rows)),
        (1,),
        [pltpu.SemaphoreType.DMA],
        0,
        2 * latent_len * all_units,
    )
    messages = [message] + [over_exp(message, s) for s in range(1, exp_count)]
    messages[-1], down_here = lax.optimization_barrier((messages[-1], down_here))
    down_here = vmem(down_here)
    latent, terms = kernel_call(
        unfold_kernel,
        (shaped(BF16, all_rows, half), shaped(BF16, exp_count * terms_rows, LANES)),
        messages,
        (),
        [],
        0,
        4 * all_rows * half,
    )
    other = over_tp(latent, 1)
    pre = kernel_call(
        first_kernel,
        shaped(F32, all_rows, all_units),
        (latent, up_here),
        (),
        [],
        all_rows * latent_len * all_units,
        latent_len * all_units,
    )
    hidden, theirs = kernel_call(
        second_kernel,
        (shaped(BF16, all_rows, all_units), shaped(BF16, all_rows, half)),
        (terms, other, pre, up_here, down_here),
        (),
        [],
        2 * all_rows * latent_len * all_units,
        2 * latent_len * all_units,
    )
    mine = kernel_call(
        third_kernel,
        shaped(F32, all_rows, half),
        (hidden, down_here),
        (),
        [],
        all_rows * latent_len * all_units,
        latent_len * all_units,
    )
    part = (mine + over_tp(theirs, 1).astype(F32)).astype(BF16)
    blocks = part.reshape(exp_count, rows, half)
    mixed = blocks[0].astype(F32)
    for s in (exp_count - 1, *range(1, exp_count - 1)):
        mixed = mixed + over_exp(blocks[s], s).astype(F32)
    mixed = across(mixed).astype(BF16)
    lat_up = vmem(lat_up)
    own_part = kernel_call(
        up_own_kernel,
        shaped(F32, rows, out_len),
        (mixed, lat_up),
        (),
        [],
        rows * latent_len * out_len,
        latent_len * out_len,
    )
    return kernel_call(
        up_kernel,
        shaped(BF16, rows, out_len),
        (own_part, over_tp(mixed, 1), lat_up),
        (),
        [pltpu.VMEM((rows, out_len), BF16), pltpu.SemaphoreType.DMA((2,))],
        rows * latent_len * out_len,
        latent_len * out_len,
        pltpu.HBM,
    )


def solution(mesh):
    return jax.shard_map(
        on_device,
        mesh=mesh,
        in_specs=(
            P(("grp", "exp"), "tp"),
            P(None, "tp"),
            P(None, "tp"),
            P("exp", "tp", None),
            P("exp", "tp", None),
            P(("grp", "exp"), None),
            P(("grp", "exp"), None),
        ),
        out_specs=P(("grp", "exp"), "tp"),
        check_vma=False,
    )
```

```python
import jax
import jax.numpy as jnp
from jax import lax
from jax.experimental import pallas as pl
from jax.experimental.pallas import tpu as pltpu
from jax.sharding import PartitionSpec as P

BF16, F32 = jnp.bfloat16, jnp.float32
NT = (((1,), (1,)), ((), ()))
NN = (((1,), (0,)), ((), ()))
VMEM_LIMIT = 24 << 20
LANES = 128
CHUNKS = 1
TILE = 16


def hbm(x):
    return pltpu.with_memory_space_constraint(x, pltpu.HBM)


def vmem(x):
    return pltpu.with_memory_space_constraint(x, pltpu.VMEM)


def shaped(dtype, *shape):
    return jax.ShapeDtypeStruct(shape, dtype)


def kernel_call(body, out_shape, args, in_hbm, scratch, flops, moved, out_space=pltpu.VMEM):
    def spec(space):
        return pl.BlockSpec(memory_space=space)

    return pl.pallas_call(
        body,
        out_shape=out_shape,
        in_specs=[spec(pltpu.HBM if i in in_hbm else pltpu.VMEM) for i in range(len(args))],
        out_specs=jax.tree.map(lambda _: spec(out_space), out_shape),
        scratch_shapes=scratch,
        compiler_params=pltpu.CompilerParams(vmem_limit_bytes=VMEM_LIMIT),
        cost_estimate=pl.CostEstimate(flops=flops, bytes_accessed=moved, transcendentals=0),
    )(*args)


def dot(a, b, dims):
    return lax.dot_general(a, b, dims, preferred_element_type=F32)


def half_at(own, half):
    bits = lax.axis_index("exp")
    for b in range(lax.axis_size("tp").bit_length() - 1):
        bits = bits + lax.axis_index("tp") // (1 << b)
    odd = bits % 2
    return pl.multiple_of((odd if own else 1 - odd) * half, half)


def down_kernel(tokens_hbm, weight_hbm, theirs_ref, tokens, mine_weight, weight, sems):
    half = theirs_ref.shape[1]
    size = half // CHUNKS
    load = pltpu.make_async_copy(tokens_hbm, tokens, sems.at[0])
    load.start()
    chunks = []
    for i in range(CHUNKS):
        start = pl.multiple_of(half_at(False, half) + i * size, size)
        chunks.append(
            pltpu.make_async_copy(
                weight_hbm.at[pl.ds(start, size), :],
                weight.at[pl.ds(i * size, size), :],
                sems.at[2 + i],
            )
        )
        chunks[i].start()
    later = pltpu.make_async_copy(
        weight_hbm.at[pl.ds(half_at(True, half), half), :], mine_weight, sems.at[1]
    )
    later.start()
    load.wait()
    x = tokens[...]
    for i in range(CHUNKS):
        chunks[i].wait()
        at = slice(i * size, (i + 1) * size)
        theirs_ref[:, at] = dot(x, weight[at, :], NT).astype(BF16)
    later.wait()


def down_own_kernel(tokens_ref, weight_ref, mine_ref):
    mine_ref[...] = dot(tokens_ref[...], weight_ref[...], NT)


def load_kernel(after_ref, hbm_ref, here_ref, sem):
    copy = pltpu.make_async_copy(hbm_ref, here_ref, sem)
    copy.start()
    copy.wait()


def group_at(group, experts_all):
    side_by_side = LANES // (2 * experts_all)
    return group // side_by_side, group % side_by_side * 2 * experts_all


def terms_kernel(
    experts_all, after_ref, routes_hbm, scale_hbm, up_hbm, terms_ref, up_ref, routes, scale, sems
):
    pairs = [(routes_hbm, routes), (scale_hbm, scale), (up_hbm, up_ref)]
    copies = [pltpu.make_async_copy(a, b, sems.at[i]) for i, (a, b) in enumerate(pairs)]
    for copy in copies:
        copy.start()
    copies[0].wait()
    copies[1].wait()
    rows = routes.shape[1]
    row = lax.broadcasted_iota(jnp.int32, (LANES, rows), 0)
    expert = jnp.where(row < experts_all, row, row - experts_all)
    combine = jnp.zeros((LANES, rows), F32)
    for r in range(routes.shape[0]):
        combine += jnp.where(expert == routes[r : r + 1, :], scale[r : r + 1, :], 0.0)
    combine = jnp.where(row < 2 * experts_all, combine, 0.0)
    high = combine.astype(BF16).astype(F32)
    combine = jnp.where(row < experts_all, high, combine - high)
    combine = jnp.concatenate([combine, jnp.zeros((LANES, LANES - rows), F32)], axis=1)
    turned = combine.T
    packed = [jnp.zeros((TILE, LANES), F32)] * (terms_ref.shape[0] // TILE)
    for g in range(rows // TILE):
        tile, at = group_at(g, experts_all)
        part = turned[g * TILE : (g + 1) * TILE, :]
        packed[tile] += pltpu.roll(part, at, 1) if at else part
    for tile, part in enumerate(packed):
        terms_ref[tile * TILE : (tile + 1) * TILE, :] = part.astype(BF16)
    copies[2].wait()


def fold_kernel(latent_ref, terms_ref, message_ref):
    rows, half = latent_ref.shape
    for c in range(half // LANES):
        columns = latent_ref[:, c * LANES : (c + 1) * LANES]
        message_ref[c * rows : (c + 1) * rows, :] = columns.astype(BF16)
    message_ref[half // LANES * rows :, :] = terms_ref[...]


def unfold_kernel(*refs):
    *messages, latent_ref, terms_ref = refs
    rows = latent_ref.shape[0] // len(messages)
    tiles = terms_ref.shape[0] // len(messages)
    parts = latent_ref.shape[1] // LANES
    for b, message in enumerate(messages):
        for c in range(parts):
            columns = message[c * rows : (c + 1) * rows, :]
            latent_ref[b * rows : (b + 1) * rows, c * LANES : (c + 1) * LANES] = columns
        terms_ref[b * tiles : (b + 1) * tiles, :] = message[parts * rows :, :]


def first_kernel(own_ref, up_ref, pre_ref):
    local_count, units, latent_len = up_ref.shape
    half = latent_len // 2
    rows = own_ref[...]
    for k in range(local_count):
        weight = up_ref[k, :, pl.ds(half_at(True, half), half)]
        pre_ref[:, k * units : (k + 1) * units] = dot(rows, weight, NT)


def second_kernel(terms_ref, other_ref, pre_ref, up_ref, down_ref, hidden_ref, theirs_ref):
    local_count, units, latent_len = up_ref.shape
    half = latent_len // 2
    blocks = lax.axis_size("exp")
    experts_all = local_count * blocks
    groups = other_ref.shape[0] // blocks // TILE
    tiles = terms_ref.shape[0] // blocks // TILE
    first = lax.axis_index("exp") * local_count
    lane = lax.broadcasted_iota(jnp.int32, (TILE, LANES), 1)
    rows = other_ref[...]
    for k in range(local_count):
        weight = []
        for b in range(blocks):
            for g in range(groups):
                tile, at = group_at(g, experts_all)
                tile = (b * tiles + tile) * TILE
                terms = terms_ref[tile : tile + TILE, :].astype(F32)
                named = (lane == at + first + k) | (lane == at + first + k + experts_all)
                weight.append(jnp.sum(jnp.where(named, terms, 0.0), axis=1, keepdims=True))
        weight = jnp.concatenate(weight, axis=0)
        at = slice(k * units, (k + 1) * units)
        pre_act = pre_ref[:, at] + dot(rows, up_ref[k, :, pl.ds(half_at(False, half), half)], NT)
        active = jnp.maximum(pre_act, 0.0)
        hidden_ref[:, at] = (active * active * weight).astype(BF16)
    theirs = dot(hidden_ref[...], down_ref[:, pl.ds(half_at(False, half), half)], NN)
    theirs_ref[...] = theirs.astype(BF16)


def third_kernel(hidden_ref, down_ref, mine_ref):
    half = mine_ref.shape[1]
    mine_ref[...] = dot(hidden_ref[...], down_ref[:, pl.ds(half_at(True, half), half)], NN)


def up_own_kernel(own_ref, weight_ref, out_ref):
    half = own_ref.shape[1]
    out_ref[...] = dot(own_ref[...], weight_ref[pl.ds(half_at(True, half), half), :], NN)


def up_kernel(part_ref, other_ref, weight_ref, out_hbm, out, sems):
    other = other_ref[...]
    at_rows = pl.ds(half_at(False, other.shape[1]), other.shape[1])
    length = out.shape[1]
    copies = []
    for i, at in enumerate((slice(0, length // 4 * 3), slice(length // 4 * 3, length))):
        out[:, at] = (part_ref[:, at] + dot(other, weight_ref[at_rows, at], NN)).astype(BF16)
        copies.append(pltpu.make_async_copy(out.at[:, at], out_hbm.at[:, at], sems.at[i]))
        copies[i].start()
    for copy in copies:
        copy.wait()


def on_device(tokens, lat_down, lat_up, expert_up, expert_down, routes, route_weights):
    exp_count, tp_count = lax.axis_size("exp"), lax.axis_size("tp")
    local_count, units, latent_len = expert_up.shape
    rows, width = tokens.shape
    half = latent_len // 2
    all_rows = exp_count * rows
    all_units = local_count * units
    out_len = lat_up.shape[1]
    experts_all = local_count * exp_count
    parts = half // LANES
    terms_rows = -(-rows // TILE // (LANES // (2 * experts_all))) * TILE
    pair_masks = [(1 << b) + 1 for b in range(1, tp_count.bit_length() - 1)]

    def over_tp(x, mask):
        return lax.ppermute(x, "tp", [(t, t ^ mask) for t in range(tp_count)])

    def over_exp(x, mask):
        turn = mask % 2
        places = [(e, t) for e in range(exp_count) for t in range(tp_count)]
        hops = [(e * tp_count + t, (e ^ mask) * tp_count + (t ^ turn)) for e, t in places]
        return lax.ppermute(x, ("exp", "tp"), hops)

    def across(x):
        for mask in pair_masks:
            x = x + over_tp(x.astype(BF16), mask).astype(F32)
        return x

    theirs, tokens_here, weight_here = kernel_call(
        down_kernel,
        (
            shaped(BF16, rows, half),
            pltpu.VMEM((rows, width), BF16),
            pltpu.VMEM((half, width), BF16),
        ),
        (hbm(tokens), hbm(lat_down)),
        (0, 1),
        [pltpu.VMEM((half, width), BF16), pltpu.SemaphoreType.DMA((CHUNKS + 2,))],
        2 * rows * width * half,
        4 * width * half,
    )
    mine = kernel_call(
        down_own_kernel,
        shaped(F32, rows, half),
        (vmem(tokens_here), vmem(weight_here)),
        (),
        [],
        2 * rows * width * half,
        2 * width * half,
    )
    mine = mine + over_tp(theirs, 1).astype(F32)
    terms, up_here = kernel_call(
        lambda *refs: terms_kernel(experts_all, *refs),
        (shaped(BF16, terms_rows, LANES), pltpu.VMEM(expert_up.shape, BF16)),
        (mine.astype(BF16), *(hbm(x) for x in (routes.T, route_weights.T, expert_up))),
        (1, 2, 3),
        [
            pltpu.VMEM(routes.shape[::-1], jnp.int32),
            pltpu.VMEM(routes.shape[::-1], F32),
            pltpu.SemaphoreType.DMA((3,)),
        ],
        0,
        2 * latent_len * all_units,
    )
    up_here = vmem(up_here)
    message = kernel_call(
        fold_kernel,
        shaped(BF16, parts * rows + terms_rows, LANES),
        (across(mine), terms),
        (),
        [],
        0,
        6 * rows * half,
    )
    down_rows = expert_down.reshape(all_units, latent_len)
    down_here = kernel_call(
        load_kernel,
        pltpu.VMEM(down_rows.shape, BF16),
        (message, hbm(down_rows)),
        (1,),
        [pltpu.SemaphoreType.DMA],
        0,
        2 * latent_len * all_units,
    )
    messages = [message] + [over_exp(message, s) for s in range(1, exp_count)]
    messages[-1], down_here = lax.optimization_barrier((messages[-1], down_here))
    down_here = vmem(down_here)
    latent, terms = kernel_call(
        unfold_kernel,
        (shaped(BF16, all_rows, half), shaped(BF16, exp_count * terms_rows, LANES)),
        messages,
        (),
        [],
        0,
        4 * all_rows * half,
    )
    other = over_tp(latent, 1)
    pre = kernel_call(
        first_kernel,
        shaped(F32, all_rows, all_units),
        (latent, up_here),
        (),
        [],
        all_rows * latent_len * all_units,
        latent_len * all_units,
    )
    hidden, theirs = kernel_call(
        second_kernel,
        (shaped(BF16, all_rows, all_units), shaped(BF16, all_rows, half)),
        (terms, other, pre, up_here, down_here),
        (),
        [],
        2 * all_rows * latent_len * all_units,
        2 * latent_len * all_units,
    )
    mine = kernel_call(
        third_kernel,
        shaped(F32, all_rows, half),
        (hidden, down_here),
        (),
        [],
        all_rows * latent_len * all_units,
        latent_len * all_units,
    )
    part = (mine + over_tp(theirs, 1).astype(F32)).astype(BF16)
    blocks = part.reshape(exp_count, rows, half)
    mixed = blocks[0].astype(F32)
    for s in (exp_count - 1, *range(exp_count - 2, 0, -1)):
        mixed = mixed + over_exp(blocks[s], s).astype(F32)
    mixed = across(mixed).astype(BF16)
    lat_up = vmem(lat_up)
    own_part = kernel_call(
        up_own_kernel,
        shaped(F32, rows, out_len),
        (mixed, lat_up),
        (),
        [],
        rows * latent_len * out_len,
        latent_len * out_len,
    )
    return kernel_call(
        up_kernel,
        shaped(BF16, rows, out_len),
        (own_part, over_tp(mixed, 1), lat_up),
        (),
        [pltpu.VMEM((rows, out_len), BF16), pltpu.SemaphoreType.DMA((2,))],
        rows * latent_len * out_len,
        latent_len * out_len,
        pltpu.HBM,
    )


def solution(mesh):
    return jax.shard_map(
        on_device,
        mesh=mesh,
        in_specs=(
            P(("grp", "exp"), "tp"),
            P(None, "tp"),
            P(None, "tp"),
            P("exp", "tp", None),
            P("exp", "tp", None),
            P(("grp", "exp"), None),
            P(("grp", "exp"), None),
        ),
        out_specs=P(("grp", "exp"), "tp"),
        check_vma=False,
    )
```

```python
import jax
import jax.numpy as jnp
from jax import lax
from jax.experimental import pallas as pl
from jax.experimental.pallas import tpu as pltpu
from jax.sharding import PartitionSpec as P

BF16, F32 = jnp.bfloat16, jnp.float32
NT = (((1,), (1,)), ((), ()))
NN = (((1,), (0,)), ((), ()))
VMEM_LIMIT = 24 << 20
LANES = 128
CHUNKS = 1
TILE = 16


def hbm(x):
    return pltpu.with_memory_space_constraint(x, pltpu.HBM)


def vmem(x):
    return pltpu.with_memory_space_constraint(x, pltpu.VMEM)


def shaped(dtype, *shape):
    return jax.ShapeDtypeStruct(shape, dtype)


def kernel_call(body, out_shape, args, in_hbm, scratch, flops, moved, out_space=pltpu.VMEM):
    def spec(space):
        return pl.BlockSpec(memory_space=space)

    return pl.pallas_call(
        body,
        out_shape=out_shape,
        in_specs=[spec(pltpu.HBM if i in in_hbm else pltpu.VMEM) for i in range(len(args))],
        out_specs=jax.tree.map(lambda _: spec(out_space), out_shape),
        scratch_shapes=scratch,
        compiler_params=pltpu.CompilerParams(vmem_limit_bytes=VMEM_LIMIT),
        cost_estimate=pl.CostEstimate(flops=flops, bytes_accessed=moved, transcendentals=0),
    )(*args)


def dot(a, b, dims):
    return lax.dot_general(a, b, dims, preferred_element_type=F32)


def half_at(own, half):
    bits = lax.axis_index("exp")
    for b in range(lax.axis_size("tp").bit_length() - 1):
        bits = bits + lax.axis_index("tp") // (1 << b)
    odd = bits % 2
    return pl.multiple_of((odd if own else 1 - odd) * half, half)


def down_kernel(tokens_hbm, weight_hbm, theirs_ref, tokens, mine_weight, weight, sems):
    half = theirs_ref.shape[1]
    size = half // CHUNKS
    chunks = []
    for i in range(CHUNKS):
        start = pl.multiple_of(half_at(False, half) + i * size, size)
        chunks.append(
            pltpu.make_async_copy(
                weight_hbm.at[pl.ds(start, size), :],
                weight.at[pl.ds(i * size, size), :],
                sems.at[2 + i],
            )
        )
        chunks[i].start()
    load = pltpu.make_async_copy(tokens_hbm, tokens, sems.at[0])
    load.start()
    later = pltpu.make_async_copy(
        weight_hbm.at[pl.ds(half_at(True, half), half), :], mine_weight, sems.at[1]
    )
    later.start()
    load.wait()
    x = tokens[...]
    for i in range(CHUNKS):
        chunks[i].wait()
        at = slice(i * size, (i + 1) * size)
        theirs_ref[:, at] = dot(x, weight[at, :], NT).astype(BF16)
    later.wait()


def down_own_kernel(tokens_ref, weight_ref, mine_ref):
    mine_ref[...] = dot(tokens_ref[...], weight_ref[...], NT)


def load_kernel(after_ref, hbm_ref, here_ref, sem):
    copy = pltpu.make_async_copy(hbm_ref, here_ref, sem)
    copy.start()
    copy.wait()


def group_at(group, experts_all):
    side_by_side = LANES // (2 * experts_all)
    return group // side_by_side, group % side_by_side * 2 * experts_all


def terms_kernel(
    experts_all, after_ref, routes_hbm, scale_hbm, up_hbm, terms_ref, up_ref, routes, scale, sems
):
    pairs = [(routes_hbm, routes), (scale_hbm, scale), (up_hbm, up_ref)]
    copies = [pltpu.make_async_copy(a, b, sems.at[i]) for i, (a, b) in enumerate(pairs)]
    for copy in copies:
        copy.start()
    copies[0].wait()
    copies[1].wait()
    rows = routes.shape[1]
    row = lax.broadcasted_iota(jnp.int32, (LANES, rows), 0)
    expert = jnp.where(row < experts_all, row, row - experts_all)
    combine = jnp.zeros((LANES, rows), F32)
    for r in range(routes.shape[0]):
        combine += jnp.where(expert == routes[r : r + 1, :], scale[r : r + 1, :], 0.0)
    combine = jnp.where(row < 2 * experts_all, combine, 0.0)
    high = combine.astype(BF16).astype(F32)
    combine = jnp.where(row < experts_all, high, combine - high)
    combine = jnp.concatenate([combine, jnp.zeros((LANES, LANES - rows), F32)], axis=1)
    turned = combine.T
    packed = [jnp.zeros((TILE, LANES), F32)] * (terms_ref.shape[0] // TILE)
    for g in range(rows // TILE):
        tile, at = group_at(g, experts_all)
        part = turned[g * TILE : (g + 1) * TILE, :]
        packed[tile] += pltpu.roll(part, at, 1) if at else part
    for tile, part in enumerate(packed):
        terms_ref[tile * TILE : (tile + 1) * TILE, :] = part.astype(BF16)
    copies[2].wait()


def fold_kernel(latent_ref, terms_ref, message_ref):
    rows, half = latent_ref.shape
    for c in range(half // LANES):
        columns = latent_ref[:, c * LANES : (c + 1) * LANES]
        message_ref[c * rows : (c + 1) * rows, :] = columns.astype(BF16)
    message_ref[half // LANES * rows :, :] = terms_ref[...]


def unfold_kernel(*refs):
    *messages, latent_ref, terms_ref = refs
    rows = latent_ref.shape[0] // len(messages)
    tiles = terms_ref.shape[0] // len(messages)
    parts = latent_ref.shape[1] // LANES
    for b, message in enumerate(messages):
        for c in range(parts):
            columns = message[c * rows : (c + 1) * rows, :]
            latent_ref[b * rows : (b + 1) * rows, c * LANES : (c + 1) * LANES] = columns
        terms_ref[b * tiles : (b + 1) * tiles, :] = message[parts * rows :, :]


def first_kernel(own_ref, up_ref, pre_ref):
    local_count, units, latent_len = up_ref.shape
    half = latent_len // 2
    rows = own_ref[...]
    for k in range(local_count):
        weight = up_ref[k, :, pl.ds(half_at(True, half), half)]
        pre_ref[:, k * units : (k + 1) * units] = dot(rows, weight, NT)


def second_kernel(terms_ref, other_ref, pre_ref, up_ref, down_ref, hidden_ref, theirs_ref):
    local_count, units, latent_len = up_ref.shape
    half = latent_len // 2
    blocks = lax.axis_size("exp")
    experts_all = local_count * blocks
    groups = other_ref.shape[0] // blocks // TILE
    tiles = terms_ref.shape[0] // blocks // TILE
    first = lax.axis_index("exp") * local_count
    lane = lax.broadcasted_iota(jnp.int32, (TILE, LANES), 1)
    rows = other_ref[...]
    for k in range(local_count):
        weight = []
        for b in range(blocks):
            for g in range(groups):
                tile, at = group_at(g, experts_all)
                tile = (b * tiles + tile) * TILE
                terms = terms_ref[tile : tile + TILE, :].astype(F32)
                named = (lane == at + first + k) | (lane == at + first + k + experts_all)
                weight.append(jnp.sum(jnp.where(named, terms, 0.0), axis=1, keepdims=True))
        weight = jnp.concatenate(weight, axis=0)
        at = slice(k * units, (k + 1) * units)
        pre_act = pre_ref[:, at] + dot(rows, up_ref[k, :, pl.ds(half_at(False, half), half)], NT)
        active = jnp.maximum(pre_act, 0.0)
        hidden_ref[:, at] = (active * active * weight).astype(BF16)
    theirs = dot(hidden_ref[...], down_ref[:, pl.ds(half_at(False, half), half)], NN)
    theirs_ref[...] = theirs.astype(BF16)


def third_kernel(hidden_ref, down_ref, mine_ref):
    half = mine_ref.shape[1]
    mine_ref[...] = dot(hidden_ref[...], down_ref[:, pl.ds(half_at(True, half), half)], NN)


def up_own_kernel(own_ref, weight_ref, out_ref):
    half = own_ref.shape[1]
    out_ref[...] = dot(own_ref[...], weight_ref[pl.ds(half_at(True, half), half), :], NN)


def up_kernel(part_ref, other_ref, weight_ref, out_hbm, out, sem):
    other = other_ref[...]
    at_rows = pl.ds(half_at(False, other.shape[1]), other.shape[1])
    out[...] = (part_ref[...] + dot(other, weight_ref[at_rows, :], NN)).astype(BF16)
    copy = pltpu.make_async_copy(out, out_hbm, sem)
    copy.start()
    copy.wait()


def on_device(tokens, lat_down, lat_up, expert_up, expert_down, routes, route_weights):
    exp_count, tp_count = lax.axis_size("exp"), lax.axis_size("tp")
    local_count, units, latent_len = expert_up.shape
    rows, width = tokens.shape
    half = latent_len // 2
    all_rows = exp_count * rows
    all_units = local_count * units
    out_len = lat_up.shape[1]
    experts_all = local_count * exp_count
    parts = half // LANES
    terms_rows = -(-rows // TILE // (LANES // (2 * experts_all))) * TILE
    pair_masks = [(1 << b) + 1 for b in range(1, tp_count.bit_length() - 1)]

    def over_tp(x, mask):
        return lax.ppermute(x, "tp", [(t, t ^ mask) for t in range(tp_count)])

    def over_exp(x, mask):
        turn = mask % 2
        places = [(e, t) for e in range(exp_count) for t in range(tp_count)]
        hops = [(e * tp_count + t, (e ^ mask) * tp_count + (t ^ turn)) for e, t in places]
        return lax.ppermute(x, ("exp", "tp"), hops)

    def across(x):
        for mask in pair_masks:
            x = x + over_tp(x.astype(BF16), mask).astype(F32)
        return x

    theirs, tokens_here, weight_here = kernel_call(
        down_kernel,
        (
            shaped(BF16, rows, half),
            pltpu.VMEM((rows, width), BF16),
            pltpu.VMEM((half, width), BF16),
        ),
        (hbm(tokens), hbm(lat_down)),
        (0, 1),
        [pltpu.VMEM((half, width), BF16), pltpu.SemaphoreType.DMA((CHUNKS + 2,))],
        2 * rows * width * half,
        4 * width * half,
    )
    mine = kernel_call(
        down_own_kernel,
        shaped(F32, rows, half),
        (vmem(tokens_here), vmem(weight_here)),
        (),
        [],
        2 * rows * width * half,
        2 * width * half,
    )
    mine = mine + over_tp(theirs, 1).astype(F32)
    terms, up_here = kernel_call(
        lambda *refs: terms_kernel(experts_all, *refs),
        (shaped(BF16, terms_rows, LANES), pltpu.VMEM(expert_up.shape, BF16)),
        (mine.astype(BF16), *(hbm(x) for x in (routes.T, route_weights.T, expert_up))),
        (1, 2, 3),
        [
            pltpu.VMEM(routes.shape[::-1], jnp.int32),
            pltpu.VMEM(routes.shape[::-1], F32),
            pltpu.SemaphoreType.DMA((3,)),
        ],
        0,
        2 * latent_len * all_units,
    )
    up_here = vmem(up_here)
    message = kernel_call(
        fold_kernel,
        shaped(BF16, parts * rows + terms_rows, LANES),
        (across(mine), terms),
        (),
        [],
        0,
        6 * rows * half,
    )
    down_rows = expert_down.reshape(all_units, latent_len)
    down_here = kernel_call(
        load_kernel,
        pltpu.VMEM(down_rows.shape, BF16),
        (message, hbm(down_rows)),
        (1,),
        [pltpu.SemaphoreType.DMA],
        0,
        2 * latent_len * all_units,
    )
    messages = [message] + [over_exp(message, s) for s in range(1, exp_count)]
    messages[-1], down_here = lax.optimization_barrier((messages[-1], down_here))
    down_here = vmem(down_here)
    latent, terms = kernel_call(
        unfold_kernel,
        (shaped(BF16, all_rows, half), shaped(BF16, exp_count * terms_rows, LANES)),
        messages,
        (),
        [],
        0,
        4 * all_rows * half,
    )
    other = over_tp(latent, 1)
    pre = kernel_call(
        first_kernel,
        shaped(F32, all_rows, all_units),
        (latent, up_here),
        (),
        [],
        all_rows * latent_len * all_units,
        latent_len * all_units,
    )
    hidden, theirs = kernel_call(
        second_kernel,
        (shaped(BF16, all_rows, all_units), shaped(BF16, all_rows, half)),
        (terms, other, pre, up_here, down_here),
        (),
        [],
        2 * all_rows * latent_len * all_units,
        2 * latent_len * all_units,
    )
    mine = kernel_call(
        third_kernel,
        shaped(F32, all_rows, half),
        (hidden, down_here),
        (),
        [],
        all_rows * latent_len * all_units,
        latent_len * all_units,
    )
    part = (mine + over_tp(theirs, 1).astype(F32)).astype(BF16)
    blocks = part.reshape(exp_count, rows, half)
    mixed = blocks[0].astype(F32)
    for s in (exp_count - 1, *range(1, exp_count - 1)):
        mixed = mixed + over_exp(blocks[s], s).astype(F32)
    mixed = across(mixed).astype(BF16)
    lat_up = vmem(lat_up)
    own_part = kernel_call(
        up_own_kernel,
        shaped(F32, rows, out_len),
        (mixed, lat_up),
        (),
        [],
        rows * latent_len * out_len,
        latent_len * out_len,
    )
    return kernel_call(
        up_kernel,
        shaped(BF16, rows, out_len),
        (own_part, over_tp(mixed, 1), lat_up),
        (),
        [pltpu.VMEM((rows, out_len), BF16), pltpu.SemaphoreType.DMA],
        rows * latent_len * out_len,
        latent_len * out_len,
        pltpu.HBM,
    )


def solution(mesh):
    return jax.shard_map(
        on_device,
        mesh=mesh,
        in_specs=(
            P(("grp", "exp"), "tp"),
            P(None, "tp"),
            P(None, "tp"),
            P("exp", "tp", None),
            P("exp", "tp", None),
            P(("grp", "exp"), None),
            P(("grp", "exp"), None),
        ),
        out_specs=P(("grp", "exp"), "tp"),
        check_vma=False,
    )
```

```python
import jax
import jax.numpy as jnp
from jax import lax
from jax.experimental import pallas as pl
from jax.experimental.pallas import tpu as pltpu
from jax.sharding import PartitionSpec as P

BF16, F32 = jnp.bfloat16, jnp.float32
NT = (((1,), (1,)), ((), ()))
NN = (((1,), (0,)), ((), ()))
VMEM_LIMIT = 24 << 20
LANES = 128
CHUNKS = 1
TILE = 16


def hbm(x):
    return pltpu.with_memory_space_constraint(x, pltpu.HBM)


def vmem(x):
    return pltpu.with_memory_space_constraint(x, pltpu.VMEM)


def shaped(dtype, *shape):
    return jax.ShapeDtypeStruct(shape, dtype)


def kernel_call(body, out_shape, args, in_hbm, scratch, flops, moved, out_space=pltpu.VMEM):
    def spec(space):
        return pl.BlockSpec(memory_space=space)

    return pl.pallas_call(
        body,
        out_shape=out_shape,
        in_specs=[spec(pltpu.HBM if i in in_hbm else pltpu.VMEM) for i in range(len(args))],
        out_specs=jax.tree.map(lambda _: spec(out_space), out_shape),
        scratch_shapes=scratch,
        compiler_params=pltpu.CompilerParams(vmem_limit_bytes=VMEM_LIMIT),
        cost_estimate=pl.CostEstimate(flops=flops, bytes_accessed=moved, transcendentals=0),
    )(*args)


def dot(a, b, dims):
    return lax.dot_general(a, b, dims, preferred_element_type=F32)


def half_at(own, half):
    bits = lax.axis_index("exp")
    for b in range(lax.axis_size("tp").bit_length() - 1):
        bits = bits + lax.axis_index("tp") // (1 << b)
    odd = bits % 2
    return pl.multiple_of((odd if own else 1 - odd) * half, half)


def down_kernel(tokens_hbm, weight_hbm, theirs_ref, tokens, mine_weight, weight, sems):
    half = theirs_ref.shape[1]
    size = half // CHUNKS
    chunks = []
    for i in range(CHUNKS):
        start = pl.multiple_of(half_at(False, half) + i * size, size)
        chunks.append(
            pltpu.make_async_copy(
                weight_hbm.at[pl.ds(start, size), :],
                weight.at[pl.ds(i * size, size), :],
                sems.at[2 + i],
            )
        )
        chunks[i].start()
    load = pltpu.make_async_copy(tokens_hbm, tokens, sems.at[0])
    load.start()
    later = pltpu.make_async_copy(
        weight_hbm.at[pl.ds(half_at(True, half), half), :], mine_weight, sems.at[1]
    )
    later.start()
    load.wait()
    x = tokens[...]
    for i in range(CHUNKS):
        chunks[i].wait()
        at = slice(i * size, (i + 1) * size)
        theirs_ref[:, at] = dot(x, weight[at, :], NT).astype(BF16)
    later.wait()


def down_own_kernel(tokens_ref, weight_ref, mine_ref):
    mine_ref[...] = dot(tokens_ref[...], weight_ref[...], NT)


def load_kernel(after_ref, hbm_ref, here_ref, sem):
    copy = pltpu.make_async_copy(hbm_ref, here_ref, sem)
    copy.start()
    copy.wait()


def group_at(group, experts_all):
    side_by_side = LANES // (2 * experts_all)
    return group // side_by_side, group % side_by_side * 2 * experts_all


def terms_kernel(
    experts_all, after_ref, routes_hbm, scale_hbm, up_hbm, terms_ref, up_ref, routes, scale, sems
):
    pairs = [(routes_hbm, routes), (scale_hbm, scale), (up_hbm, up_ref)]
    copies = [pltpu.make_async_copy(a, b, sems.at[i]) for i, (a, b) in enumerate(pairs)]
    for copy in copies:
        copy.start()
    copies[0].wait()
    copies[1].wait()
    rows = routes.shape[1]
    row = lax.broadcasted_iota(jnp.int32, (LANES, rows), 0)
    expert = jnp.where(row < experts_all, row, row - experts_all)
    combine = jnp.zeros((LANES, rows), F32)
    for r in range(routes.shape[0]):
        combine += jnp.where(expert == routes[r : r + 1, :], scale[r : r + 1, :], 0.0)
    combine = jnp.where(row < 2 * experts_all, combine, 0.0)
    high = combine.astype(BF16).astype(F32)
    combine = jnp.where(row < experts_all, high, combine - high)
    combine = jnp.concatenate([combine, jnp.zeros((LANES, LANES - rows), F32)], axis=1)
    turned = combine.T
    packed = [jnp.zeros((TILE, LANES), F32)] * (terms_ref.shape[0] // TILE)
    for g in range(rows // TILE):
        tile, at = group_at(g, experts_all)
        part = turned[g * TILE : (g + 1) * TILE, :]
        packed[tile] += pltpu.roll(part, at, 1) if at else part
    for tile, part in enumerate(packed):
        terms_ref[tile * TILE : (tile + 1) * TILE, :] = part.astype(BF16)
    copies[2].wait()


def fold_kernel(latent_ref, terms_ref, message_ref):
    rows, half = latent_ref.shape
    for c in range(half // LANES):
        columns = latent_ref[:, c * LANES : (c + 1) * LANES]
        message_ref[c * rows : (c + 1) * rows, :] = columns.astype(BF16)
    message_ref[half // LANES * rows :, :] = terms_ref[...]


def unfold_kernel(*refs):
    *messages, latent_ref, terms_ref = refs
    rows = latent_ref.shape[0] // len(messages)
    tiles = terms_ref.shape[0] // len(messages)
    parts = latent_ref.shape[1] // LANES
    for b, message in enumerate(messages):
        for c in range(parts):
            columns = message[c * rows : (c + 1) * rows, :]
            latent_ref[b * rows : (b + 1) * rows, c * LANES : (c + 1) * LANES] = columns
        terms_ref[b * tiles : (b + 1) * tiles, :] = message[parts * rows :, :]


def first_kernel(own_ref, up_ref, pre_ref):
    local_count, units, latent_len = up_ref.shape
    half = latent_len // 2
    rows = own_ref[...]
    for k in range(local_count):
        weight = up_ref[k, :, pl.ds(half_at(True, half), half)]
        pre_ref[:, k * units : (k + 1) * units] = dot(rows, weight, NT)


def second_kernel(terms_ref, other_ref, pre_ref, up_ref, down_ref, hidden_ref, theirs_ref):
    local_count, units, latent_len = up_ref.shape
    half = latent_len // 2
    blocks = lax.axis_size("exp")
    experts_all = local_count * blocks
    groups = other_ref.shape[0] // blocks // TILE
    tiles = terms_ref.shape[0] // blocks // TILE
    first = lax.axis_index("exp") * local_count
    lane = lax.broadcasted_iota(jnp.int32, (TILE, LANES), 1)
    rows = other_ref[...]
    for k in range(local_count):
        weight = []
        for b in range(blocks):
            for g in range(groups):
                tile, at = group_at(g, experts_all)
                tile = (b * tiles + tile) * TILE
                terms = terms_ref[tile : tile + TILE, :].astype(F32)
                named = (lane == at + first + k) | (lane == at + first + k + experts_all)
                weight.append(jnp.sum(jnp.where(named, terms, 0.0), axis=1, keepdims=True))
        weight = jnp.concatenate(weight, axis=0)
        at = slice(k * units, (k + 1) * units)
        pre_act = pre_ref[:, at] + dot(rows, up_ref[k, :, pl.ds(half_at(False, half), half)], NT)
        active = jnp.maximum(pre_act, 0.0)
        hidden_ref[:, at] = (active * active * weight).astype(BF16)
    theirs = dot(hidden_ref[...], down_ref[:, pl.ds(half_at(False, half), half)], NN)
    theirs_ref[...] = theirs.astype(BF16)


def third_kernel(hidden_ref, down_ref, mine_ref):
    half = mine_ref.shape[1]
    mine = dot(hidden_ref[...], down_ref[:, pl.ds(half_at(True, half), half)], NN)
    mine_ref[...] = mine.astype(BF16)


def up_own_kernel(own_ref, weight_ref, out_ref):
    half = own_ref.shape[1]
    out_ref[...] = dot(own_ref[...], weight_ref[pl.ds(half_at(True, half), half), :], NN)


def up_kernel(part_ref, other_ref, weight_ref, out_hbm, out, sem):
    other = other_ref[...]
    at_rows = pl.ds(half_at(False, other.shape[1]), other.shape[1])
    out[...] = (part_ref[...] + dot(other, weight_ref[at_rows, :], NN)).astype(BF16)
    copy = pltpu.make_async_copy(out, out_hbm, sem)
    copy.start()
    copy.wait()


def on_device(tokens, lat_down, lat_up, expert_up, expert_down, routes, route_weights):
    exp_count, tp_count = lax.axis_size("exp"), lax.axis_size("tp")
    local_count, units, latent_len = expert_up.shape
    rows, width = tokens.shape
    half = latent_len // 2
    all_rows = exp_count * rows
    all_units = local_count * units
    out_len = lat_up.shape[1]
    experts_all = local_count * exp_count
    parts = half // LANES
    terms_rows = -(-rows // TILE // (LANES // (2 * experts_all))) * TILE
    pair_masks = [(1 << b) + 1 for b in range(1, tp_count.bit_length() - 1)]

    def over_tp(x, mask):
        return lax.ppermute(x, "tp", [(t, t ^ mask) for t in range(tp_count)])

    def over_exp(x, mask):
        turn = mask % 2
        places = [(e, t) for e in range(exp_count) for t in range(tp_count)]
        hops = [(e * tp_count + t, (e ^ mask) * tp_count + (t ^ turn)) for e, t in places]
        return lax.ppermute(x, ("exp", "tp"), hops)

    def across(x):
        for mask in pair_masks:
            x = x + over_tp(x.astype(BF16), mask).astype(F32)
        return x

    theirs, tokens_here, weight_here = kernel_call(
        down_kernel,
        (
            shaped(BF16, rows, half),
            pltpu.VMEM((rows, width), BF16),
            pltpu.VMEM((half, width), BF16),
        ),
        (hbm(tokens), hbm(lat_down)),
        (0, 1),
        [pltpu.VMEM((half, width), BF16), pltpu.SemaphoreType.DMA((CHUNKS + 2,))],
        2 * rows * width * half,
        4 * width * half,
    )
    mine = kernel_call(
        down_own_kernel,
        shaped(F32, rows, half),
        (vmem(tokens_here), vmem(weight_here)),
        (),
        [],
        2 * rows * width * half,
        2 * width * half,
    )
    mine = mine + over_tp(theirs, 1).astype(F32)
    terms, up_here = kernel_call(
        lambda *refs: terms_kernel(experts_all, *refs),
        (shaped(BF16, terms_rows, LANES), pltpu.VMEM(expert_up.shape, BF16)),
        (mine.astype(BF16), *(hbm(x) for x in (routes.T, route_weights.T, expert_up))),
        (1, 2, 3),
        [
            pltpu.VMEM(routes.shape[::-1], jnp.int32),
            pltpu.VMEM(routes.shape[::-1], F32),
            pltpu.SemaphoreType.DMA((3,)),
        ],
        0,
        2 * latent_len * all_units,
    )
    up_here = vmem(up_here)
    message = kernel_call(
        fold_kernel,
        shaped(BF16, parts * rows + terms_rows, LANES),
        (across(mine), terms),
        (),
        [],
        0,
        6 * rows * half,
    )
    down_rows = expert_down.reshape(all_units, latent_len)
    down_here = kernel_call(
        load_kernel,
        pltpu.VMEM(down_rows.shape, BF16),
        (message, hbm(down_rows)),
        (1,),
        [pltpu.SemaphoreType.DMA],
        0,
        2 * latent_len * all_units,
    )
    messages = [message] + [over_exp(message, s) for s in range(1, exp_count)]
    messages[-1], down_here = lax.optimization_barrier((messages[-1], down_here))
    down_here = vmem(down_here)
    latent, terms = kernel_call(
        unfold_kernel,
        (shaped(BF16, all_rows, half), shaped(BF16, exp_count * terms_rows, LANES)),
        messages,
        (),
        [],
        0,
        4 * all_rows * half,
    )
    other = over_tp(latent, 1)
    pre = kernel_call(
        first_kernel,
        shaped(F32, all_rows, all_units),
        (latent, up_here),
        (),
        [],
        all_rows * latent_len * all_units,
        latent_len * all_units,
    )
    hidden, theirs = kernel_call(
        second_kernel,
        (shaped(BF16, all_rows, all_units), shaped(BF16, all_rows, half)),
        (terms, other, pre, up_here, down_here),
        (),
        [],
        2 * all_rows * latent_len * all_units,
        2 * latent_len * all_units,
    )
    mine = kernel_call(
        third_kernel,
        shaped(BF16, all_rows, half),
        (hidden, down_here),
        (),
        [],
        all_rows * latent_len * all_units,
        latent_len * all_units,
    )
    part = (mine.astype(F32) + over_tp(theirs, 1).astype(F32)).astype(BF16)
    blocks = part.reshape(exp_count, rows, half)
    mixed = blocks[0].astype(F32)
    for s in (exp_count - 1, *range(1, exp_count - 1)):
        mixed = mixed + over_exp(blocks[s], s).astype(F32)
    mixed = across(mixed).astype(BF16)
    lat_up = vmem(lat_up)
    own_part = kernel_call(
        up_own_kernel,
        shaped(F32, rows, out_len),
        (mixed, lat_up),
        (),
        [],
        rows * latent_len * out_len,
        latent_len * out_len,
    )
    return kernel_call(
        up_kernel,
        shaped(BF16, rows, out_len),
        (own_part, over_tp(mixed, 1), lat_up),
        (),
        [pltpu.VMEM((rows, out_len), BF16), pltpu.SemaphoreType.DMA],
        rows * latent_len * out_len,
        latent_len * out_len,
        pltpu.HBM,
    )


def solution(mesh):
    return jax.shard_map(
        on_device,
        mesh=mesh,
        in_specs=(
            P(("grp", "exp"), "tp"),
            P(None, "tp"),
            P(None, "tp"),
            P("exp", "tp", None),
            P("exp", "tp", None),
            P(("grp", "exp"), None),
            P(("grp", "exp"), None),
        ),
        out_specs=P(("grp", "exp"), "tp"),
        check_vma=False,
    )
```
